128 devices in a mesh: nodes: 32 (over y, z, core), rel: 4 (over x).
Axes of the slice: x: 4, y: 4, z: 4, core: 2. Of those that a mesh axis runs over, the one named last changes fastest.
Arguments:
- grad_out: bfloat16 [147456, 1024], P('nodes'), may hold values from -6 to 6
- paper_feat: bfloat16 [147456, 768], P('nodes'), may hold values from -6 to 6
- saved_agg: bfloat16 [4, 147456, 256], P('rel', 'nodes'), may hold values from -6 to 6
- rel_weight: bfloat16 [4, 256, 1024], P('rel'), may hold values from -0.375 to 0.375
- slot_paper: int32 [32, 4, 32, 128], P('nodes', 'rel'), may hold values from 0 to 4607, as said below
- slot_author: int32 [32, 4, 32, 128], P('nodes', 'rel'), may hold values from 0 to 2047, as said below
- block_count: int32 [32, 4, 32], P('nodes', 'rel'), may hold values from 4 to 128, as said below
Outputs:
- grad_author: float32 [65536, 256], P(('nodes', 'rel'))
- grad_rel: float32 [4, 256, 1024], P('rel', 'nodes')
- grad_self: float32 [768, 1024], P('nodes', 'rel')
The draws below stay inside these ranges and needn't reach their ends.
Inputs may be any that keep to these rules, and one draw needn't show every extreme that they name: `slot_paper`: every draw uses the first and the last paper of a shard. `slot_author`: rows repeat across slots and blocks. `block_count`: live slots are counted from slot 0; some blocks are full.
All inputs are finite; a program needn't handle non-finite values.
Results may differ from the reference program's by a relative error of at most 0.0065.
Values may be sent and summed in bfloat16 or wider, within the bound.
A program may use at most 128 MiB of HBM per device.

```python
import jax
import jax.numpy as jnp
from jax import lax

AUTHOR_W = 256
PAPER_W = 768
OUT_W = 1024
SLOTS = 128
KBLK = 1
P_DEV = 4608
R = 4
NB = 32
GROUP_ROWS = 2048
PAPERS = 147456
AUTHORS = 65536
N_NODES = 32


def shuffled_slots(order_key):
    return jax.random.permutation(order_key, NB * SLOTS)


def draw_slot_paper(key, part):
    key = jax.random.fold_in(key, 11)
    keys = jax.random.split(key, N_NODES * R)
    orders = jax.vmap(shuffled_slots)(keys)
    values = (orders % P_DEV).reshape(N_NODES, R, NB, SLOTS)
    values = values.at[:, :, 0, 0].set(P_DEV - 1)
    values = values.at[:, :, 0, 1].set(0)
    return values.astype(jnp.int32)


def draw_slot_author(key, part):
    key = jax.random.fold_in(key, 23)
    values = jax.random.randint(key, (N_NODES, R, NB, SLOTS), 0, GROUP_ROWS)
    values = values.at[:, :, 0, 0].set(GROUP_ROWS - 1)
    values = values.at[:, :, 0, 1].set(0)
    return values.astype(jnp.int32)


def draw_block_count(key, part):
    key = jax.random.fold_in(key, 37)
    first_key, second_key = jax.random.split(key)
    heavy = jax.random.randint(first_key, (N_NODES, R, 1), 0, 2)
    lowest = jnp.where(heavy == 1, SLOTS // 2, 4)
    values = jax.random.randint(second_key, (N_NODES, R, NB), lowest, SLOTS + 1)
    values = values.at[:, :, 0].set(SLOTS)
    values = values.at[:, :, 1].set(4)
    return values.astype(jnp.int32)


def levels(rng, shape, pieces, low, top_value):
    gain = 1.0
    for dim, blocks in pieces:
        steps = jax.random.uniform(jax.random.fold_in(jax.random.fold_in(rng, 6), dim), (blocks,), jnp.float32, low / len(pieces), top_value / len(pieces))
        gain = gain * jnp.repeat(jnp.exp(steps), shape[dim] // blocks).reshape((-1,) + (1,) * (len(shape) - 1 - dim))
    return gain


def gaussian(stream_key, shape, width, most, cuts=(), held_as=jnp.bfloat16):
    result = jax.random.normal(stream_key, shape, jnp.float32) * width
    if len(cuts) > 0:
        result = levels(stream_key, shape, cuts, -0.22, 0.18) * result
    return jnp.clip(result, min=-most, max=most).astype(held_as)


def setup_inputs(seed: int = 0) -> dict:
    streams_of = jax.random.split(jax.random.key(seed), 8)
    grad_out = gaussian(streams_of[0], (PAPERS, OUT_W), 1.0, 6.0, ((0, 32),))
    paper_feat = gaussian(streams_of[1], (PAPERS, PAPER_W), 1.0, 6.0, ((0, 32),))
    saved_agg = gaussian(streams_of[2], (R, PAPERS, AUTHOR_W), 1.0, 6.0, ((0, 4), (1, 32)))
    rel_weight = gaussian(streams_of[3], (R, AUTHOR_W, OUT_W), AUTHOR_W ** -0.5, 0.375, ((0, 4),))
    slot_paper = draw_slot_paper(jax.random.fold_in(streams_of[7], 71), 0)
    slot_author = draw_slot_author(jax.random.fold_in(streams_of[7], 71), 0)
    block_count = draw_block_count(jax.random.fold_in(streams_of[7], 71), 0)
    return dict(grad_out=grad_out, paper_feat=paper_feat, saved_agg=saved_agg, rel_weight=rel_weight, slot_paper=slot_paper, slot_author=slot_author, block_count=block_count)


def reference(grad_out, paper_feat, saved_agg, rel_weight, slot_paper, slot_author, block_count):
    slot_ids = jnp.arange(SLOTS, dtype=jnp.int32)
    group_base = jnp.arange(NB, dtype=jnp.int32) // KBLK * GROUP_ROWS
    grad_author = jnp.zeros((AUTHORS, AUTHOR_W), jnp.float32)
    grad_list = []
    for relation in range(R):
        back_rows = lax.dot_general(grad_out, rel_weight[relation], (((1,), (1,)), ((), ())), preferred_element_type=jnp.float32)

        def shard_step(running, operands):
            shard_index, papers, authors, counts = operands
            paper_rows = lax.dynamic_slice_in_dim(back_rows, (shard_index * P_DEV).astype(jnp.int32), P_DEV, 0)
            rounded = paper_rows[papers.reshape(-1)].astype(jnp.bfloat16)
            messages = lax.optimization_barrier(rounded).astype(jnp.float32)
            alive_mask = (slot_ids[None, :] < counts[:, None]).astype(jnp.float32)
            weights = lax.rsqrt(counts.astype(jnp.float32))[:, None] * alive_mask
            values = messages * weights.reshape(-1, 1)
            targets = (authors + group_base[:, None]).reshape(-1).astype(jnp.int32)
            return (running.at[targets].add(values), None)
        operands = (jnp.arange(N_NODES, dtype=jnp.int32), slot_paper[:, relation], slot_author[:, relation], block_count[:, relation])
        grad_author, _ = lax.scan(shard_step, grad_author, operands)
        grad_list.append(lax.dot_general(saved_agg[relation], grad_out, (((0,), (0,)), ((), ())), preferred_element_type=jnp.float32))
    grad_rel = jnp.stack(grad_list, axis=0)
    grad_self = lax.dot_general(paper_feat, grad_out, (((0,), (0,)), ((), ())), preferred_element_type=jnp.float32)
    return (grad_author, grad_rel, grad_self)
```

```python
import jax
import jax.numpy as jnp
from jax import lax
from jax.experimental import pallas as pl
from jax.experimental.pallas import tpu as pltpu
from jax.sharding import PartitionSpec as P

MESH = pl.DeviceIdType.MESH
F32 = jnp.float32
BF16 = jnp.bfloat16
DOTS = dict(preferred_element_type=F32)

NODES, REL = 32, 4
YN, ZN, CN = 4, 4, 2
PAPERS, OUT_W, AUTH_W, PAPER_W = 4608, 1024, 256, 768
SLOTS, GROUP, OWN = 128, 2048, 512
CHUNK = 768
CHUNKS = PAPERS // CHUNK
PIECE = 112
PER_SCAT = 4
SCAT_ROWS = 1024
WHOLE = 24
LATE = NODES - WHOLE
HALF = AUTH_W // 2
PART = OWN // 2


def chunk(k):
    return pl.ds(pl.multiple_of(k * CHUNK, CHUNK), CHUNK)


def block(t):
    if isinstance(t, int):
        return pl.ds(t * SLOTS, SLOTS)
    return pl.ds(pl.multiple_of(t * SLOTS, SLOTS), SLOTS)


ROW, COLUMN = 0, 1
GROUPS = [(ROW, 2, 0), (ROW, 2, 1), (COLUMN, 2), (ROW, 0, 0), (ROW, 0, 1), (COLUMN, 0), (COLUMN, 1), (COLUMN, 3)]


def in_group(group, j):
    if group[0] == ROW:
        return group[1], j, group[2]
    return 1 + 2 * (j // 2), group[1], j % 2


SLOT_OFFSETS = [in_group(group, j) for group in GROUPS for j in range(4)]
HERE = SLOT_OFFSETS.index((0, 0, 0))
OTHERS = [t for t in range(NODES) if t != HERE]
RELAYED = [t for t in OTHERS if 2 in SLOT_OFFSETS[t][:2]]
DIRECT = [t for t in OTHERS if t < WHOLE and t not in RELAYED]


def first_hop(t):
    dy, dz, dc = SLOT_OFFSETS[t]
    step = 1 + 2 * dc
    return step * (dy == 2), step * (dz == 2), 0


def second_hop(t):
    dy, dz, dc = SLOT_OFFSETS[t]
    hy, hz, _ = first_hop(t)
    return (dy - hy) % YN, (dz - hz) % ZN, dc


class Place:
    def __init__(self):
        me = lax.axis_index("nodes")
        self.me = me
        self.y = lax.div(me, ZN * CN)
        self.z = lax.rem(lax.div(me, CN), ZN)
        self.c = lax.rem(me, CN)
        sign = 1 + 2 * self.c
        self.ys = [lax.rem(self.y + sign * k, YN) * (ZN * CN) for k in range(YN)]
        self.zs = [lax.rem(self.z + sign * k, ZN) * CN for k in range(ZN)]
        self.cs = [self.c, 1 - self.c]
        self.sign = sign

    def node(self, dy, dz, dc):
        return self.ys[dy] + self.zs[dz] + self.cs[dc]

    def peer(self, t):
        return self.node(*SLOT_OFFSETS[t])

    def peer_in(self, k, j):
        group = GROUPS[k]
        if group[0] == ROW:
            return self.ys[group[1]] + lax.rem(self.z + self.sign * j, ZN) * CN + self.cs[group[2]]
        y = lax.rem(self.y + self.sign * (1 + 2 * lax.div(j, 2)), YN)
        return y * (ZN * CN) + self.zs[group[1]] + lax.rem(self.c + lax.rem(j, 2), CN)


def each(slots, body):
    for t in slots:
        body(t)


def loop(lo, hi, body):
    def step(t, _):
        body(t)
        return 0

    lax.fori_loop(lo, hi, step, 0)


def kernel(
    papers, counts, authors, w_hbm, go_hbm, pf_hbm, sa_hbm,
    ga, gr, gs,
    w, wt, g, feat, agg, table, rows, send, relay, recv, late_send, late_recv, auth, acc,
    racc, sacc, wg, csend, crecv, yfar_send, yfar_recv, ynear_send, ynear_recv, own_sum, zsend, zrecv,
    far_send, far_recv, near_send, near_recv,
    wsem, gsem, fsem, asem, au_s, au_r, ms_s, ms_r, rl_s, rl_r, lt_s, lt_r,
    c_s, c_r, yf_s, yf_r, yn_s, yn_r, z_s, z_r, far_s, far_r, near_s, near_r,
):
    at = Place()
    q = lax.axis_index("rel")
    me, y, z, c, node = at.me, at.y, at.z, at.c, at.node

    def g_copy(k):
        return pltpu.make_async_copy(go_hbm.at[chunk(k)], g.at[chunk(k)], gsem.at[k])

    def f_copy(k):
        return pltpu.make_async_copy(pf_hbm.at[chunk(k)], feat.at[chunk(k)], fsem.at[k])

    def a_copy(k):
        return pltpu.make_async_copy(sa_hbm.at[chunk(k)], agg.at[chunk(k)], asem.at[k])

    def load_rest(k):
        a_copy(k).start()
        f_copy(k).start()

    w_copy = pltpu.make_async_copy(w_hbm, w, wsem)
    w_copy.start()
    loop(0, CHUNKS, lambda k: g_copy(k).start())

    barrier = pltpu.get_barrier_semaphore()

    def greet(t):
        pl.semaphore_signal(barrier, inc=1, device_id={"nodes": at.peer(t)}, device_id_type=MESH)

    each(OTHERS, greet)
    for d in (1, REL - 1):
        pl.semaphore_signal(
            barrier, inc=1, device_id={"rel": lax.rem(q + d, REL)}, device_id_type=MESH
        )

    w_copy.wait()
    wt[...] = w[...].astype(F32).T.astype(BF16)

    def back_step(k):
        g_copy(k).wait()
        part = CHUNK // 2
        for m in range(2):
            lo = k * CHUNK + m * part
            back = jnp.dot(g[pl.ds(pl.multiple_of(lo, part), part), :], wt[...], **DOTS)
            for h in range(2):
                table[pl.ds(2 * lo + h, part, stride=2), :] = back[:, h * HALF:h * HALF + HALF]

    loop(0, CHUNKS, back_step)
    loop(0, CHUNKS, load_rest)
    pl.semaphore_wait(barrier, NODES - 1 + 2)

    def remote(src, dst, sems, i, to):
        return pltpu.make_async_remote_copy(
            src_ref=src, dst_ref=dst, send_sem=sems[0].at[i], recv_sem=sems[1].at[i],
            device_id={"nodes": to}, device_id_type=MESH,
        )

    def auth_copy(t):
        return remote(authors.at[at.peer(t)], auth.at[t], (au_s, au_r), t, at.peer(t))

    def relay_copy(t):
        i = RELAYED.index(t)
        return remote(send.at[block(t)], relay.at[block(i)], (rl_s, rl_r), i, node(*first_hop(t)))

    def msg_copy(t):
        if t in RELAYED:
            source, to = relay.at[block(RELAYED.index(t))], node(*second_hop(t))
        else:
            source, to = send.at[block(t)], at.peer(t)
        return remote(source, recv.at[block(t)], (ms_s, ms_r), t, to)

    def late_copy(h, i):
        return remote(
            late_send.at[h, block(i)], late_recv.at[h, block(i)],
            (lt_s, lt_r), h * LATE + i, at.peer(WHOLE + i),
        )

    def gather(b):
        for u in range(SLOTS):
            p = papers[b, u] * 2
            rows[2 * u:2 * u + 2, :] = table[pl.ds(p, 2), :]
        live = counts[b]
        scale = lax.rsqrt(jnp.full((1, HALF), live, jnp.int32).astype(F32))
        slot = lax.broadcasted_iota(jnp.int32, (SLOTS, HALF), 0)
        return [
            jnp.where(slot < live, rows[pl.ds(h, SLOTS, stride=2), :] * scale, 0.0).astype(BF16)
            for h in range(2)
        ]

    for k in range(WHOLE // 4):

        def whole_step(j):
            left, right = gather(at.peer_in(k, j))
            send[block(k * 4 + j), :HALF] = left
            send[block(k * 4 + j), HALF:] = right

        loop(0, 4, whole_step)
        for t in range(k * 4, k * 4 + 4):
            if t in RELAYED:
                relay_copy(t).start()
            elif t != HERE:
                msg_copy(t).start()
    for k in range(LATE // 4):

        def late_step(j):
            left, right = gather(at.peer_in(WHOLE // 4 + k, j))
            late_send[0, block(k * 4 + j), :] = left
            late_send[1, block(k * 4 + j), :] = right

        loop(0, 4, late_step)
    each(OTHERS, lambda t: auth_copy(t).start())
    auth[HERE] = authors[me]
    recv[block(HERE), :] = send[block(HERE), :]

    racc[...] = jnp.zeros_like(racc)
    sacc[...] = jnp.zeros_like(sacc)
    cols = pl.ds(pl.multiple_of(q * AUTH_W, AUTH_W), AUTH_W)
    over0 = (((0,), (0,)), ((), ()))

    def grads_step(k):
        a_copy(k).wait()
        f_copy(k).wait()
        racc[...] += lax.dot_general(agg[chunk(k), :], g[chunk(k), :], over0, **DOTS)
        sacc[...] += lax.dot_general(g[chunk(k), cols], feat[chunk(k), :], over0, **DOTS)

    def forward(t):
        relay_copy(t).wait_recv()
        msg_copy(t).start()

    loop(0, 2, grads_step)
    each(RELAYED, forward)
    loop(2, CHUNKS, grads_step)

    sacc_t = sacc[...].T
    for n in range(NODES):
        co, yz = n % CN, n // CN
        for k in range(8):
            wg[co, yz, 8 * k:8 * k + 8, :] = racc[8 * n:8 * n + 8, 128 * k:128 * k + 128]
        for i in range(3):
            for h in range(2):
                r0 = 64 + (2 * i + h) * 8
                wg[co, yz, r0:r0 + 8, :] = sacc_t[24 * n + 8 * i:24 * n + 8 * i + 8, 128 * h:128 * h + 128]

    core_copy = pltpu.make_async_remote_copy(
        src_ref=csend, dst_ref=crecv, send_sem=c_s, recv_sem=c_r,
        device_id={"nodes": node(0, 0, 1)}, device_id_type=MESH,
    )

    def core_round(i):
        csend[i] = wg[1 - c, i].astype(BF16)

    loop(0, YN * ZN, core_round)
    core_copy.start()
    for h in range(2):
        each(range(LATE), lambda i: late_copy(h, i).start())

    acc[...] = jnp.zeros_like(acc)
    each(OTHERS, lambda t: auth_copy(t).wait_recv())

    def add_rows(first_slot, msg, cols):
        targets = [auth[first_slot + u] for u in range(PER_SCAT)]

        def some(m):
            span = pl.ds(pl.multiple_of(m * SCAT_ROWS, SCAT_ROWS), SCAT_ROWS)
            ids = lax.broadcasted_iota(jnp.int32, (SCAT_ROWS, SLOTS), 0) + m * SCAT_ROWS
            onehot = jnp.concatenate(
                [jnp.where(ids == a, 1.0, 0.0).astype(BF16) for a in targets], axis=1
            )
            acc[span, cols] += jnp.dot(onehot, msg, **DOTS)

        loop(0, GROUP // SCAT_ROWS, some)

    def group(s):
        width = PER_SCAT * SLOTS
        return pl.ds(pl.multiple_of(s * width, width), width)

    def scatter(s):
        for u in range(PER_SCAT):
            if s * PER_SCAT + u != HERE:
                msg_copy(s * PER_SCAT + u).wait_recv()
        add_rows(s * PER_SCAT, recv[group(s), :], slice(None))

    def scatter_late(h, s):
        for u in range(PER_SCAT):
            late_copy(h, s * PER_SCAT + u).wait_recv()
        add_rows(WHOLE + s * PER_SCAT, late_recv[h, group(s), :], slice(h * HALF, h * HALF + HALF))

    def y_to(d):
        return lax.div(at.ys[1 + 2 * d], ZN * CN)

    def pair(to, p):
        return to * ZN + 2 * p

    def yfar_copy(d):
        return remote(yfar_send.at[d], yfar_recv.at[d], (yf_s, yf_r), d, node(1 + 2 * d, 0, 0))

    def ynear_copy(d, p):
        return remote(
            ynear_send.at[d, p], ynear_recv.at[d, p], (yn_s, yn_r), 2 * d + p, node(1 + 2 * d, 0, 0)
        )

    def z_copy(d):
        to = lax.div(at.zs[d], CN)
        return remote(zsend.at[to], zrecv.at[d - 1], (z_s, z_r), d - 1, node(0, d, 0))

    def core_sum(i):
        wg[c, i] = wg[c, i] + crecv[i].astype(F32)

    def y_first():
        core_copy.wait_recv()
        loop(0, YN * ZN, core_sum)
        for d in range(2):
            for i in range(2):
                yfar_send[d, i] = wg[c, pair(lax.rem(y + 2, YN), d) + i].astype(BF16)
            yfar_copy(d).start()
        for d in range(2):
            for i in range(2):
                ynear_send[d, 1 - d, i] = wg[c, pair(y_to(d), 1 - d) + i].astype(BF16)
            ynear_copy(d, 1 - d).start()

    def y_second():
        for d in range(2):
            yfar_copy(d).wait_recv()
            for i in range(2):
                total = wg[c, pair(y_to(d), d) + i] + yfar_recv[d, i].astype(F32)
                ynear_send[d, d, i] = total.astype(BF16)
            ynear_copy(d, d).start()

    def z_first():
        for p in range(2):
            for d in range(2):
                ynear_copy(d, p).wait_recv()
            for i in range(2):
                total = (
                    wg[c, pair(y, p) + i]
                    + ynear_recv[0, p, i].astype(F32) + ynear_recv[1, p, i].astype(F32)
                )
                own_sum[2 * p + i] = total
                zsend[2 * p + i] = total.astype(BF16)
        for d in range(1, ZN):
            z_copy(d).start()

    def z_last():
        for d in range(1, ZN):
            z_copy(d).wait_recv()
        total = own_sum[z]
        for d in range(ZN - 1):
            total = total + zrecv[d].astype(F32)
        for k in range(8):
            gr[:, 128 * k:128 * k + 128] = total[8 * k:8 * k + 8, :]
        for i in range(3):
            for h in range(2):
                r0 = 64 + (2 * i + h) * 8
                gs[8 * i:8 * i + 8, 128 * h:128 * h + 128] = total[r0:r0 + 8, :]

    def towards(d):
        return lax.rem(q + (1, REL - 1)[d], REL)

    def rows_of(owner, p):
        return pl.ds(pl.multiple_of(owner * OWN + p * PART, PART), PART)

    def far_copy(h, d):
        return pltpu.make_async_remote_copy(
            src_ref=far_send.at[h, d], dst_ref=far_recv.at[h, d],
            send_sem=far_s.at[h, d], recv_sem=far_r.at[h, d],
            device_id={"rel": towards(d)}, device_id_type=MESH,
        )

    def near_copy(h, d, p):
        return pltpu.make_async_remote_copy(
            src_ref=near_send.at[h, d, p], dst_ref=near_recv.at[h, d, p],
            send_sem=near_s.at[h, d, p], recv_sem=near_r.at[h, d, p],
            device_id={"rel": towards(d)}, device_id_type=MESH,
        )

    def half(h):
        return slice(h * HALF, h * HALF + HALF)

    def rel_first(h):
        for d in range(2):
            far_send[h, d] = acc[rows_of(lax.rem(q + 2, REL), d), half(h)].astype(BF16)
            far_copy(h, d).start()
        for d in range(2):
            near_send[h, d, 1 - d] = acc[rows_of(towards(d), 1 - d), half(h)].astype(BF16)
            near_copy(h, d, 1 - d).start()

    def rel_second(h):
        for d in range(2):
            far_copy(h, d).wait_recv()
            mine = acc[rows_of(towards(d), d), half(h)]
            near_send[h, d, d] = (mine + far_recv[h, d].astype(F32)).astype(BF16)
            near_copy(h, d, d).start()

    def rel_last(h):
        for p in range(2):
            for d in range(2):
                near_copy(h, d, p).wait_recv()
            ga[p * PART:p * PART + PART, half(h)] = (
                acc[rows_of(q, p), half(h)]
                + near_recv[h, 0, p].astype(F32) + near_recv[h, 1, p].astype(F32)
            )

    scatter(3)
    scatter(5)
    scatter(4)
    y_first()
    scatter(0)
    scatter(1)
    y_second()
    scatter(2)
    scatter_late(0, 0)
    scatter_late(0, 1)
    rel_first(0)
    z_first()
    scatter_late(1, 0)
    rel_second(0)
    scatter_late(1, 1)
    rel_first(1)
    z_last()
    rel_last(0)
    rel_second(1)
    rel_last(1)

    core_copy.wait_send()
    each(OTHERS, lambda t: auth_copy(t).wait_send())
    each(RELAYED, lambda t: relay_copy(t).wait_send())
    each(RELAYED + DIRECT, lambda t: msg_copy(t).wait_send())
    for h in range(2):
        each(range(LATE), lambda i: late_copy(h, i).wait_send())
        for d in range(2):
            far_copy(h, d).wait_send()
            for p in range(2):
                near_copy(h, d, p).wait_send()
    for d in range(2):
        yfar_copy(d).wait_send()
        for p in range(2):
            ynear_copy(d, p).wait_send()
    for d in range(1, ZN):
        z_copy(d).wait_send()


def hand_over(a, b, c, ao, bo, co):
    ao[...] = a[...]
    bo[...] = b[...]
    co[...] = c[...]


def on_device(grad_out, paper_feat, saved_agg, rel_weight, slot_paper, slot_author, block_count):
    vmem = pl.BlockSpec(memory_space=pltpu.VMEM)
    smem = pl.BlockSpec(memory_space=pltpu.SMEM)
    hbm = pl.BlockSpec(memory_space=pl.ANY)
    dma = pltpu.SemaphoreType.DMA
    limit = 56 * 1024 * 1024
    whole = (WHOLE * SLOTS, AUTH_W)
    late = (2, LATE * SLOTS, HALF)
    ga, gr, gs = pl.pallas_call(
        kernel,
        out_shape=(
            jax.ShapeDtypeStruct((OWN, AUTH_W), F32),
            jax.ShapeDtypeStruct((8, OUT_W), F32),
            jax.ShapeDtypeStruct((24, AUTH_W), F32),
        ),
        in_specs=[smem, smem, vmem, hbm, hbm, hbm, hbm],
        out_specs=(vmem, vmem, vmem),
        scratch_shapes=[
            pltpu.VMEM((AUTH_W, OUT_W), BF16),
            pltpu.VMEM((OUT_W, AUTH_W), BF16),
            pltpu.VMEM((PAPERS, OUT_W), BF16),
            pltpu.VMEM((PAPERS, PAPER_W), BF16),
            pltpu.VMEM((PAPERS, AUTH_W), BF16),
            pltpu.VMEM((2 * PAPERS, HALF), F32),
            pltpu.VMEM((2 * SLOTS, HALF), F32),
            pltpu.VMEM(whole, BF16),
            pltpu.VMEM((len(RELAYED) * SLOTS, AUTH_W), BF16),
            pltpu.VMEM(whole, BF16),
            pltpu.VMEM(late, BF16),
            pltpu.VMEM(late, BF16),
            pltpu.VMEM((NODES, 1, SLOTS), jnp.int32),
            pltpu.VMEM((GROUP, AUTH_W), F32),
            pltpu.VMEM((AUTH_W, OUT_W), F32),
            pltpu.VMEM((AUTH_W, PAPER_W), F32),
            pltpu.VMEM((CN, YN * ZN, PIECE, 128), F32),
            pltpu.VMEM((YN * ZN, PIECE, 128), BF16),
            pltpu.VMEM((YN * ZN, PIECE, 128), BF16),
            pltpu.VMEM((2, 2, PIECE, 128), BF16),
            pltpu.VMEM((2, 2, PIECE, 128), BF16),
            pltpu.VMEM((2, 2, 2, PIECE, 128), BF16),
            pltpu.VMEM((2, 2, 2, PIECE, 128), BF16),
            pltpu.VMEM((ZN, PIECE, 128), F32),
            pltpu.VMEM((ZN, PIECE, 128), BF16),
            pltpu.VMEM((ZN - 1, PIECE, 128), BF16),
            pltpu.VMEM((2, 2, PART, HALF), BF16),
            pltpu.VMEM((2, 2, PART, HALF), BF16),
            pltpu.VMEM((2, 2, 2, PART, HALF), BF16),
            pltpu.VMEM((2, 2, 2, PART, HALF), BF16),
            dma, dma((CHUNKS,)), dma((CHUNKS,)), dma((CHUNKS,)),
            dma((NODES,)), dma((NODES,)), dma((WHOLE,)), dma((WHOLE,)),
            dma((len(RELAYED),)), dma((len(RELAYED),)), dma((2 * LATE,)), dma((2 * LATE,)),
            dma, dma, dma((2,)), dma((2,)), dma((4,)), dma((4,)), dma((3,)), dma((3,)),
            dma((2, 2)), dma((2, 2)), dma((2, 2, 2)), dma((2, 2, 2)),
        ],
        compiler_params=pltpu.CompilerParams(
            collective_id=0, has_side_effects=True, vmem_limit_bytes=limit
        ),
    )(
        slot_paper[0, 0], block_count[0, 0],
        slot_author[0, 0][:, None, :], rel_weight[0], grad_out, paper_feat, saved_agg[0],
    )
    ga, gr, gs = pl.pallas_call(
        hand_over,
        out_shape=tuple(jax.ShapeDtypeStruct(v.shape, F32) for v in (ga, gr, gs)),
        in_specs=[vmem] * 3,
        out_specs=(vmem,) * 3,
    )(ga, gr, gs)
    return ga, gr[None], gs


def solution(mesh):
    return jax.shard_map(
        on_device,
        mesh=mesh,
        in_specs=(
            P("nodes", None),
            P("nodes", None),
            P("rel", "nodes", None),
            P("rel", None, None),
            P("nodes", "rel", None, None),
            P("nodes", "rel", None, None),
            P("nodes", "rel", None),
        ),
        out_specs=(P(("nodes", "rel"), None), P("rel", "nodes", None), P("nodes", "rel")),
        check_vma=False,
    )
```

```python
import jax
import jax.numpy as jnp
from jax import lax
from jax.experimental import pallas as pl
from jax.experimental.pallas import tpu as pltpu
from jax.sharding import PartitionSpec as P

MESH = pl.DeviceIdType.MESH
F32 = jnp.float32
BF16 = jnp.bfloat16
DOTS = dict(preferred_element_type=F32)

NODES, REL = 32, 4
SIDE, CN = 4, 2
PAPERS, OUT_W, AUTH_W, PAPER_W = 4608, 1024, 256, 768
SLOTS, GROUP, OWN = 128, 2048, 512
CHUNK = 768
CHUNKS = PAPERS // CHUNK
PIECE = 112
PER_SCAT = 4
SCAT_ROWS = 1024
WHOLE = 24
LATE = NODES - WHOLE
HALF = AUTH_W // 2
PART = OWN // 2


def chunk(k):
    return pl.ds(pl.multiple_of(k * CHUNK, CHUNK), CHUNK)


def block(t):
    if isinstance(t, int):
        return pl.ds(t * SLOTS, SLOTS)
    return pl.ds(pl.multiple_of(t * SLOTS, SLOTS), SLOTS)


ROW, COLUMN = 0, 1
GROUPS = [(ROW, 2, 0), (COLUMN, 2), (ROW, 2, 1), (ROW, 0, 0), (COLUMN, 0), (ROW, 0, 1), (COLUMN, 1), (COLUMN, 3)]


def in_group(group, j):
    if group[0] == ROW:
        return group[1], j, group[2]
    return 1 + 2 * (j // 2), group[1], j % 2


SLOT_OFFSETS = [in_group(group, j) for group in GROUPS for j in range(4)]
HERE = SLOT_OFFSETS.index((0, 0, 0))
OTHERS = [t for t in range(NODES) if t != HERE]
RELAYED = [t for t in OTHERS if 2 in SLOT_OFFSETS[t][:2]]
DIRECT = [t for t in OTHERS if t < WHOLE and t not in RELAYED]


def first_hop(t):
    da, db, dc = SLOT_OFFSETS[t]
    ha = (1 if db < 2 else 3) if da == 2 else 0
    hb = (1 if da in (1, 2) else 3) if db == 2 else 0
    return ha, hb, 0


def second_hop(t):
    da, db, dc = SLOT_OFFSETS[t]
    ha, hb, _ = first_hop(t)
    return (da - ha) % SIDE, (db - hb) % SIDE, dc


class Place:
    def __init__(self):
        me = lax.axis_index("nodes")
        y = lax.div(me, SIDE * CN)
        z = lax.rem(lax.div(me, CN), SIDE)
        c = lax.rem(me, CN)
        self.me, self.c = me, c
        self.a, self.b = y + c * (z - y), z + c * (y - z)
        self.stride_a = SIDE * CN - (SIDE * CN - CN) * c
        self.stride_b = CN + (SIDE * CN - CN) * c
        self.sign = 1 + 2 * c
        self.a_at = [lax.rem(self.a + self.sign * k, SIDE) for k in range(SIDE)]
        self.b_at = [lax.rem(self.b + self.sign * k, SIDE) for k in range(SIDE)]
        self.a_nodes = [v * self.stride_a for v in self.a_at]
        self.b_nodes = [v * self.stride_b for v in self.b_at]
        self.cs = [c, 1 - c]

    def node(self, da, db, dc):
        return self.a_nodes[da] + self.b_nodes[db] + self.cs[dc]

    def peer(self, t):
        return self.node(*SLOT_OFFSETS[t])

    def peer_in(self, k, j):
        group = GROUPS[k]
        if group[0] == ROW:
            b = lax.rem(self.b + self.sign * j, SIDE)
            return self.a_nodes[group[1]] + b * self.stride_b + self.cs[group[2]]
        a = lax.rem(self.a + self.sign * (1 + 2 * lax.div(j, 2)), SIDE)
        return a * self.stride_a + self.b_nodes[group[1]] + lax.rem(self.c + lax.rem(j, 2), CN)


def each(slots, body):
    for t in slots:
        body(t)


def loop(lo, hi, body):
    def step(t, _):
        body(t)
        return 0

    lax.fori_loop(lo, hi, step, 0)


def kernel(
    papers, counts, authors, w_hbm, go_hbm, pf_hbm, sa_hbm,
    ga, gr, gs,
    w, wt, g, feat, agg, table, rows, send, relay, recv, late_send, late_recv, auth, acc,
    racc, sacc, wg, csend, crecv, afar_send, afar_recv, anear_send, anear_recv, own_sum, b_send, b_recv,
    far_send, far_recv, near_send, near_recv,
    wsem, gsem, fsem, asem, au_s, au_r, ms_s, ms_r, rl_s, rl_r, lt_s, lt_r,
    c_s, c_r, af_s, af_r, an_s, an_r, b_s, b_r, far_s, far_r, near_s, near_r,
):
    at = Place()
    q = lax.axis_index("rel")
    me, c, node = at.me, at.c, at.node

    def g_copy(k):
        return pltpu.make_async_copy(go_hbm.at[chunk(k)], g.at[chunk(k)], gsem.at[k])

    def f_copy(k):
        return pltpu.make_async_copy(pf_hbm.at[chunk(k)], feat.at[chunk(k)], fsem.at[k])

    def a_copy(k):
        return pltpu.make_async_copy(sa_hbm.at[chunk(k)], agg.at[chunk(k)], asem.at[k])

    def load_rest(k):
        a_copy(k).start()
        f_copy(k).start()

    w_copy = pltpu.make_async_copy(w_hbm, w, wsem)
    w_copy.start()
    loop(0, CHUNKS, lambda k: g_copy(k).start())

    barrier = pltpu.get_barrier_semaphore()

    def greet(t):
        pl.semaphore_signal(barrier, inc=1, device_id={"nodes": at.peer(t)}, device_id_type=MESH)

    each(OTHERS, greet)
    for d in (1, REL - 1):
        pl.semaphore_signal(
            barrier, inc=1, device_id={"rel": lax.rem(q + d, REL)}, device_id_type=MESH
        )

    w_copy.wait()
    wt[...] = w[...].astype(F32).T.astype(BF16)

    pl.semaphore_wait(barrier, NODES - 1 + 2)

    def remote(src, dst, sems, i, to):
        return pltpu.make_async_remote_copy(
            src_ref=src, dst_ref=dst, send_sem=sems[0].at[i], recv_sem=sems[1].at[i],
            device_id={"nodes": to}, device_id_type=MESH,
        )

    def auth_copy(t):
        return remote(authors.at[at.peer(t)], auth.at[t], (au_s, au_r), t, at.peer(t))

    each(OTHERS, lambda t: auth_copy(t).start())
    auth[HERE] = authors[me]

    def back_step(k):
        g_copy(k).wait()
        part = CHUNK // 2
        for m in range(2):
            lo = k * CHUNK + m * part
            back = jnp.dot(g[pl.ds(pl.multiple_of(lo, part), part), :], wt[...], **DOTS)
            for h in range(2):
                table[pl.ds(2 * lo + h, part, stride=2), :] = back[:, h * HALF:h * HALF + HALF]

    loop(0, CHUNKS, back_step)
    loop(0, CHUNKS, load_rest)
    def relay_copy(t):
        i = RELAYED.index(t)
        return remote(send.at[block(t)], relay.at[block(i)], (rl_s, rl_r), i, node(*first_hop(t)))

    def msg_copy(t):
        if t in RELAYED:
            source, to = relay.at[block(RELAYED.index(t))], node(*second_hop(t))
        else:
            source, to = send.at[block(t)], at.peer(t)
        return remote(source, recv.at[block(t)], (ms_s, ms_r), t, to)

    def late_copy(h, i):
        return remote(
            late_send.at[h, block(i)], late_recv.at[h, block(i)],
            (lt_s, lt_r), h * LATE + i, at.peer(WHOLE + i),
        )

    def gather(b):
        for u in range(SLOTS):
            p = papers[b, u] * 2
            rows[2 * u:2 * u + 2, :] = table[pl.ds(p, 2), :]
        live = counts[b]
        scale = lax.rsqrt(jnp.full((1, HALF), live, jnp.int32).astype(F32))
        slot = lax.broadcasted_iota(jnp.int32, (SLOTS, HALF), 0)
        return [
            jnp.where(slot < live, rows[pl.ds(h, SLOTS, stride=2), :] * scale, 0.0).astype(BF16)
            for h in range(2)
        ]

    for k in range(WHOLE // 4):

        def whole_step(j):
            left, right = gather(at.peer_in(k, j))
            send[block(k * 4 + j), :HALF] = left
            send[block(k * 4 + j), HALF:] = right

        loop(0, 4, whole_step)
        for t in range(k * 4, k * 4 + 4):
            if t in RELAYED:
                relay_copy(t).start()
            elif t != HERE:
                msg_copy(t).start()
    for k in range(LATE // 4):

        def late_step(j):
            left, right = gather(at.peer_in(WHOLE // 4 + k, j))
            late_send[0, block(k * 4 + j), :] = left
            late_send[1, block(k * 4 + j), :] = right

        loop(0, 4, late_step)
    recv[block(HERE), :] = send[block(HERE), :]

    racc[...] = jnp.zeros_like(racc)
    sacc[...] = jnp.zeros_like(sacc)
    cols = pl.ds(pl.multiple_of(q * AUTH_W, AUTH_W), AUTH_W)
    over0 = (((0,), (0,)), ((), ()))

    def grads_step(k):
        a_copy(k).wait()
        f_copy(k).wait()
        racc[...] += lax.dot_general(agg[chunk(k), :], g[chunk(k), :], over0, **DOTS)
        sacc[...] += lax.dot_general(g[chunk(k), cols], feat[chunk(k), :], over0, **DOTS)

    def forward(t):
        relay_copy(t).wait_recv()
        msg_copy(t).start()

    loop(0, 2, grads_step)
    each(RELAYED, forward)
    loop(2, CHUNKS, grads_step)

    sacc_t = sacc[...].T
    for n in range(NODES):
        co, y, z = n % CN, n // CN // SIDE, n // CN % SIDE
        ab = (y * SIDE + z, z * SIDE + y)[co]
        for k in range(8):
            wg[co, ab, 8 * k:8 * k + 8, :] = racc[8 * n:8 * n + 8, 128 * k:128 * k + 128]
        for i in range(3):
            for h in range(2):
                r0 = 64 + (2 * i + h) * 8
                wg[co, ab, r0:r0 + 8, :] = sacc_t[24 * n + 8 * i:24 * n + 8 * i + 8, 128 * h:128 * h + 128]

    core_copy = pltpu.make_async_remote_copy(
        src_ref=csend, dst_ref=crecv, send_sem=c_s, recv_sem=c_r,
        device_id={"nodes": node(0, 0, 1)}, device_id_type=MESH,
    )

    def core_round(i):
        csend[i] = wg[1 - c, i].astype(BF16)

    loop(0, SIDE * SIDE, core_round)
    core_copy.start()
    for h in range(2):
        each(range(LATE), lambda i: late_copy(h, i).start())

    acc[...] = jnp.zeros_like(acc)
    each(OTHERS, lambda t: auth_copy(t).wait_recv())

    def add_rows(first_slot, msg, cols):
        targets = [auth[first_slot + u] for u in range(PER_SCAT)]

        def some(m):
            span = pl.ds(pl.multiple_of(m * SCAT_ROWS, SCAT_ROWS), SCAT_ROWS)
            ids = lax.broadcasted_iota(jnp.int32, (SCAT_ROWS, SLOTS), 0) + m * SCAT_ROWS
            onehot = jnp.concatenate(
                [jnp.where(ids == a, 1.0, 0.0).astype(BF16) for a in targets], axis=1
            )
            acc[span, cols] += jnp.dot(onehot, msg, **DOTS)

        loop(0, GROUP // SCAT_ROWS, some)

    def group(s):
        width = PER_SCAT * SLOTS
        return pl.ds(pl.multiple_of(s * width, width), width)

    def scatter(s):
        for u in range(PER_SCAT):
            if s * PER_SCAT + u != HERE:
                msg_copy(s * PER_SCAT + u).wait_recv()
        add_rows(s * PER_SCAT, recv[group(s), :], slice(None))

    def scatter_late(h, s):
        for u in range(PER_SCAT):
            late_copy(h, s * PER_SCAT + u).wait_recv()
        add_rows(WHOLE + s * PER_SCAT, late_recv[h, group(s), :], slice(h * HALF, h * HALF + HALF))

    def pair(to, p):
        return to * SIDE + 2 * p

    def afar_copy(d):
        return remote(afar_send.at[d], afar_recv.at[d], (af_s, af_r), d, node(1 + 2 * d, 0, 0))

    def anear_copy(d, p):
        return remote(
            anear_send.at[d, p], anear_recv.at[d, p], (an_s, an_r), 2 * d + p, node(1 + 2 * d, 0, 0)
        )

    def b_copy(d):
        return remote(
            b_send.at[at.b_at[d]], b_recv.at[d - 1], (b_s, b_r), d - 1, node(0, d, 0)
        )

    def core_sum(i):
        wg[c, i] = wg[c, i] + crecv[i].astype(F32)

    def a_first():
        core_copy.wait_recv()
        loop(0, SIDE * SIDE, core_sum)
        for d in range(2):
            for i in range(2):
                afar_send[d, i] = wg[c, pair(at.a_at[2], d) + i].astype(BF16)
            afar_copy(d).start()
        for d in range(2):
            for i in range(2):
                anear_send[d, 1 - d, i] = wg[c, pair(at.a_at[1 + 2 * d], 1 - d) + i].astype(BF16)
            anear_copy(d, 1 - d).start()

    def a_second():
        for d in range(2):
            afar_copy(d).wait_recv()
            for i in range(2):
                total = wg[c, pair(at.a_at[1 + 2 * d], d) + i] + afar_recv[d, i].astype(F32)
                anear_send[d, d, i] = total.astype(BF16)
            anear_copy(d, d).start()

    def b_first():
        for p in range(2):
            for d in range(2):
                anear_copy(d, p).wait_recv()
            for i in range(2):
                total = (
                    wg[c, pair(at.a, p) + i]
                    + anear_recv[0, p, i].astype(F32) + anear_recv[1, p, i].astype(F32)
                )
                own_sum[2 * p + i] = total
                b_send[2 * p + i] = total.astype(BF16)
        for d in range(1, SIDE):
            b_copy(d).start()

    def b_last():
        for d in range(1, SIDE):
            b_copy(d).wait_recv()
        total = own_sum[at.b]
        for d in range(SIDE - 1):
            total = total + b_recv[d].astype(F32)
        for k in range(8):
            gr[:, 128 * k:128 * k + 128] = total[8 * k:8 * k + 8, :]
        for i in range(3):
            for h in range(2):
                r0 = 64 + (2 * i + h) * 8
                gs[8 * i:8 * i + 8, 128 * h:128 * h + 128] = total[r0:r0 + 8, :]

    def towards(d):
        return lax.rem(q + (1, REL - 1)[d] * at.sign, REL)

    def rows_of(owner, p):
        return pl.ds(pl.multiple_of(owner * OWN + p * PART, PART), PART)

    def far_copy(h, d):
        return pltpu.make_async_remote_copy(
            src_ref=far_send.at[h, d], dst_ref=far_recv.at[h, d],
            send_sem=far_s.at[h, d], recv_sem=far_r.at[h, d],
            device_id={"rel": towards(d)}, device_id_type=MESH,
        )

    def near_copy(h, d, p):
        return pltpu.make_async_remote_copy(
            src_ref=near_send.at[h, d, p], dst_ref=near_recv.at[h, d, p],
            send_sem=near_s.at[h, d, p], recv_sem=near_r.at[h, d, p],
            device_id={"rel": towards(d)}, device_id_type=MESH,
        )

    def half(h):
        return slice(h * HALF, h * HALF + HALF)

    def rel_first(h):
        for d in range(2):
            far_send[h, d] = acc[rows_of(lax.rem(q + 2, REL), d), half(h)].astype(BF16)
            far_copy(h, d).start()
        for d in range(2):
            near_send[h, d, 1 - d] = acc[rows_of(towards(d), 1 - d), half(h)].astype(BF16)
            near_copy(h, d, 1 - d).start()

    def rel_second(h):
        for d in range(2):
            far_copy(h, d).wait_recv()
            mine = acc[rows_of(towards(d), d), half(h)]
            near_send[h, d, d] = (mine + far_recv[h, d].astype(F32)).astype(BF16)
            near_copy(h, d, d).start()

    def rel_last(h):
        for p in range(2):
            for d in range(2):
                near_copy(h, d, p).wait_recv()
            ga[p * PART:p * PART + PART, half(h)] = (
                acc[rows_of(q, p), half(h)]
                + near_recv[h, 0, p].astype(F32) + near_recv[h, 1, p].astype(F32)
            )

    scatter(4)
    scatter(3)
    scatter(5)
    a_first()
    scatter(0)
    scatter(1)
    a_second()
    scatter(2)
    scatter_late(0, 0)
    scatter_late(0, 1)
    rel_first(0)
    b_first()
    scatter_late(1, 0)
    rel_second(0)
    scatter_late(1, 1)
    rel_first(1)
    b_last()
    rel_last(0)
    rel_second(1)
    rel_last(1)

    core_copy.wait_send()
    each(OTHERS, lambda t: auth_copy(t).wait_send())
    each(RELAYED, lambda t: relay_copy(t).wait_send())
    each(RELAYED + DIRECT, lambda t: msg_copy(t).wait_send())
    for h in range(2):
        each(range(LATE), lambda i: late_copy(h, i).wait_send())
        for d in range(2):
            far_copy(h, d).wait_send()
            for p in range(2):
                near_copy(h, d, p).wait_send()
    for d in range(2):
        afar_copy(d).wait_send()
        for p in range(2):
            anear_copy(d, p).wait_send()
    for d in range(1, SIDE):
        b_copy(d).wait_send()


def hand_over(a, b, c, ao, bo, co):
    ao[...] = a[...]
    bo[...] = b[...]
    co[...] = c[...]


def on_device(grad_out, paper_feat, saved_agg, rel_weight, slot_paper, slot_author, block_count):
    vmem = pl.BlockSpec(memory_space=pltpu.VMEM)
    smem = pl.BlockSpec(memory_space=pltpu.SMEM)
    hbm = pl.BlockSpec(memory_space=pl.ANY)
    dma = pltpu.SemaphoreType.DMA
    limit = 56 * 1024 * 1024
    whole = (WHOLE * SLOTS, AUTH_W)
    late = (2, LATE * SLOTS, HALF)
    ga, gr, gs = pl.pallas_call(
        kernel,
        out_shape=(
            jax.ShapeDtypeStruct((OWN, AUTH_W), F32),
            jax.ShapeDtypeStruct((8, OUT_W), F32),
            jax.ShapeDtypeStruct((24, AUTH_W), F32),
        ),
        in_specs=[smem, smem, vmem, hbm, hbm, hbm, hbm],
        out_specs=(vmem, vmem, vmem),
        scratch_shapes=[
            pltpu.VMEM((AUTH_W, OUT_W), BF16),
            pltpu.VMEM((OUT_W, AUTH_W), BF16),
            pltpu.VMEM((PAPERS, OUT_W), BF16),
            pltpu.VMEM((PAPERS, PAPER_W), BF16),
            pltpu.VMEM((PAPERS, AUTH_W), BF16),
            pltpu.VMEM((2 * PAPERS, HALF), F32),
            pltpu.VMEM((2 * SLOTS, HALF), F32),
            pltpu.VMEM(whole, BF16),
            pltpu.VMEM((len(RELAYED) * SLOTS, AUTH_W), BF16),
            pltpu.VMEM(whole, BF16),
            pltpu.VMEM(late, BF16),
            pltpu.VMEM(late, BF16),
            pltpu.VMEM((NODES, 1, SLOTS), jnp.int32),
            pltpu.VMEM((GROUP, AUTH_W), F32),
            pltpu.VMEM((AUTH_W, OUT_W), F32),
            pltpu.VMEM((AUTH_W, PAPER_W), F32),
            pltpu.VMEM((CN, SIDE * SIDE, PIECE, 128), F32),
            pltpu.VMEM((SIDE * SIDE, PIECE, 128), BF16),
            pltpu.VMEM((SIDE * SIDE, PIECE, 128), BF16),
            pltpu.VMEM((2, 2, PIECE, 128), BF16),
            pltpu.VMEM((2, 2, PIECE, 128), BF16),
            pltpu.VMEM((2, 2, 2, PIECE, 128), BF16),
            pltpu.VMEM((2, 2, 2, PIECE, 128), BF16),
            pltpu.VMEM((SIDE, PIECE, 128), F32),
            pltpu.VMEM((SIDE, PIECE, 128), BF16),
            pltpu.VMEM((SIDE - 1, PIECE, 128), BF16),
            pltpu.VMEM((2, 2, PART, HALF), BF16),
            pltpu.VMEM((2, 2, PART, HALF), BF16),
            pltpu.VMEM((2, 2, 2, PART, HALF), BF16),
            pltpu.VMEM((2, 2, 2, PART, HALF), BF16),
            dma, dma((CHUNKS,)), dma((CHUNKS,)), dma((CHUNKS,)),
            dma((NODES,)), dma((NODES,)), dma((WHOLE,)), dma((WHOLE,)),
            dma((len(RELAYED),)), dma((len(RELAYED),)), dma((2 * LATE,)), dma((2 * LATE,)),
            dma, dma, dma((2,)), dma((2,)), dma((4,)), dma((4,)), dma((3,)), dma((3,)),
            dma((2, 2)), dma((2, 2)), dma((2, 2, 2)), dma((2, 2, 2)),
        ],
        compiler_params=pltpu.CompilerParams(
            collective_id=0, has_side_effects=True, vmem_limit_bytes=limit
        ),
    )(
        slot_paper[0, 0], block_count[0, 0],
        slot_author[0, 0][:, None, :], rel_weight[0], grad_out, paper_feat, saved_agg[0],
    )
    ga, gr, gs = pl.pallas_call(
        hand_over,
        out_shape=tuple(jax.ShapeDtypeStruct(v.shape, F32) for v in (ga, gr, gs)),
        in_specs=[vmem] * 3,
        out_specs=(vmem,) * 3,
    )(ga, gr, gs)
    return ga, gr[None], gs


def solution(mesh):
    return jax.shard_map(
        on_device,
        mesh=mesh,
        in_specs=(
            P("nodes", None),
            P("nodes", None),
            P("rel", "nodes", None),
            P("rel", None, None),
            P("nodes", "rel", None, None),
            P("nodes", "rel", None, None),
            P("nodes", "rel", None),
        ),
        out_specs=(P(("nodes", "rel"), None), P("rel", "nodes", None), P("nodes", "rel")),
        check_vma=False,
    )
```

```python
import jax
import jax.numpy as jnp
from jax import lax
from jax.experimental import pallas as pl
from jax.experimental.pallas import tpu as pltpu
from jax.sharding import PartitionSpec as P

MESH = pl.DeviceIdType.MESH
F32 = jnp.float32
BF16 = jnp.bfloat16
DOTS = dict(preferred_element_type=F32)

NODES, REL = 32, 4
SIDE, CN = 4, 2
PAPERS, OUT_W, AUTH_W, PAPER_W = 4608, 1024, 256, 768
SLOTS, GROUP, OWN = 128, 2048, 512
CHUNK = 768
CHUNKS = PAPERS // CHUNK
PIECE = 112
PER_SCAT = 4
SCAT_ROWS = 1024
WHOLE = 24
COPIES = 39
HALF = AUTH_W // 2
PART = OWN // 2


def chunk(k):
    return pl.ds(pl.multiple_of(k * CHUNK, CHUNK), CHUNK)


DB = (0, 1, 3, 2)
SLOT_OFFSETS = [(da, db, dc) for db in DB for dc in range(CN) for da in range(SIDE)]
HERE = 0
OTHERS = range(1, NODES)


class Place:
    def __init__(self):
        me = lax.axis_index("nodes")
        y = lax.div(me, SIDE * CN)
        z = lax.rem(lax.div(me, CN), SIDE)
        c = lax.rem(me, CN)
        self.me, self.c = me, c
        self.a, self.b = y + c * (z - y), z + c * (y - z)
        self.stride_a = SIDE * CN - (SIDE * CN - CN) * c
        self.stride_b = CN + (SIDE * CN - CN) * c
        self.sign = 1 + 2 * c
        self.a_at = [lax.rem(self.a + self.sign * k, SIDE) for k in range(SIDE)]
        self.b_at = [lax.rem(self.b + self.sign * k, SIDE) for k in range(SIDE)]
        self.a_nodes = [v * self.stride_a for v in self.a_at]
        self.b_nodes = [v * self.stride_b for v in self.b_at]
        self.cs = [c, 1 - c]

    def node(self, da, db, dc):
        return self.a_nodes[da] + self.b_nodes[db] + self.cs[dc]

    def peer(self, t):
        return self.node(*SLOT_OFFSETS[t])

    def anywhere(self, da, db, dc):
        a = lax.rem(self.a + self.sign * da, SIDE)
        b = lax.rem(self.b + self.sign * db, SIDE)
        return a * self.stride_a + b * self.stride_b + lax.rem(self.c + dc, CN)


def each(slots, body):
    for t in slots:
        body(t)


def loop(lo, hi, body):
    def step(t, _):
        body(t)
        return 0

    lax.fori_loop(lo, hi, step, 0)


def kernel(
    papers, counts, authors, w_hbm, go_hbm, pf_hbm, sa_hbm,
    ga, gr, gs,
    w, wt, g, feat, agg, table, rows, send, mid, recv, relay_p, relay_m, relay_late,
    late_send, late_mid, late_relay, late_recv, auth, acc,
    racc, sacc, wg, csend, crecv, afar_send, afar_recv, anear_send, anear_recv, own_sum, b_send, b_recv,
    far_send, far_recv, near_send, near_recv,
    wsem, gsem, fsem, asem, au_s, au_r, ms_s, ms_r,
    c_s, c_r, af_s, af_r, an_s, an_r, b_s, b_r, far_s, far_r, near_s, near_r,
):
    at = Place()
    q = lax.axis_index("rel")
    me, c, node = at.me, at.c, at.node

    def g_copy(k):
        return pltpu.make_async_copy(go_hbm.at[chunk(k)], g.at[chunk(k)], gsem.at[k])

    def f_copy(k):
        return pltpu.make_async_copy(pf_hbm.at[chunk(k)], feat.at[chunk(k)], fsem.at[k])

    def a_copy(k):
        return pltpu.make_async_copy(sa_hbm.at[chunk(k)], agg.at[chunk(k)], asem.at[k])

    def load_rest(k):
        a_copy(k).start()
        f_copy(k).start()

    w_copy = pltpu.make_async_copy(w_hbm, w, wsem)
    w_copy.start()
    loop(0, CHUNKS, lambda k: g_copy(k).start())

    barrier = pltpu.get_barrier_semaphore()

    def greet(t):
        pl.semaphore_signal(barrier, inc=1, device_id={"nodes": at.peer(t)}, device_id_type=MESH)

    each(OTHERS, greet)
    for d in (1, REL - 1):
        pl.semaphore_signal(
            barrier, inc=1, device_id={"rel": lax.rem(q + d, REL)}, device_id_type=MESH
        )

    w_copy.wait()
    wt[...] = w[...].astype(F32).T.astype(BF16)

    pl.semaphore_wait(barrier, NODES - 1 + 2)

    def remote(src, dst, sems, i, to):
        return pltpu.make_async_remote_copy(
            src_ref=src, dst_ref=dst, send_sem=sems[0].at[i], recv_sem=sems[1].at[i],
            device_id={"nodes": to}, device_id_type=MESH,
        )

    def auth_copy(t):
        return remote(authors.at[at.peer(t)], auth.at[t], (au_s, au_r), t, at.peer(t))

    each(OTHERS, lambda t: auth_copy(t).start())
    auth[HERE] = authors[me]

    def back_step(k):
        g_copy(k).wait()
        part = CHUNK // 2
        for m in range(2):
            lo = k * CHUNK + m * part
            back = jnp.dot(g[pl.ds(pl.multiple_of(lo, part), part), :], wt[...], **DOTS)
            for h in range(2):
                table[pl.ds(2 * lo + h, part, stride=2), :] = back[:, h * HALF:h * HALF + HALF]

    loop(0, CHUNKS, back_step)
    loop(0, CHUNKS, load_rest)
    copies = {}

    def link(key, src, dst, *offset):
        copies[key] = remote(src, dst, (ms_s, ms_r), len(copies), node(*offset))

    def start(*keys):
        for key in keys:
            copies[key].start()

    def arrived(*keys):
        for key in keys:
            copies[key].wait_recv()

    link("a2+", send.at[0:2, :, 2], relay_p, 1, 0, 0)
    link("a2-", send.at[2, :, 2], relay_m, 3, 0, 0)
    link("a2late", late_send.at[:, :, 2], relay_late, 3, 0, 0)
    for da in (1, 3):
        link(("a", da), send.at[1:3, :, da], mid.at[1:3, :, da], da, 0, 0)
        link(("alate", da), late_send.at[:, :, da], late_mid.at[:, :, da], da, 0, 0)
        for dc in range(CN):
            link(("direct", da, dc), send.at[0, dc, da], recv.at[0, dc, da], da, 0, dc)
    link("core", send.at[0, 1, 0], recv.at[0, 1, 0], 0, 0, 1)
    link("f+", relay_p.at[1], mid.at[1, :, 2], 1, 0, 0)
    for dc in range(CN):
        link(("f0", dc), relay_p.at[0, dc], recv.at[0, dc, 2], 1, 0, dc)
    link("f-", relay_m, mid.at[2, :, 2], 3, 0, 0)
    link("flate", relay_late, late_mid.at[:, :, 2], 3, 0, 0)
    for i, db in ((1, 1), (2, 3)):
        for dc in range(CN):
            link(("own", i, dc), send.at[i, dc, 0], recv.at[i, dc, 0], 0, db, dc)
            link(("mid", i, dc), mid.at[i, dc, 1:4], recv.at[i, dc, 1:4], 0, db, dc)
    for h in range(2):
        link(("l0", h), late_send.at[h, :, 0], late_relay.at[h, :, 0], 0, 1, 0)
        link(("l1", h), late_mid.at[h, :, 1], late_relay.at[h, :, 1], 0, 1, 0)
        link(("l2", h), late_mid.at[h, :, 2:4], late_relay.at[h, :, 2:4], 0, 3, 0)
        for dc in range(CN):
            link(("lf+", h, dc), late_relay.at[h, dc, 0:2], late_recv.at[h, dc, 0:2], 0, 1, dc)
            link(("lf-", h, dc), late_relay.at[h, dc, 2:4], late_recv.at[h, dc, 2:4], 0, 3, dc)

    def gather(b):
        for u in range(SLOTS):
            p = papers[b, u] * 2
            rows[2 * u:2 * u + 2, :] = table[pl.ds(p, 2), :]
        live = counts[b]
        scale = lax.rsqrt(jnp.full((1, HALF), live, jnp.int32).astype(F32))
        slot = lax.broadcasted_iota(jnp.int32, (SLOTS, HALF), 0)
        return [
            jnp.where(slot < live, rows[pl.ds(h, SLOTS, stride=2), :] * scale, 0.0).astype(BF16)
            for h in range(2)
        ]

    def whole(i, db, dc, da):
        left, right = gather(at.anywhere(da, db, dc))
        send[i, dc, da, :, :HALF] = left
        send[i, dc, da, :, HALF:] = right

    def late(dc, da):
        left, right = gather(at.anywhere(da, 2, dc))
        late_send[0, dc, da] = left
        late_send[1, dc, da] = right

    def two(j):
        return lax.div(j, 2), lax.rem(j, 2)

    def sides(da):
        def body(j):
            i, dc = two(j)
            whole(1 + i, 1 + 2 * i, dc, da)

        loop(0, 4, body)

    def body_a2(j):
        i, dc = two(j)
        whole(i, i, dc, 2)

    def body_direct(j):
        i, dc = two(j)
        whole(0, 0, dc, 1 + 2 * i)

    def body_late(j):
        i, dc = two(j)
        late(dc, 1 + 2 * i)

    loop(0, 4, body_a2)
    start("a2+")
    loop(0, 2, lambda dc: whole(2, 3, dc, 2))
    loop(0, 2, lambda dc: late(dc, 2))
    start("a2-", "a2late")
    for da in (1, 3):
        sides(da)
        start(("a", da))
    loop(0, 4, body_late)
    start(("alate", 1), ("alate", 3))
    loop(0, 4, body_direct)
    start(*[("direct", da, dc) for da in (1, 3) for dc in range(CN)])
    loop(0, 2, lambda dc: late(dc, 0))
    start(("l0", 0), ("l0", 1))
    sides(0)
    start(*[("own", i, dc) for i in (1, 2) for dc in range(CN)])
    loop(0, 2, lambda dc: whole(0, 0, dc, 0))
    start("core")
    recv[0, 0, 0] = send[0, 0, 0]

    racc[...] = jnp.zeros_like(racc)
    sacc[...] = jnp.zeros_like(sacc)
    cols = pl.ds(pl.multiple_of(q * AUTH_W, AUTH_W), AUTH_W)
    over0 = (((0,), (0,)), ((), ()))

    def grads_step(k):
        a_copy(k).wait()
        f_copy(k).wait()
        racc[...] += lax.dot_general(agg[chunk(k), :], g[chunk(k), :], over0, **DOTS)
        sacc[...] += lax.dot_general(g[chunk(k), cols], feat[chunk(k), :], over0, **DOTS)

    loop(0, 1, grads_step)
    arrived("a2+", "a2-", "a2late")
    start("flate", "f-", "f+", ("f0", 0), ("f0", 1))
    loop(1, CHUNKS, grads_step)
    arrived(("a", 1), ("a", 3), ("alate", 1), ("alate", 3), "flate", "f-", "f+")
    start(*[(key, h) for h in range(2) for key in ("l1", "l2")])
    start(*[("mid", i, dc) for dc in range(CN) for i in (1, 2)])

    sacc_t = sacc[...].T
    for n in range(NODES):
        co, y, z = n % CN, n // CN // SIDE, n // CN % SIDE
        ab = (y * SIDE + z, z * SIDE + y)[co]
        for k in range(8):
            wg[co, ab, 8 * k:8 * k + 8, :] = racc[8 * n:8 * n + 8, 128 * k:128 * k + 128]
        for i in range(3):
            for h in range(2):
                r0 = 64 + (2 * i + h) * 8
                wg[co, ab, r0:r0 + 8, :] = sacc_t[24 * n + 8 * i:24 * n + 8 * i + 8, 128 * h:128 * h + 128]

    core_copy = pltpu.make_async_remote_copy(
        src_ref=csend, dst_ref=crecv, send_sem=c_s, recv_sem=c_r,
        device_id={"nodes": node(0, 0, 1)}, device_id_type=MESH,
    )

    def core_round(i):
        csend[i] = wg[1 - c, i].astype(BF16)

    loop(0, SIDE * SIDE, core_round)
    core_copy.start()

    acc[...] = jnp.zeros_like(acc)
    each(OTHERS, lambda t: auth_copy(t).wait_recv())

    def add_rows(first_slot, msg, cols):
        targets = [auth[first_slot + u] for u in range(PER_SCAT)]

        def some(m):
            span = pl.ds(pl.multiple_of(m * SCAT_ROWS, SCAT_ROWS), SCAT_ROWS)
            ids = lax.broadcasted_iota(jnp.int32, (SCAT_ROWS, SLOTS), 0) + m * SCAT_ROWS
            onehot = jnp.concatenate(
                [jnp.where(ids == a, 1.0, 0.0).astype(BF16) for a in targets], axis=1
            )
            acc[span, cols] += jnp.dot(onehot, msg, **DOTS)

        loop(0, GROUP // SCAT_ROWS, some)

    def scatter(i, dc):
        if i == 0:
            arrived(("direct", 1, dc), ("direct", 3, dc), ("f0", dc))
            if dc == 1:
                arrived("core")
        else:
            arrived(("own", i, dc), ("mid", i, dc))
        add_rows((i * CN + dc) * 4, recv[i, dc].reshape(4 * SLOTS, AUTH_W), slice(None))

    def scatter_late(h, dc):
        arrived(("lf+", h, dc), ("lf-", h, dc))
        msg = late_recv[h, dc].reshape(4 * SLOTS, HALF)
        add_rows(WHOLE + dc * 4, msg, slice(h * HALF, h * HALF + HALF))

    def forward_late(h):
        arrived(("l0", h), ("l1", h), ("l2", h))
        start(*[(key, h, dc) for dc in range(CN) for key in ("lf+", "lf-")])

    def pair(to, p):
        return to * SIDE + 2 * p

    def afar_copy(d):
        return remote(afar_send.at[d], afar_recv.at[d], (af_s, af_r), d, node(1 + 2 * d, 0, 0))

    def anear_copy(d, p):
        return remote(
            anear_send.at[d, p], anear_recv.at[d, p], (an_s, an_r), 2 * d + p, node(1 + 2 * d, 0, 0)
        )

    def b_copy(d):
        return remote(
            b_send.at[at.b_at[d]], b_recv.at[d - 1], (b_s, b_r), d - 1, node(0, d, 0)
        )

    def core_sum(i):
        wg[c, i] = wg[c, i] + crecv[i].astype(F32)

    def a_first():
        core_copy.wait_recv()
        loop(0, SIDE * SIDE, core_sum)
        for d in range(2):
            for i in range(2):
                afar_send[d, i] = wg[c, pair(at.a_at[2], d) + i].astype(BF16)
            afar_copy(d).start()
        for d in range(2):
            for i in range(2):
                anear_send[d, 1 - d, i] = wg[c, pair(at.a_at[1 + 2 * d], 1 - d) + i].astype(BF16)
            anear_copy(d, 1 - d).start()

    def a_second():
        for d in range(2):
            afar_copy(d).wait_recv()
            for i in range(2):
                total = wg[c, pair(at.a_at[1 + 2 * d], d) + i] + afar_recv[d, i].astype(F32)
                anear_send[d, d, i] = total.astype(BF16)
            anear_copy(d, d).start()

    def b_first():
        for p in range(2):
            for d in range(2):
                anear_copy(d, p).wait_recv()
            for i in range(2):
                total = (
                    wg[c, pair(at.a, p) + i]
                    + anear_recv[0, p, i].astype(F32) + anear_recv[1, p, i].astype(F32)
                )
                own_sum[2 * p + i] = total
                b_send[2 * p + i] = total.astype(BF16)
        for d in range(1, SIDE):
            b_copy(d).start()

    def b_last():
        for d in range(1, SIDE):
            b_copy(d).wait_recv()
        total = own_sum[at.b]
        for d in range(SIDE - 1):
            total = total + b_recv[d].astype(F32)
        for k in range(8):
            gr[:, 128 * k:128 * k + 128] = total[8 * k:8 * k + 8, :]
        for i in range(3):
            for h in range(2):
                r0 = 64 + (2 * i + h) * 8
                gs[8 * i:8 * i + 8, 128 * h:128 * h + 128] = total[r0:r0 + 8, :]

    def towards(d):
        return lax.rem(q + (1, REL - 1)[d] * at.sign, REL)

    def rows_of(owner, p):
        return pl.ds(pl.multiple_of(owner * OWN + p * PART, PART), PART)

    def far_copy(h, d):
        return pltpu.make_async_remote_copy(
            src_ref=far_send.at[h, d], dst_ref=far_recv.at[h, d],
            send_sem=far_s.at[h, d], recv_sem=far_r.at[h, d],
            device_id={"rel": towards(d)}, device_id_type=MESH,
        )

    def near_copy(h, d, p):
        return pltpu.make_async_remote_copy(
            src_ref=near_send.at[h, d, p], dst_ref=near_recv.at[h, d, p],
            send_sem=near_s.at[h, d, p], recv_sem=near_r.at[h, d, p],
            device_id={"rel": towards(d)}, device_id_type=MESH,
        )

    def half(h):
        return slice(h * HALF, h * HALF + HALF)

    def rel_first(h):
        for d in range(2):
            far_send[h, d] = acc[rows_of(lax.rem(q + 2, REL), d), half(h)].astype(BF16)
            far_copy(h, d).start()
        for d in range(2):
            near_send[h, d, 1 - d] = acc[rows_of(towards(d), 1 - d), half(h)].astype(BF16)
            near_copy(h, d, 1 - d).start()

    def rel_second(h):
        for d in range(2):
            far_copy(h, d).wait_recv()
            mine = acc[rows_of(towards(d), d), half(h)]
            near_send[h, d, d] = (mine + far_recv[h, d].astype(F32)).astype(BF16)
            near_copy(h, d, d).start()

    def rel_last(h):
        for p in range(2):
            for d in range(2):
                near_copy(h, d, p).wait_recv()
            ga[p * PART:p * PART + PART, half(h)] = (
                acc[rows_of(q, p), half(h)]
                + near_recv[h, 0, p].astype(F32) + near_recv[h, 1, p].astype(F32)
            )

    scatter(0, 0)
    scatter(0, 1)
    forward_late(0)
    forward_late(1)
    a_first()
    scatter(1, 0)
    scatter(2, 0)
    a_second()
    scatter(1, 1)
    scatter(2, 1)
    scatter_late(0, 0)
    scatter_late(0, 1)
    rel_first(0)
    b_first()
    scatter_late(1, 0)
    rel_second(0)
    scatter_late(1, 1)
    rel_first(1)
    b_last()
    rel_last(0)
    rel_second(1)
    rel_last(1)

    core_copy.wait_send()
    each(OTHERS, lambda t: auth_copy(t).wait_send())
    for copy in copies.values():
        copy.wait_send()
    for h in range(2):
        for d in range(2):
            far_copy(h, d).wait_send()
            for p in range(2):
                near_copy(h, d, p).wait_send()
    for d in range(2):
        afar_copy(d).wait_send()
        for p in range(2):
            anear_copy(d, p).wait_send()
    for d in range(1, SIDE):
        b_copy(d).wait_send()


def hand_over(a, b, c, ao, bo, co):
    ao[...] = a[...]
    bo[...] = b[...]
    co[...] = c[...]


def on_device(grad_out, paper_feat, saved_agg, rel_weight, slot_paper, slot_author, block_count):
    vmem = pl.BlockSpec(memory_space=pltpu.VMEM)
    smem = pl.BlockSpec(memory_space=pltpu.SMEM)
    hbm = pl.BlockSpec(memory_space=pl.ANY)
    dma = pltpu.SemaphoreType.DMA
    limit = 56 * 1024 * 1024
    whole = (3, CN, SIDE, SLOTS, AUTH_W)
    late = (2, CN, SIDE, SLOTS, HALF)
    ga, gr, gs = pl.pallas_call(
        kernel,
        out_shape=(
            jax.ShapeDtypeStruct((OWN, AUTH_W), F32),
            jax.ShapeDtypeStruct((8, OUT_W), F32),
            jax.ShapeDtypeStruct((24, AUTH_W), F32),
        ),
        in_specs=[smem, smem, vmem, hbm, hbm, hbm, hbm],
        out_specs=(vmem, vmem, vmem),
        scratch_shapes=[
            pltpu.VMEM((AUTH_W, OUT_W), BF16),
            pltpu.VMEM((OUT_W, AUTH_W), BF16),
            pltpu.VMEM((PAPERS, OUT_W), BF16),
            pltpu.VMEM((PAPERS, PAPER_W), BF16),
            pltpu.VMEM((PAPERS, AUTH_W), BF16),
            pltpu.VMEM((2 * PAPERS, HALF), F32),
            pltpu.VMEM((2 * SLOTS, HALF), F32),
            pltpu.VMEM(whole, BF16),
            pltpu.VMEM(whole, BF16),
            pltpu.VMEM(whole, BF16),
            pltpu.VMEM((2, CN, SLOTS, AUTH_W), BF16),
            pltpu.VMEM((CN, SLOTS, AUTH_W), BF16),
            pltpu.VMEM((2, CN, SLOTS, HALF), BF16),
            pltpu.VMEM(late, BF16),
            pltpu.VMEM(late, BF16),
            pltpu.VMEM(late, BF16),
            pltpu.VMEM(late, BF16),
            pltpu.VMEM((NODES, 1, SLOTS), jnp.int32),
            pltpu.VMEM((GROUP, AUTH_W), F32),
            pltpu.VMEM((AUTH_W, OUT_W), F32),
            pltpu.VMEM((AUTH_W, PAPER_W), F32),
            pltpu.VMEM((CN, SIDE * SIDE, PIECE, 128), F32),
            pltpu.VMEM((SIDE * SIDE, PIECE, 128), BF16),
            pltpu.VMEM((SIDE * SIDE, PIECE, 128), BF16),
            pltpu.VMEM((2, 2, PIECE, 128), BF16),
            pltpu.VMEM((2, 2, PIECE, 128), BF16),
            pltpu.VMEM((2, 2, 2, PIECE, 128), BF16),
            pltpu.VMEM((2, 2, 2, PIECE, 128), BF16),
            pltpu.VMEM((SIDE, PIECE, 128), F32),
            pltpu.VMEM((SIDE, PIECE, 128), BF16),
            pltpu.VMEM((SIDE - 1, PIECE, 128), BF16),
            pltpu.VMEM((2, 2, PART, HALF), BF16),
            pltpu.VMEM((2, 2, PART, HALF), BF16),
            pltpu.VMEM((2, 2, 2, PART, HALF), BF16),
            pltpu.VMEM((2, 2, 2, PART, HALF), BF16),
            dma, dma((CHUNKS,)), dma((CHUNKS,)), dma((CHUNKS,)),
            dma((NODES,)), dma((NODES,)), dma((COPIES,)), dma((COPIES,)),
            dma, dma, dma((2,)), dma((2,)), dma((4,)), dma((4,)), dma((3,)), dma((3,)),
            dma((2, 2)), dma((2, 2)), dma((2, 2, 2)), dma((2, 2, 2)),
        ],
        compiler_params=pltpu.CompilerParams(
            collective_id=0, has_side_effects=True, vmem_limit_bytes=limit
        ),
    )(
        slot_paper[0, 0], block_count[0, 0],
        slot_author[0, 0][:, None, :], rel_weight[0], grad_out, paper_feat, saved_agg[0],
    )
    ga, gr, gs = pl.pallas_call(
        hand_over,
        out_shape=tuple(jax.ShapeDtypeStruct(v.shape, F32) for v in (ga, gr, gs)),
        in_specs=[vmem] * 3,
        out_specs=(vmem,) * 3,
    )(ga, gr, gs)
    return ga, gr[None], gs


def solution(mesh):
    return jax.shard_map(
        on_device,
        mesh=mesh,
        in_specs=(
            P("nodes", None),
            P("nodes", None),
            P("rel", "nodes", None),
            P("rel", None, None),
            P("nodes", "rel", None, None),
            P("nodes", "rel", None, None),
            P("nodes", "rel", None),
        ),
        out_specs=(P(("nodes", "rel"), None), P("rel", "nodes", None), P("nodes", "rel")),
        check_vma=False,
    )
```

```python
import jax
import jax.numpy as jnp
from jax import lax
from jax.experimental import pallas as pl
from jax.experimental.pallas import tpu as pltpu
from jax.sharding import PartitionSpec as P

MESH = pl.DeviceIdType.MESH
F32 = jnp.float32
BF16 = jnp.bfloat16
DOTS = dict(preferred_element_type=F32)

NODES, REL = 32, 4
SIDE, CN = 4, 2
PAPERS, OUT_W, AUTH_W, PAPER_W = 4608, 1024, 256, 768
SLOTS, GROUP, OWN = 128, 2048, 512
CHUNK = 768
CHUNKS = PAPERS // CHUNK
STEP = 384
STEPS = PAPERS // STEP
AHEAD = 5
PIECE = 112
PER_SCAT = 4
SCAT_ROWS = 1024
WHOLE = 20
LATE = NODES - WHOLE
HALF = AUTH_W // 2
PART = OWN // 2


def chunk(k):
    return pl.ds(pl.multiple_of(k * CHUNK, CHUNK), CHUNK)


def block(t):
    if isinstance(t, int):
        return pl.ds(t * SLOTS, SLOTS)
    return pl.ds(pl.multiple_of(t * SLOTS, SLOTS), SLOTS)


ROW, COLUMN = 0, 1
GROUPS = [(ROW, 2, 0), (COLUMN, 2), (ROW, 2, 1), (ROW, 0, 0), (ROW, 0, 1), (COLUMN, 0), (COLUMN, 1), (COLUMN, 3)]


def in_group(group, j):
    if group[0] == ROW:
        return group[1], j, group[2]
    return 1 + 2 * (j // 2), group[1], j % 2


SLOT_OFFSETS = [in_group(group, j) for group in GROUPS for j in range(4)]
HERE = SLOT_OFFSETS.index((0, 0, 0))
OTHERS = [t for t in range(NODES) if t != HERE]
RELAYED = [t for t in OTHERS if 2 in SLOT_OFFSETS[t][:2]]
DIRECT = [t for t in OTHERS if t < WHOLE and t not in RELAYED]


def first_hop(t):
    da, db, dc = SLOT_OFFSETS[t]
    ha = (1 if db < 2 else 3) if da == 2 else 0
    hb = (1 if da in (1, 2) else 3) if db == 2 else 0
    return ha, hb, 0


def second_hop(t):
    da, db, dc = SLOT_OFFSETS[t]
    ha, hb, _ = first_hop(t)
    return (da - ha) % SIDE, (db - hb) % SIDE, dc


class Place:
    def __init__(self):
        me = lax.axis_index("nodes")
        y = lax.div(me, SIDE * CN)
        z = lax.rem(lax.div(me, CN), SIDE)
        c = lax.rem(me, CN)
        self.me, self.c = me, c
        self.a, self.b = y + c * (z - y), z + c * (y - z)
        self.stride_a = SIDE * CN - (SIDE * CN - CN) * c
        self.stride_b = CN + (SIDE * CN - CN) * c
        self.sign = 1 + 2 * c
        self.a_at = [lax.rem(self.a + self.sign * k, SIDE) for k in range(SIDE)]
        self.b_at = [lax.rem(self.b + self.sign * k, SIDE) for k in range(SIDE)]
        self.a_nodes = [v * self.stride_a for v in self.a_at]
        self.b_nodes = [v * self.stride_b for v in self.b_at]
        self.cs = [c, 1 - c]

    def node(self, da, db, dc):
        return self.a_nodes[da] + self.b_nodes[db] + self.cs[dc]

    def peer(self, t):
        return self.node(*SLOT_OFFSETS[t])

    def peer_in(self, k, j):
        group = GROUPS[k]
        if group[0] == ROW:
            b = lax.rem(self.b + self.sign * j, SIDE)
            return self.a_nodes[group[1]] + b * self.stride_b + self.cs[group[2]]
        a = lax.rem(self.a + self.sign * (1 + 2 * lax.div(j, 2)), SIDE)
        return a * self.stride_a + self.b_nodes[group[1]] + lax.rem(self.c + lax.rem(j, 2), CN)


def each(slots, body):
    for t in slots:
        body(t)


def loop(lo, hi, body):
    def step(t, _):
        body(t)
        return 0

    lax.fori_loop(lo, hi, step, 0)


def kernel(
    papers, counts, authors, w_hbm, go_hbm, pf_hbm, sa_hbm,
    ga, gr, gs,
    w, wt, g, feat, agg, table, rows, send, relay, recv, late_send, late_recv, auth, acc,
    racc, sacc, wg, csend, crecv, afar_send, afar_recv, anear_send, anear_recv, own_sum, b_send, b_recv,
    far_send, far_recv, near_send, near_recv,
    wsem, gsem, fsem, asem, au_s, au_r, ms_s, ms_r, rl_s, rl_r, lt_s, lt_r,
    c_s, c_r, af_s, af_r, an_s, an_r, b_s, b_r, far_s, far_r, near_s, near_r,
):
    at = Place()
    q = lax.axis_index("rel")
    me, c, node = at.me, at.c, at.node

    def g_copy(k):
        span = pl.ds(pl.multiple_of(k * STEP, STEP), STEP)
        return pltpu.make_async_copy(go_hbm.at[span], g.at[span], gsem.at[k])

    def f_copy(k):
        return pltpu.make_async_copy(pf_hbm.at[chunk(k)], feat.at[chunk(k)], fsem.at[k])

    def a_copy(k):
        return pltpu.make_async_copy(sa_hbm.at[chunk(k)], agg.at[chunk(k)], asem.at[k])

    def load_rest(k):
        a_copy(k).start()
        f_copy(k).start()

    w_copy = pltpu.make_async_copy(w_hbm, w, wsem)
    w_copy.start()
    loop(0, AHEAD, lambda k: g_copy(k).start())

    barrier = pltpu.get_barrier_semaphore()

    def greet(t):
        pl.semaphore_signal(barrier, inc=1, device_id={"nodes": at.peer(t)}, device_id_type=MESH)

    each(OTHERS, greet)
    for d in (1, REL - 1):
        pl.semaphore_signal(
            barrier, inc=1, device_id={"rel": lax.rem(q + d, REL)}, device_id_type=MESH
        )

    w_copy.wait()
    wt[...] = w[...].astype(F32).T.astype(BF16)

    pl.semaphore_wait(barrier, NODES - 1 + 2)

    def remote(src, dst, sems, i, to):
        return pltpu.make_async_remote_copy(
            src_ref=src, dst_ref=dst, send_sem=sems[0].at[i], recv_sem=sems[1].at[i],
            device_id={"nodes": to}, device_id_type=MESH,
        )

    def auth_copy(t):
        return pltpu.make_async_remote_copy(
            src_ref=authors.at[at.peer(t)], dst_ref=auth.at[t], send_sem=au_s, recv_sem=au_r,
            device_id={"nodes": at.peer(t)}, device_id_type=MESH,
        )

    def all_authors(sem):
        rows_of_all = auth.at[0:NODES - 1]
        pltpu.make_async_copy(rows_of_all, rows_of_all, sem).wait()

    def back_step(k):
        g_copy(k).wait()

        @pl.when(k + AHEAD < STEPS)
        def _():
            g_copy(k + AHEAD).start()

        lo = pl.multiple_of(k * STEP, STEP)
        back = jnp.dot(g[pl.ds(lo, STEP), :], wt[...], **DOTS)
        for h in range(2):
            table[pl.ds(2 * lo + h, STEP, stride=2), :] = back[:, h * HALF:h * HALF + HALF]

    loop(0, STEPS, back_step)
    loop(0, CHUNKS, load_rest)
    def relay_copy(t):
        i = RELAYED.index(t)
        return remote(send.at[block(t)], relay.at[block(i)], (rl_s, rl_r), i, node(*first_hop(t)))

    def msg_copy(t):
        if t in RELAYED:
            source, to = relay.at[block(RELAYED.index(t))], node(*second_hop(t))
        else:
            source, to = send.at[block(t)], at.peer(t)
        return remote(source, recv.at[block(t)], (ms_s, ms_r), t, to)

    def late_copy(h, i):
        return remote(
            late_send.at[h, block(i)], late_recv.at[h, block(i)],
            (lt_s, lt_r), h * LATE + i, at.peer(WHOLE + i),
        )

    def gather(b):
        for u in range(SLOTS):
            p = papers[b, u] * 2
            rows[2 * u:2 * u + 2, :] = table[pl.ds(p, 2), :]
        live = counts[b]
        scale = lax.rsqrt(jnp.full((1, HALF), live, jnp.int32).astype(F32))
        slot = lax.broadcasted_iota(jnp.int32, (SLOTS, HALF), 0)
        return [
            jnp.where(slot < live, rows[pl.ds(h, SLOTS, stride=2), :] * scale, 0.0).astype(BF16)
            for h in range(2)
        ]

    for k in range(WHOLE // 4):

        def whole_step(j):
            left, right = gather(at.peer_in(k, j))
            send[block(k * 4 + j), :HALF] = left
            send[block(k * 4 + j), HALF:] = right

        loop(0, 4, whole_step)
        for t in range(k * 4, k * 4 + 4):
            if t in RELAYED:
                relay_copy(t).start()
            elif t != HERE:
                msg_copy(t).start()
    for k in range(LATE // 4):

        def late_step(j):
            left, right = gather(at.peer_in(WHOLE // 4 + k, j))
            late_send[0, block(k * 4 + j), :] = left
            late_send[1, block(k * 4 + j), :] = right

        loop(0, 4, late_step)
    each(OTHERS, lambda t: auth_copy(t).start())
    auth[HERE] = authors[me]
    recv[block(HERE), :] = send[block(HERE), :]

    racc[...] = jnp.zeros_like(racc)
    sacc[...] = jnp.zeros_like(sacc)
    cols = pl.ds(pl.multiple_of(q * AUTH_W, AUTH_W), AUTH_W)
    over0 = (((0,), (0,)), ((), ()))

    def grads_step(k):
        a_copy(k).wait()
        f_copy(k).wait()
        racc[...] += lax.dot_general(agg[chunk(k), :], g[chunk(k), :], over0, **DOTS)
        sacc[...] += lax.dot_general(g[chunk(k), cols], feat[chunk(k), :], over0, **DOTS)

    def forward(t):
        relay_copy(t).wait_recv()
        msg_copy(t).start()

    loop(0, 2, grads_step)
    each(RELAYED, forward)
    for h in range(2):
        each(range(LATE), lambda i: late_copy(h, i).start())
    loop(2, CHUNKS, grads_step)

    sacc_t = sacc[...].T
    for n in range(NODES):
        co, y, z = n % CN, n // CN // SIDE, n // CN % SIDE
        ab = (y * SIDE + z, z * SIDE + y)[co]
        for k in range(8):
            wg[co, ab, 8 * k:8 * k + 8, :] = racc[8 * n:8 * n + 8, 128 * k:128 * k + 128]
        for i in range(3):
            for h in range(2):
                r0 = 64 + (2 * i + h) * 8
                wg[co, ab, r0:r0 + 8, :] = sacc_t[24 * n + 8 * i:24 * n + 8 * i + 8, 128 * h:128 * h + 128]

    core_copy = pltpu.make_async_remote_copy(
        src_ref=csend, dst_ref=crecv, send_sem=c_s, recv_sem=c_r,
        device_id={"nodes": node(0, 0, 1)}, device_id_type=MESH,
    )

    def core_round(i):
        csend[i] = wg[1 - c, i].astype(BF16)

    loop(0, SIDE * SIDE, core_round)
    core_copy.start()

    acc[...] = jnp.zeros_like(acc)
    all_authors(au_r)

    def add_rows(first_slot, msg, cols):
        targets = [auth[first_slot + u] for u in range(PER_SCAT)]

        def some(m):
            span = pl.ds(pl.multiple_of(m * SCAT_ROWS, SCAT_ROWS), SCAT_ROWS)
            ids = lax.broadcasted_iota(jnp.int32, (SCAT_ROWS, SLOTS), 0) + m * SCAT_ROWS
            onehot = jnp.concatenate(
                [jnp.where(ids == a, 1.0, 0.0).astype(BF16) for a in targets], axis=1
            )
            acc[span, cols] += jnp.dot(onehot, msg, **DOTS)

        loop(0, GROUP // SCAT_ROWS, some)

    def group(s):
        width = PER_SCAT * SLOTS
        return pl.ds(pl.multiple_of(s * width, width), width)

    def scatter(s):
        for u in range(PER_SCAT):
            if s * PER_SCAT + u != HERE:
                msg_copy(s * PER_SCAT + u).wait_recv()
        add_rows(s * PER_SCAT, recv[group(s), :], slice(None))

    def scatter_late(h, s):
        for u in range(PER_SCAT):
            late_copy(h, s * PER_SCAT + u).wait_recv()
        add_rows(WHOLE + s * PER_SCAT, late_recv[h, group(s), :], slice(h * HALF, h * HALF + HALF))

    def pair(to, p):
        return to * SIDE + 2 * p

    def afar_copy(d):
        return remote(afar_send.at[d], afar_recv.at[d], (af_s, af_r), d, node(1 + 2 * d, 0, 0))

    def anear_copy(d, p):
        return remote(
            anear_send.at[d, p], anear_recv.at[d, p], (an_s, an_r), 2 * d + p, node(1 + 2 * d, 0, 0)
        )

    def b_copy(d):
        return remote(
            b_send.at[at.b_at[d]], b_recv.at[d - 1], (b_s, b_r), d - 1, node(0, d, 0)
        )

    def core_sum(i):
        wg[c, i] = wg[c, i] + crecv[i].astype(F32)

    def a_first():
        core_copy.wait_recv()
        loop(0, SIDE * SIDE, core_sum)
        for d in range(2):
            for i in range(2):
                afar_send[d, i] = wg[c, pair(at.a_at[2], d) + i].astype(BF16)
            afar_copy(d).start()
        for d in range(2):
            for i in range(2):
                anear_send[d, 1 - d, i] = wg[c, pair(at.a_at[1 + 2 * d], 1 - d) + i].astype(BF16)
            anear_copy(d, 1 - d).start()

    def a_second():
        for d in range(2):
            afar_copy(d).wait_recv()
            for i in range(2):
                total = wg[c, pair(at.a_at[1 + 2 * d], d) + i] + afar_recv[d, i].astype(F32)
                anear_send[d, d, i] = total.astype(BF16)
            anear_copy(d, d).start()

    def b_first():
        for p in range(2):
            for d in range(2):
                anear_copy(d, p).wait_recv()
            for i in range(2):
                total = (
                    wg[c, pair(at.a, p) + i]
                    + anear_recv[0, p, i].astype(F32) + anear_recv[1, p, i].astype(F32)
                )
                own_sum[2 * p + i] = total
                b_send[2 * p + i] = total.astype(BF16)
        for d in range(1, SIDE):
            b_copy(d).start()

    def b_last():
        for d in range(1, SIDE):
            b_copy(d).wait_recv()
        total = own_sum[at.b]
        for d in range(SIDE - 1):
            total = total + b_recv[d].astype(F32)
        for k in range(8):
            gr[:, 128 * k:128 * k + 128] = total[8 * k:8 * k + 8, :]
        for i in range(3):
            for h in range(2):
                r0 = 64 + (2 * i + h) * 8
                gs[8 * i:8 * i + 8, 128 * h:128 * h + 128] = total[r0:r0 + 8, :]

    def towards(d):
        return lax.rem(q + (1, REL - 1)[d] * at.sign, REL)

    def rows_of(owner, p):
        return pl.ds(pl.multiple_of(owner * OWN + p * PART, PART), PART)

    def far_copy(h, d):
        return pltpu.make_async_remote_copy(
            src_ref=far_send.at[h, d], dst_ref=far_recv.at[h, d],
            send_sem=far_s.at[h, d], recv_sem=far_r.at[h, d],
            device_id={"rel": towards(d)}, device_id_type=MESH,
        )

    def near_copy(h, d, p):
        return pltpu.make_async_remote_copy(
            src_ref=near_send.at[h, d, p], dst_ref=near_recv.at[h, d, p],
            send_sem=near_s.at[h, d, p], recv_sem=near_r.at[h, d, p],
            device_id={"rel": towards(d)}, device_id_type=MESH,
        )

    def half(h):
        return slice(h * HALF, h * HALF + HALF)

    def rel_first(h):
        for d in range(2):
            far_send[h, d] = acc[rows_of(lax.rem(q + 2, REL), d), half(h)].astype(BF16)
            far_copy(h, d).start()
        for d in range(2):
            near_send[h, d, 1 - d] = acc[rows_of(towards(d), 1 - d), half(h)].astype(BF16)
            near_copy(h, d, 1 - d).start()

    def rel_second(h):
        for d in range(2):
            far_copy(h, d).wait_recv()
            mine = acc[rows_of(towards(d), d), half(h)]
            near_send[h, d, d] = (mine + far_recv[h, d].astype(F32)).astype(BF16)
            near_copy(h, d, d).start()

    def rel_last(h):
        for p in range(2):
            for d in range(2):
                near_copy(h, d, p).wait_recv()
            ga[p * PART:p * PART + PART, half(h)] = (
                acc[rows_of(q, p), half(h)]
                + near_recv[h, 0, p].astype(F32) + near_recv[h, 1, p].astype(F32)
            )

    scatter(3)
    scatter(4)
    for i in range(3):
        scatter(i)
    for i in range(LATE // PER_SCAT):
        scatter_late(0, i)
    rel_first(0)
    scatter_late(1, 0)
    rel_second(0)
    a_first()
    for i in range(1, LATE // PER_SCAT):
        scatter_late(1, i)
    rel_first(1)
    a_second()
    rel_last(0)
    rel_second(1)
    b_first()
    all_authors(au_s)
    each(RELAYED, lambda t: relay_copy(t).wait_send())
    each(RELAYED + DIRECT, lambda t: msg_copy(t).wait_send())
    for h in range(2):
        each(range(LATE), lambda i: late_copy(h, i).wait_send())
    core_copy.wait_send()
    b_last()
    rel_last(1)

    for h in range(2):
        for d in range(2):
            far_copy(h, d).wait_send()
            for p in range(2):
                near_copy(h, d, p).wait_send()
    for d in range(2):
        afar_copy(d).wait_send()
        for p in range(2):
            anear_copy(d, p).wait_send()
    for d in range(1, SIDE):
        b_copy(d).wait_send()


def hand_over(a, b, c, ao, bo, co):
    ao[...] = a[...]
    bo[...] = b[...]
    co[...] = c[...]


def on_device(grad_out, paper_feat, saved_agg, rel_weight, slot_paper, slot_author, block_count):
    vmem = pl.BlockSpec(memory_space=pltpu.VMEM)
    smem = pl.BlockSpec(memory_space=pltpu.SMEM)
    hbm = pl.BlockSpec(memory_space=pl.ANY)
    dma = pltpu.SemaphoreType.DMA
    limit = 56 * 1024 * 1024
    whole = (WHOLE * SLOTS, AUTH_W)
    late = (2, LATE * SLOTS, HALF)
    ga, gr, gs = pl.pallas_call(
        kernel,
        out_shape=(
            jax.ShapeDtypeStruct((OWN, AUTH_W), F32),
            jax.ShapeDtypeStruct((8, OUT_W), F32),
            jax.ShapeDtypeStruct((24, AUTH_W), F32),
        ),
        in_specs=[smem, smem, vmem, hbm, hbm, hbm, hbm],
        out_specs=(vmem, vmem, vmem),
        scratch_shapes=[
            pltpu.VMEM((AUTH_W, OUT_W), BF16),
            pltpu.VMEM((OUT_W, AUTH_W), BF16),
            pltpu.VMEM((PAPERS, OUT_W), BF16),
            pltpu.VMEM((PAPERS, PAPER_W), BF16),
            pltpu.VMEM((PAPERS, AUTH_W), BF16),
            pltpu.VMEM((2 * PAPERS, HALF), F32),
            pltpu.VMEM((2 * SLOTS, HALF), F32),
            pltpu.VMEM(whole, BF16),
            pltpu.VMEM((len(RELAYED) * SLOTS, AUTH_W), BF16),
            pltpu.VMEM(whole, BF16),
            pltpu.VMEM(late, BF16),
            pltpu.VMEM(late, BF16),
            pltpu.VMEM((NODES, 1, SLOTS), jnp.int32),
            pltpu.VMEM((GROUP, AUTH_W), F32),
            pltpu.VMEM((AUTH_W, OUT_W), F32),
            pltpu.VMEM((AUTH_W, PAPER_W), F32),
            pltpu.VMEM((CN, SIDE * SIDE, PIECE, 128), F32),
            pltpu.VMEM((SIDE * SIDE, PIECE, 128), BF16),
            pltpu.VMEM((SIDE * SIDE, PIECE, 128), BF16),
            pltpu.VMEM((2, 2, PIECE, 128), BF16),
            pltpu.VMEM((2, 2, PIECE, 128), BF16),
            pltpu.VMEM((2, 2, 2, PIECE, 128), BF16),
            pltpu.VMEM((2, 2, 2, PIECE, 128), BF16),
            pltpu.VMEM((SIDE, PIECE, 128), F32),
            pltpu.VMEM((SIDE, PIECE, 128), BF16),
            pltpu.VMEM((SIDE - 1, PIECE, 128), BF16),
            pltpu.VMEM((2, 2, PART, HALF), BF16),
            pltpu.VMEM((2, 2, PART, HALF), BF16),
            pltpu.VMEM((2, 2, 2, PART, HALF), BF16),
            pltpu.VMEM((2, 2, 2, PART, HALF), BF16),
            dma, dma((STEPS,)), dma((CHUNKS,)), dma((CHUNKS,)),
            dma, dma, dma((WHOLE,)), dma((WHOLE,)),
            dma((len(RELAYED),)), dma((len(RELAYED),)), dma((2 * LATE,)), dma((2 * LATE,)),
            dma, dma, dma((2,)), dma((2,)), dma((4,)), dma((4,)), dma((3,)), dma((3,)),
            dma((2, 2)), dma((2, 2)), dma((2, 2, 2)), dma((2, 2, 2)),
        ],
        compiler_params=pltpu.CompilerParams(
            collective_id=0, has_side_effects=True, vmem_limit_bytes=limit
        ),
    )(
        slot_paper[0, 0], block_count[0, 0],
        slot_author[0, 0][:, None, :], rel_weight[0], grad_out, paper_feat, saved_agg[0],
    )
    ga, gr, gs = pl.pallas_call(
        hand_over,
        out_shape=tuple(jax.ShapeDtypeStruct(v.shape, F32) for v in (ga, gr, gs)),
        in_specs=[vmem] * 3,
        out_specs=(vmem,) * 3,
    )(ga, gr, gs)
    return ga, gr[None], gs


def solution(mesh):
    return jax.shard_map(
        on_device,
        mesh=mesh,
        in_specs=(
            P("nodes", None),
            P("nodes", None),
            P("rel", "nodes", None),
            P("rel", None, None),
            P("nodes", "rel", None, None),
            P("nodes", "rel", None, None),
            P("nodes", "rel", None),
        ),
        out_specs=(P(("nodes", "rel"), None), P("rel", "nodes", None), P("nodes", "rel")),
        check_vma=False,
    )
```

```python
import jax
import jax.numpy as jnp
from jax import lax
from jax.experimental import pallas as pl
from jax.experimental.pallas import tpu as pltpu
from jax.sharding import PartitionSpec as P

MESH = pl.DeviceIdType.MESH
F32 = jnp.float32
BF16 = jnp.bfloat16
DOTS = dict(preferred_element_type=F32)

NODES, REL = 32, 4
SIDE, CN = 4, 2
PAPERS, OUT_W, AUTH_W, PAPER_W = 4608, 1024, 256, 768
SLOTS, GROUP, OWN = 128, 2048, 512
CHUNK = 768
CHUNKS = PAPERS // CHUNK
STEP = 384
STEPS = PAPERS // STEP
AHEAD = 5
PIECE = 112
PER_SCAT = 4
SCAT_ROWS = 1024
WHOLE = 20
LATE = NODES - WHOLE
HALF = AUTH_W // 2
PART = OWN // 2


def chunk(k):
    return pl.ds(pl.multiple_of(k * CHUNK, CHUNK), CHUNK)


def block(t):
    if isinstance(t, int):
        return pl.ds(t * SLOTS, SLOTS)
    return pl.ds(pl.multiple_of(t * SLOTS, SLOTS), SLOTS)


ROW, COLUMN = 0, 1
GROUPS = [(ROW, 2, 0), (COLUMN, 2), (ROW, 2, 1), (ROW, 0, 0), (ROW, 0, 1), (COLUMN, 0), (COLUMN, 1), (COLUMN, 3)]


def in_group(group, j):
    if group[0] == ROW:
        return group[1], j, group[2]
    return 1 + 2 * (j // 2), group[1], j % 2


SLOT_OFFSETS = [in_group(group, j) for group in GROUPS for j in range(4)]
HERE = SLOT_OFFSETS.index((0, 0, 0))
OTHERS = [t for t in range(NODES) if t != HERE]
RELAYED = [t for t in OTHERS if 2 in SLOT_OFFSETS[t][:2]]
DIRECT = [t for t in OTHERS if t < WHOLE and t not in RELAYED]


def first_hop(t):
    da, db, dc = SLOT_OFFSETS[t]
    ha = (1 if db < 2 else 3) if da == 2 else 0
    hb = (1 if da in (1, 2) else 3) if db == 2 else 0
    return ha, hb, 0


def second_hop(t):
    da, db, dc = SLOT_OFFSETS[t]
    ha, hb, _ = first_hop(t)
    return (da - ha) % SIDE, (db - hb) % SIDE, dc


class Place:
    def __init__(self):
        me = lax.axis_index("nodes")
        y = lax.div(me, SIDE * CN)
        z = lax.rem(lax.div(me, CN), SIDE)
        c = lax.rem(me, CN)
        self.me, self.c = me, c
        self.a, self.b = y + c * (z - y), z + c * (y - z)
        self.stride_a = SIDE * CN - (SIDE * CN - CN) * c
        self.stride_b = CN + (SIDE * CN - CN) * c
        self.sign = 1 + 2 * c
        self.a_at = [lax.rem(self.a + self.sign * k, SIDE) for k in range(SIDE)]
        self.b_at = [lax.rem(self.b + self.sign * k, SIDE) for k in range(SIDE)]
        self.a_nodes = [v * self.stride_a for v in self.a_at]
        self.b_nodes = [v * self.stride_b for v in self.b_at]
        self.cs = [c, 1 - c]

    def node(self, da, db, dc):
        return self.a_nodes[da] + self.b_nodes[db] + self.cs[dc]

    def peer(self, t):
        return self.node(*SLOT_OFFSETS[t])

    def peer_in(self, k, j):
        group = GROUPS[k]
        if group[0] == ROW:
            b = lax.rem(self.b + self.sign * j, SIDE)
            return self.a_nodes[group[1]] + b * self.stride_b + self.cs[group[2]]
        a = lax.rem(self.a + self.sign * (1 + 2 * lax.div(j, 2)), SIDE)
        return a * self.stride_a + self.b_nodes[group[1]] + lax.rem(self.c + lax.rem(j, 2), CN)


def each(slots, body):
    for t in slots:
        body(t)


def loop(lo, hi, body):
    def step(t, _):
        body(t)
        return 0

    lax.fori_loop(lo, hi, step, 0)


def kernel(
    papers, counts, authors, w_hbm, go_hbm, pf_hbm, sa_hbm,
    ga, gr, gs,
    w, wt, g, feat, agg, table, rows, send, relay, recv, late_send, late_recv, late_hot, auth, acc,
    racc, sacc, wg, csend, crecv, afar_send, afar_recv, anear_send, anear_recv, own_sum, b_send, b_recv,
    far_send, far_recv, near_send, near_recv,
    wsem, gsem, fsem, asem, au_s, au_r, ms_s, ms_r, rl_s, rl_r, lt_s, lt_r,
    c_s, c_r, af_s, af_r, an_s, an_r, b_s, b_r, far_s, far_r, near_s, near_r,
):
    at = Place()
    q = lax.axis_index("rel")
    me, c, node = at.me, at.c, at.node

    def g_copy(k):
        span = pl.ds(pl.multiple_of(k * STEP, STEP), STEP)
        return pltpu.make_async_copy(go_hbm.at[span], g.at[span], gsem.at[k])

    def f_copy(k):
        return pltpu.make_async_copy(pf_hbm.at[chunk(k)], feat.at[chunk(k)], fsem.at[k])

    def a_copy(k):
        return pltpu.make_async_copy(sa_hbm.at[chunk(k)], agg.at[chunk(k)], asem.at[k])

    def load_rest(k):
        a_copy(k).start()
        f_copy(k).start()

    w_copy = pltpu.make_async_copy(w_hbm, w, wsem)
    w_copy.start()
    loop(0, AHEAD, lambda k: g_copy(k).start())

    barrier = pltpu.get_barrier_semaphore()

    def greet(t):
        pl.semaphore_signal(barrier, inc=1, device_id={"nodes": at.peer(t)}, device_id_type=MESH)

    each(OTHERS, greet)
    for d in (1, REL - 1):
        pl.semaphore_signal(
            barrier, inc=1, device_id={"rel": lax.rem(q + d, REL)}, device_id_type=MESH
        )

    w_copy.wait()
    wt[...] = w[...].astype(F32).T.astype(BF16)

    def remote(src, dst, sems, i, to):
        return pltpu.make_async_remote_copy(
            src_ref=src, dst_ref=dst, send_sem=sems[0].at[i], recv_sem=sems[1].at[i],
            device_id={"nodes": to}, device_id_type=MESH,
        )

    def auth_copy(t):
        return pltpu.make_async_remote_copy(
            src_ref=authors.at[at.peer(t)], dst_ref=auth.at[t], send_sem=au_s, recv_sem=au_r,
            device_id={"nodes": at.peer(t)}, device_id_type=MESH,
        )

    def all_authors(sem):
        rows_of_all = auth.at[0:NODES - 1]
        pltpu.make_async_copy(rows_of_all, rows_of_all, sem).wait()

    def back_step(k):
        g_copy(k).wait()

        @pl.when(k + AHEAD < STEPS)
        def _():
            g_copy(k + AHEAD).start()

        lo = pl.multiple_of(k * STEP, STEP)
        back = jnp.dot(g[pl.ds(lo, STEP), :], wt[...], **DOTS)
        for h in range(2):
            table[pl.ds(2 * lo + h, STEP, stride=2), :] = back[:, h * HALF:h * HALF + HALF]

    loop(0, STEPS, back_step)
    loop(0, CHUNKS, load_rest)
    pl.semaphore_wait(barrier, NODES - 1 + 2)

    def relay_copy(t):
        i = RELAYED.index(t)
        return remote(send.at[block(t)], relay.at[block(i)], (rl_s, rl_r), i, node(*first_hop(t)))

    def msg_copy(t):
        if t in RELAYED:
            source, to = relay.at[block(RELAYED.index(t))], node(*second_hop(t))
        else:
            source, to = send.at[block(t)], at.peer(t)
        return remote(source, recv.at[block(t)], (ms_s, ms_r), t, to)

    def late_copy(h, i):
        return remote(
            late_send.at[h, block(i)], late_recv.at[h, block(i)],
            (lt_s, lt_r), h * LATE + i, at.peer(WHOLE + i),
        )

    def gather(b):
        for u in range(SLOTS):
            p = papers[b, u] * 2
            rows[2 * u:2 * u + 2, :] = table[pl.ds(p, 2), :]
        live = counts[b]
        scale = lax.rsqrt(jnp.full((1, HALF), live, jnp.int32).astype(F32))
        slot = lax.broadcasted_iota(jnp.int32, (SLOTS, HALF), 0)
        return [
            jnp.where(slot < live, rows[pl.ds(h, SLOTS, stride=2), :] * scale, 0.0).astype(BF16)
            for h in range(2)
        ]

    for k in range(WHOLE // 4):

        def whole_step(j):
            left, right = gather(at.peer_in(k, j))
            send[block(k * 4 + j), :HALF] = left
            send[block(k * 4 + j), HALF:] = right

        loop(0, 4, whole_step)
        for t in range(k * 4, k * 4 + 4):
            if t in RELAYED:
                relay_copy(t).start()
            elif t != HERE:
                msg_copy(t).start()
    for k in range(LATE // 4):

        def late_step(j):
            left, right = gather(at.peer_in(WHOLE // 4 + k, j))
            late_send[0, block(k * 4 + j), :] = left
            late_send[1, block(k * 4 + j), :] = right

        loop(0, 4, late_step)
    each(OTHERS, lambda t: auth_copy(t).start())
    auth[HERE] = authors[me]
    recv[block(HERE), :] = send[block(HERE), :]

    racc[...] = jnp.zeros_like(racc)
    sacc[...] = jnp.zeros_like(sacc)
    cols = pl.ds(pl.multiple_of(q * AUTH_W, AUTH_W), AUTH_W)
    over0 = (((0,), (0,)), ((), ()))

    def grads_step(k):
        a_copy(k).wait()
        f_copy(k).wait()
        racc[...] += lax.dot_general(agg[chunk(k), :], g[chunk(k), :], over0, **DOTS)
        sacc[...] += lax.dot_general(g[chunk(k), cols], feat[chunk(k), :], over0, **DOTS)

    def forward(t):
        relay_copy(t).wait_recv()
        msg_copy(t).start()

    loop(0, 2, grads_step)
    each(RELAYED, forward)
    for h in range(2):
        each(range(LATE), lambda i: late_copy(h, i).start())
    loop(2, CHUNKS, grads_step)

    sacc_t = sacc[...].T
    for n in range(NODES):
        co, y, z = n % CN, n // CN // SIDE, n // CN % SIDE
        ab = (y * SIDE + z, z * SIDE + y)[co]
        for k in range(8):
            wg[co, ab, 8 * k:8 * k + 8, :] = racc[8 * n:8 * n + 8, 128 * k:128 * k + 128]
        for i in range(3):
            for h in range(2):
                r0 = 64 + (2 * i + h) * 8
                wg[co, ab, r0:r0 + 8, :] = sacc_t[24 * n + 8 * i:24 * n + 8 * i + 8, 128 * h:128 * h + 128]

    core_copy = pltpu.make_async_remote_copy(
        src_ref=csend, dst_ref=crecv, send_sem=c_s, recv_sem=c_r,
        device_id={"nodes": node(0, 0, 1)}, device_id_type=MESH,
    )

    def core_round(i):
        csend[i] = wg[1 - c, i].astype(BF16)

    loop(0, SIDE * SIDE, core_round)
    core_copy.start()

    acc[...] = jnp.zeros_like(acc)
    all_authors(au_r)

    def add_rows(first_slot, msg, cols):
        targets = [auth[first_slot + u] for u in range(PER_SCAT)]

        def some(m):
            span = pl.ds(pl.multiple_of(m * SCAT_ROWS, SCAT_ROWS), SCAT_ROWS)
            ids = lax.broadcasted_iota(jnp.int32, (SCAT_ROWS, SLOTS), 0) + m * SCAT_ROWS
            onehot = jnp.concatenate(
                [jnp.where(ids == a, 1.0, 0.0).astype(BF16) for a in targets], axis=1
            )
            acc[span, cols] += jnp.dot(onehot, msg, **DOTS)

        loop(0, GROUP // SCAT_ROWS, some)

    def group(s):
        width = PER_SCAT * SLOTS
        return pl.ds(pl.multiple_of(s * width, width), width)

    def scatter(s):
        for u in range(PER_SCAT):
            if s * PER_SCAT + u != HERE:
                msg_copy(s * PER_SCAT + u).wait_recv()
        add_rows(s * PER_SCAT, recv[group(s), :], slice(None))

    def hot_rows(m):
        span = pl.ds(pl.multiple_of(m * 256, 256), 256)
        ids = lax.broadcasted_iota(jnp.int32, (256, SLOTS), 0) + m * 256
        for u in range(LATE):
            late_hot[span, u * SLOTS:u * SLOTS + SLOTS] = jnp.where(
                ids == auth[WHOLE + u], 1.0, 0.0
            ).astype(BF16)

    def pair(to, p):
        return to * SIDE + 2 * p

    def afar_copy(d):
        return remote(afar_send.at[d], afar_recv.at[d], (af_s, af_r), d, node(1 + 2 * d, 0, 0))

    def anear_copy(d, p):
        return remote(
            anear_send.at[d, p], anear_recv.at[d, p], (an_s, an_r), 2 * d + p, node(1 + 2 * d, 0, 0)
        )

    def b_copy(d):
        return remote(
            b_send.at[at.b_at[d]], b_recv.at[d - 1], (b_s, b_r), d - 1, node(0, d, 0)
        )

    def core_sum(i):
        wg[c, i] = wg[c, i] + crecv[i].astype(F32)

    def a_first():
        core_copy.wait_recv()
        loop(0, SIDE * SIDE, core_sum)
        for d in range(2):
            for i in range(2):
                afar_send[d, i] = wg[c, pair(at.a_at[2], d) + i].astype(BF16)
            afar_copy(d).start()
        for d in range(2):
            for i in range(2):
                anear_send[d, 1 - d, i] = wg[c, pair(at.a_at[1 + 2 * d], 1 - d) + i].astype(BF16)
            anear_copy(d, 1 - d).start()

    def a_second():
        for d in range(2):
            afar_copy(d).wait_recv()
            for i in range(2):
                total = wg[c, pair(at.a_at[1 + 2 * d], d) + i] + afar_recv[d, i].astype(F32)
                anear_send[d, d, i] = total.astype(BF16)
            anear_copy(d, d).start()

    def b_first():
        for p in range(2):
            for d in range(2):
                anear_copy(d, p).wait_recv()
            for i in range(2):
                total = (
                    wg[c, pair(at.a, p) + i]
                    + anear_recv[0, p, i].astype(F32) + anear_recv[1, p, i].astype(F32)
                )
                own_sum[2 * p + i] = total
                b_send[2 * p + i] = total.astype(BF16)
        for d in range(1, SIDE):
            b_copy(d).start()

    def b_last():
        for d in range(1, SIDE):
            b_copy(d).wait_recv()
        total = own_sum[at.b]
        for d in range(SIDE - 1):
            total = total + b_recv[d].astype(F32)
        for k in range(8):
            gr[:, 128 * k:128 * k + 128] = total[8 * k:8 * k + 8, :]
        for i in range(3):
            for h in range(2):
                r0 = 64 + (2 * i + h) * 8
                gs[8 * i:8 * i + 8, 128 * h:128 * h + 128] = total[r0:r0 + 8, :]

    def towards(d):
        return lax.rem(q + (1, REL - 1)[d] * at.sign, REL)

    def rows_of(owner, p):
        return pl.ds(pl.multiple_of(owner * OWN + p * PART, PART), PART)

    def far_copy(h, d):
        return pltpu.make_async_remote_copy(
            src_ref=far_send.at[h, d], dst_ref=far_recv.at[h, d],
            send_sem=far_s.at[h, d], recv_sem=far_r.at[h, d],
            device_id={"rel": towards(d)}, device_id_type=MESH,
        )

    def near_copy(h, d, p):
        return pltpu.make_async_remote_copy(
            src_ref=near_send.at[h, d, p], dst_ref=near_recv.at[h, d, p],
            send_sem=near_s.at[h, d, p], recv_sem=near_r.at[h, d, p],
            device_id={"rel": towards(d)}, device_id_type=MESH,
        )

    def half(h):
        return slice(h * HALF, h * HALF + HALF)

    def late_rows(h, owner):
        span = pl.ds(pl.multiple_of(owner * OWN, OWN), OWN)
        acc[span, half(h)] += jnp.dot(late_hot[span, :], late_recv[h], **DOTS)

    def rel_first(h):
        each(range(LATE), lambda i: late_copy(h, i).wait_recv())
        across = lax.rem(q + 2, REL)
        late_rows(h, across)
        for d in range(2):
            far_send[h, d] = acc[rows_of(across, d), half(h)].astype(BF16)
            far_copy(h, d).start()
        for d in range(2):
            late_rows(h, towards(d))
            near_send[h, d, 1 - d] = acc[rows_of(towards(d), 1 - d), half(h)].astype(BF16)
            near_copy(h, d, 1 - d).start()
        late_rows(h, q)

    def rel_second(h):
        for d in range(2):
            far_copy(h, d).wait_recv()
            mine = acc[rows_of(towards(d), d), half(h)]
            near_send[h, d, d] = (mine + far_recv[h, d].astype(F32)).astype(BF16)
            near_copy(h, d, d).start()

    def rel_last(h):
        for p in range(2):
            for d in range(2):
                near_copy(h, d, p).wait_recv()
            ga[p * PART:p * PART + PART, half(h)] = (
                acc[rows_of(q, p), half(h)]
                + near_recv[h, 0, p].astype(F32) + near_recv[h, 1, p].astype(F32)
            )

    loop(0, GROUP // 256, hot_rows)
    scatter(3)
    scatter(4)
    for i in range(3):
        scatter(i)
    rel_first(0)
    rel_second(0)
    a_first()
    rel_first(1)
    a_second()
    rel_last(0)
    rel_second(1)
    b_first()
    all_authors(au_s)
    each(RELAYED, lambda t: relay_copy(t).wait_send())
    each(RELAYED + DIRECT, lambda t: msg_copy(t).wait_send())
    for h in range(2):
        each(range(LATE), lambda i: late_copy(h, i).wait_send())
    core_copy.wait_send()
    b_last()
    rel_last(1)

    for h in range(2):
        for d in range(2):
            far_copy(h, d).wait_send()
            for p in range(2):
                near_copy(h, d, p).wait_send()
    for d in range(2):
        afar_copy(d).wait_send()
        for p in range(2):
            anear_copy(d, p).wait_send()
    for d in range(1, SIDE):
        b_copy(d).wait_send()


def hand_over(a, b, c, ao, bo, co):
    ao[...] = a[...]
    bo[...] = b[...]
    co[...] = c[...]


def on_device(grad_out, paper_feat, saved_agg, rel_weight, slot_paper, slot_author, block_count):
    vmem = pl.BlockSpec(memory_space=pltpu.VMEM)
    smem = pl.BlockSpec(memory_space=pltpu.SMEM)
    hbm = pl.BlockSpec(memory_space=pl.ANY)
    dma = pltpu.SemaphoreType.DMA
    limit = 56 * 1024 * 1024
    whole = (WHOLE * SLOTS, AUTH_W)
    late = (2, LATE * SLOTS, HALF)
    ga, gr, gs = pl.pallas_call(
        kernel,
        out_shape=(
            jax.ShapeDtypeStruct((OWN, AUTH_W), F32),
            jax.ShapeDtypeStruct((8, OUT_W), F32),
            jax.ShapeDtypeStruct((24, AUTH_W), F32),
        ),
        in_specs=[smem, smem, vmem, hbm, hbm, hbm, hbm],
        out_specs=(vmem, vmem, vmem),
        scratch_shapes=[
            pltpu.VMEM((AUTH_W, OUT_W), BF16),
            pltpu.VMEM((OUT_W, AUTH_W), BF16),
            pltpu.VMEM((PAPERS, OUT_W), BF16),
            pltpu.VMEM((PAPERS, PAPER_W), BF16),
            pltpu.VMEM((PAPERS, AUTH_W), BF16),
            pltpu.VMEM((2 * PAPERS, HALF), F32),
            pltpu.VMEM((2 * SLOTS, HALF), F32),
            pltpu.VMEM(whole, BF16),
            pltpu.VMEM((len(RELAYED) * SLOTS, AUTH_W), BF16),
            pltpu.VMEM(whole, BF16),
            pltpu.VMEM(late, BF16),
            pltpu.VMEM(late, BF16),
            pltpu.VMEM((GROUP, LATE * SLOTS), BF16),
            pltpu.VMEM((NODES, 1, SLOTS), jnp.int32),
            pltpu.VMEM((GROUP, AUTH_W), F32),
            pltpu.VMEM((AUTH_W, OUT_W), F32),
            pltpu.VMEM((AUTH_W, PAPER_W), F32),
            pltpu.VMEM((CN, SIDE * SIDE, PIECE, 128), F32),
            pltpu.VMEM((SIDE * SIDE, PIECE, 128), BF16),
            pltpu.VMEM((SIDE * SIDE, PIECE, 128), BF16),
            pltpu.VMEM((2, 2, PIECE, 128), BF16),
            pltpu.VMEM((2, 2, PIECE, 128), BF16),
            pltpu.VMEM((2, 2, 2, PIECE, 128), BF16),
            pltpu.VMEM((2, 2, 2, PIECE, 128), BF16),
            pltpu.VMEM((SIDE, PIECE, 128), F32),
            pltpu.VMEM((SIDE, PIECE, 128), BF16),
            pltpu.VMEM((SIDE - 1, PIECE, 128), BF16),
            pltpu.VMEM((2, 2, PART, HALF), BF16),
            pltpu.VMEM((2, 2, PART, HALF), BF16),
            pltpu.VMEM((2, 2, 2, PART, HALF), BF16),
            pltpu.VMEM((2, 2, 2, PART, HALF), BF16),
            dma, dma((STEPS,)), dma((CHUNKS,)), dma((CHUNKS,)),
            dma, dma, dma((WHOLE,)), dma((WHOLE,)),
            dma((len(RELAYED),)), dma((len(RELAYED),)), dma((2 * LATE,)), dma((2 * LATE,)),
            dma, dma, dma((2,)), dma((2,)), dma((4,)), dma((4,)), dma((3,)), dma((3,)),
            dma((2, 2)), dma((2, 2)), dma((2, 2, 2)), dma((2, 2, 2)),
        ],
        compiler_params=pltpu.CompilerParams(
            collective_id=0, has_side_effects=True, vmem_limit_bytes=limit
        ),
    )(
        slot_paper[0, 0], block_count[0, 0],
        slot_author[0, 0][:, None, :], rel_weight[0], grad_out, paper_feat, saved_agg[0],
    )
    ga, gr, gs = pl.pallas_call(
        hand_over,
        out_shape=tuple(jax.ShapeDtypeStruct(v.shape, F32) for v in (ga, gr, gs)),
        in_specs=[vmem] * 3,
        out_specs=(vmem,) * 3,
    )(ga, gr, gs)
    return ga, gr[None], gs


def solution(mesh):
    return jax.shard_map(
        on_device,
        mesh=mesh,
        in_specs=(
            P("nodes", None),
            P("nodes", None),
            P("rel", "nodes", None),
            P("rel", None, None),
            P("nodes", "rel", None, None),
            P("nodes", "rel", None, None),
            P("nodes", "rel", None),
        ),
        out_specs=(P(("nodes", "rel"), None), P("rel", "nodes", None), P("nodes", "rel")),
        check_vma=False,
    )
```

```python
import jax
import jax.numpy as jnp
from jax import lax
from jax.experimental import pallas as pl
from jax.experimental.pallas import tpu as pltpu
from jax.sharding import PartitionSpec as P

MESH = pl.DeviceIdType.MESH
F32 = jnp.float32
BF16 = jnp.bfloat16
DOTS = dict(preferred_element_type=F32)

NODES, REL = 32, 4
SIDE, CN = 4, 2
PAPERS, OUT_W, AUTH_W, PAPER_W = 4608, 1024, 256, 768
SLOTS, GROUP, OWN = 128, 2048, 512
CHUNK = 768
CHUNKS = PAPERS // CHUNK
STEP = 768
STEPS = PAPERS // STEP
AHEAD = 3
PIECE = 112
PER_SCAT = 4
SCAT_ROWS = 1024
WHOLE = 20
LATE = NODES - WHOLE
HALF = AUTH_W // 2
PART = OWN // 2


def chunk(k):
    return pl.ds(pl.multiple_of(k * CHUNK, CHUNK), CHUNK)


def block(t):
    if isinstance(t, int):
        return pl.ds(t * SLOTS, SLOTS)
    return pl.ds(pl.multiple_of(t * SLOTS, SLOTS), SLOTS)


ROW, COLUMN = 0, 1
GROUPS = [(ROW, 2, 0), (COLUMN, 2), (ROW, 2, 1), (ROW, 0, 0), (ROW, 0, 1), (COLUMN, 0), (COLUMN, 1), (COLUMN, 3)]


def in_group(group, j):
    if group[0] == ROW:
        return group[1], j, group[2]
    return 1 + 2 * (j // 2), group[1], j % 2


SLOT_OFFSETS = [in_group(group, j) for group in GROUPS for j in range(4)]
HERE = SLOT_OFFSETS.index((0, 0, 0))
OTHERS = [t for t in range(NODES) if t != HERE]
RELAYED = [t for t in OTHERS if 2 in SLOT_OFFSETS[t][:2]]
DIRECT = [t for t in OTHERS if t < WHOLE and t not in RELAYED]


def first_hop(t):
    da, db, dc = SLOT_OFFSETS[t]
    ha = (1 if db < 2 else 3) if da == 2 else 0
    hb = (1 if da in (1, 2) else 3) if db == 2 else 0
    return ha, hb, 0


def second_hop(t):
    da, db, dc = SLOT_OFFSETS[t]
    ha, hb, _ = first_hop(t)
    return (da - ha) % SIDE, (db - hb) % SIDE, dc


class Place:
    def __init__(self):
        me = lax.axis_index("nodes")
        y = lax.div(me, SIDE * CN)
        z = lax.rem(lax.div(me, CN), SIDE)
        c = lax.rem(me, CN)
        self.me, self.c = me, c
        self.a, self.b = y + c * (z - y), z + c * (y - z)
        self.stride_a = SIDE * CN - (SIDE * CN - CN) * c
        self.stride_b = CN + (SIDE * CN - CN) * c
        self.sign = 1 + 2 * c
        self.a_at = [lax.rem(self.a + self.sign * k, SIDE) for k in range(SIDE)]
        self.b_at = [lax.rem(self.b + self.sign * k, SIDE) for k in range(SIDE)]
        self.a_nodes = [v * self.stride_a for v in self.a_at]
        self.b_nodes = [v * self.stride_b for v in self.b_at]
        self.cs = [c, 1 - c]

    def node(self, da, db, dc):
        return self.a_nodes[da] + self.b_nodes[db] + self.cs[dc]

    def peer(self, t):
        return self.node(*SLOT_OFFSETS[t])

    def peer_in(self, k, j):
        group = GROUPS[k]
        if group[0] == ROW:
            b = lax.rem(self.b + self.sign * j, SIDE)
            return self.a_nodes[group[1]] + b * self.stride_b + self.cs[group[2]]
        a = lax.rem(self.a + self.sign * (1 + 2 * lax.div(j, 2)), SIDE)
        return a * self.stride_a + self.b_nodes[group[1]] + lax.rem(self.c + lax.rem(j, 2), CN)


def each(slots, body):
    for t in slots:
        body(t)


def loop(lo, hi, body):
    def step(t, _):
        body(t)
        return 0

    lax.fori_loop(lo, hi, step, 0)


def kernel(
    papers, counts, authors, w_hbm, go_hbm, pf_hbm, sa_hbm,
    ga, gr, gs,
    w, wt, g, feat, agg, table, rows, send, relay, recv, late_send, late_recv, late_hot, auth, acc,
    racc, sacc, wg, csend, crecv, afar_send, afar_recv, anear_send, anear_recv, own_sum, b_send, b_recv,
    far_send, far_recv, near_send, near_recv,
    wsem, gsem, fsem, asem, au_s, au_r, ms_s, ms_r, rl_s, rl_r, lt_s, lt_r,
    c_s, c_r, af_s, af_r, an_s, an_r, b_s, b_r, far_s, far_r, near_s, near_r,
):
    at = Place()
    q = lax.axis_index("rel")
    me, c, node = at.me, at.c, at.node

    def g_copy(k):
        span = pl.ds(pl.multiple_of(k * STEP, STEP), STEP)
        return pltpu.make_async_copy(go_hbm.at[span], g.at[span], gsem.at[k])

    def f_copy(k):
        return pltpu.make_async_copy(pf_hbm.at[chunk(k)], feat.at[chunk(k)], fsem.at[k])

    def a_copy(k):
        return pltpu.make_async_copy(sa_hbm.at[chunk(k)], agg.at[chunk(k)], asem.at[k])

    def load_rest(k):
        a_copy(k).start()
        f_copy(k).start()

    w_copy = pltpu.make_async_copy(w_hbm, w, wsem)
    w_copy.start()
    loop(0, AHEAD, lambda k: g_copy(k).start())

    barrier = pltpu.get_barrier_semaphore()

    def greet(t):
        pl.semaphore_signal(barrier, inc=1, device_id={"nodes": at.peer(t)}, device_id_type=MESH)

    each(OTHERS, greet)
    for d in (1, REL - 1):
        pl.semaphore_signal(
            barrier, inc=1, device_id={"rel": lax.rem(q + d, REL)}, device_id_type=MESH
        )

    w_copy.wait()
    wt[...] = w[...].astype(F32).T.astype(BF16)

    def remote(src, dst, sems, i, to):
        return pltpu.make_async_remote_copy(
            src_ref=src, dst_ref=dst, send_sem=sems[0].at[i], recv_sem=sems[1].at[i],
            device_id={"nodes": to}, device_id_type=MESH,
        )

    def auth_copy(t):
        return pltpu.make_async_remote_copy(
            src_ref=authors.at[at.peer(t)], dst_ref=auth.at[t], send_sem=au_s, recv_sem=au_r,
            device_id={"nodes": at.peer(t)}, device_id_type=MESH,
        )

    def all_authors(sem):
        rows_of_all = auth.at[0:NODES - 1]
        pltpu.make_async_copy(rows_of_all, rows_of_all, sem).wait()

    def back_step(k):
        g_copy(k).wait()

        @pl.when(k + AHEAD < STEPS)
        def _():
            g_copy(k + AHEAD).start()

        lo = pl.multiple_of(k * STEP, STEP)
        back = jnp.dot(g[pl.ds(lo, STEP), :], wt[...], **DOTS)
        for h in range(2):
            table[pl.ds(2 * lo + h, STEP, stride=2), :] = back[:, h * HALF:h * HALF + HALF]

    loop(0, STEPS, back_step)
    loop(0, CHUNKS, load_rest)
    pl.semaphore_wait(barrier, NODES - 1 + 2)

    def relay_copy(t):
        i = RELAYED.index(t)
        return remote(send.at[block(t)], relay.at[block(i)], (rl_s, rl_r), i, node(*first_hop(t)))

    def msg_copy(t):
        if t in RELAYED:
            source, to = relay.at[block(RELAYED.index(t))], node(*second_hop(t))
        else:
            source, to = send.at[block(t)], at.peer(t)
        return remote(source, recv.at[block(t)], (ms_s, ms_r), t, to)

    def late_copy(h, i):
        return remote(
            late_send.at[h, block(i)], late_recv.at[h, block(i)],
            (lt_s, lt_r), h * LATE + i, at.peer(WHOLE + i),
        )

    def gather(b):
        for u in range(SLOTS):
            p = papers[b, u] * 2
            rows[2 * u:2 * u + 2, :] = table[pl.ds(p, 2), :]
        live = counts[b]
        scale = lax.rsqrt(jnp.full((1, HALF), live, jnp.int32).astype(F32))
        slot = lax.broadcasted_iota(jnp.int32, (SLOTS, HALF), 0)
        return [
            jnp.where(slot < live, rows[pl.ds(h, SLOTS, stride=2), :] * scale, 0.0).astype(BF16)
            for h in range(2)
        ]

    for k in range(WHOLE // 4):

        def whole_step(j):
            left, right = gather(at.peer_in(k, j))
            send[block(k * 4 + j), :HALF] = left
            send[block(k * 4 + j), HALF:] = right

        loop(0, 4, whole_step)
        for t in range(k * 4, k * 4 + 4):
            if t in RELAYED:
                relay_copy(t).start()
            elif t != HERE:
                msg_copy(t).start()
    for k in range(LATE // 4):

        def late_step(j):
            left, right = gather(at.peer_in(WHOLE // 4 + k, j))
            late_send[0, block(k * 4 + j), :] = left
            late_send[1, block(k * 4 + j), :] = right

        loop(0, 4, late_step)
    each(OTHERS, lambda t: auth_copy(t).start())
    auth[HERE] = authors[me]
    recv[block(HERE), :] = send[block(HERE), :]

    racc[...] = jnp.zeros_like(racc)
    sacc[...] = jnp.zeros_like(sacc)
    cols = pl.ds(pl.multiple_of(q * AUTH_W, AUTH_W), AUTH_W)
    over0 = (((0,), (0,)), ((), ()))

    def grads_step(k):
        a_copy(k).wait()
        f_copy(k).wait()
        racc[...] += lax.dot_general(agg[chunk(k), :], g[chunk(k), :], over0, **DOTS)
        sacc[...] += lax.dot_general(g[chunk(k), cols], feat[chunk(k), :], over0, **DOTS)

    def forward(t):
        relay_copy(t).wait_recv()
        msg_copy(t).start()

    each(range(LATE), lambda i: late_copy(0, i).start())
    each(RELAYED, forward)
    each(range(LATE), lambda i: late_copy(1, i).start())
    loop(0, CHUNKS, grads_step)

    sacc_t = sacc[...].T
    for n in range(NODES):
        co, y, z = n % CN, n // CN // SIDE, n // CN % SIDE
        ab = (y * SIDE + z, z * SIDE + y)[co]
        for k in range(8):
            wg[co, ab, 8 * k:8 * k + 8, :] = racc[8 * n:8 * n + 8, 128 * k:128 * k + 128]
        for i in range(3):
            for h in range(2):
                r0 = 64 + (2 * i + h) * 8
                wg[co, ab, r0:r0 + 8, :] = sacc_t[24 * n + 8 * i:24 * n + 8 * i + 8, 128 * h:128 * h + 128]

    core_copy = pltpu.make_async_remote_copy(
        src_ref=csend, dst_ref=crecv, send_sem=c_s, recv_sem=c_r,
        device_id={"nodes": node(0, 0, 1)}, device_id_type=MESH,
    )

    def core_round(i):
        csend[i] = wg[1 - c, i].astype(BF16)

    loop(0, SIDE * SIDE, core_round)
    core_copy.start()

    acc[...] = jnp.zeros_like(acc)
    all_authors(au_r)

    def add_rows(first_slot, msg, cols):
        targets = [auth[first_slot + u] for u in range(PER_SCAT)]

        def some(m):
            span = pl.ds(pl.multiple_of(m * SCAT_ROWS, SCAT_ROWS), SCAT_ROWS)
            ids = lax.broadcasted_iota(jnp.int32, (SCAT_ROWS, SLOTS), 0) + m * SCAT_ROWS
            onehot = jnp.concatenate(
                [jnp.where(ids == a, 1.0, 0.0).astype(BF16) for a in targets], axis=1
            )
            acc[span, cols] += jnp.dot(onehot, msg, **DOTS)

        loop(0, GROUP // SCAT_ROWS, some)

    def group(s):
        width = PER_SCAT * SLOTS
        return pl.ds(pl.multiple_of(s * width, width), width)

    def scatter(s):
        for u in range(PER_SCAT):
            if s * PER_SCAT + u != HERE:
                msg_copy(s * PER_SCAT + u).wait_recv()
        add_rows(s * PER_SCAT, recv[group(s), :], slice(None))

    def hot_rows(m):
        span = pl.ds(pl.multiple_of(m * 256, 256), 256)
        ids = lax.broadcasted_iota(jnp.int32, (256, SLOTS), 0) + m * 256
        for u in range(LATE):
            late_hot[span, u * SLOTS:u * SLOTS + SLOTS] = jnp.where(
                ids == auth[WHOLE + u], 1.0, 0.0
            ).astype(BF16)

    def pair(to, p):
        return to * SIDE + 2 * p

    def afar_copy(d):
        return remote(afar_send.at[d], afar_recv.at[d], (af_s, af_r), d, node(1 + 2 * d, 0, 0))

    def anear_copy(d, p):
        return remote(
            anear_send.at[d, p], anear_recv.at[d, p], (an_s, an_r), 2 * d + p, node(1 + 2 * d, 0, 0)
        )

    def b_copy(d):
        return remote(
            b_send.at[at.b_at[d]], b_recv.at[d - 1], (b_s, b_r), d - 1, node(0, d, 0)
        )

    def core_sum(i):
        wg[c, i] = wg[c, i] + crecv[i].astype(F32)

    def a_first():
        core_copy.wait_recv()
        loop(0, SIDE * SIDE, core_sum)
        for d in range(2):
            for i in range(2):
                afar_send[d, i] = wg[c, pair(at.a_at[2], d) + i].astype(BF16)
            afar_copy(d).start()
        for d in range(2):
            for i in range(2):
                anear_send[d, 1 - d, i] = wg[c, pair(at.a_at[1 + 2 * d], 1 - d) + i].astype(BF16)
            anear_copy(d, 1 - d).start()

    def a_second():
        for d in range(2):
            afar_copy(d).wait_recv()
            for i in range(2):
                total = wg[c, pair(at.a_at[1 + 2 * d], d) + i] + afar_recv[d, i].astype(F32)
                anear_send[d, d, i] = total.astype(BF16)
            anear_copy(d, d).start()

    def b_first():
        for p in range(2):
            for d in range(2):
                anear_copy(d, p).wait_recv()
            for i in range(2):
                total = (
                    wg[c, pair(at.a, p) + i]
                    + anear_recv[0, p, i].astype(F32) + anear_recv[1, p, i].astype(F32)
                )
                own_sum[2 * p + i] = total
                b_send[2 * p + i] = total.astype(BF16)
        for d in range(1, SIDE):
            b_copy(d).start()

    def b_last():
        for d in range(1, SIDE):
            b_copy(d).wait_recv()
        total = own_sum[at.b]
        for d in range(SIDE - 1):
            total = total + b_recv[d].astype(F32)
        for k in range(8):
            gr[:, 128 * k:128 * k + 128] = total[8 * k:8 * k + 8, :]
        for i in range(3):
            for h in range(2):
                r0 = 64 + (2 * i + h) * 8
                gs[8 * i:8 * i + 8, 128 * h:128 * h + 128] = total[r0:r0 + 8, :]

    def towards(d):
        return lax.rem(q + (1, REL - 1)[d] * at.sign, REL)

    def rows_of(owner, p):
        return pl.ds(pl.multiple_of(owner * OWN + p * PART, PART), PART)

    def far_copy(h, d):
        return pltpu.make_async_remote_copy(
            src_ref=far_send.at[h, d], dst_ref=far_recv.at[h, d],
            send_sem=far_s.at[h, d], recv_sem=far_r.at[h, d],
            device_id={"rel": towards(d)}, device_id_type=MESH,
        )

    def near_copy(h, d, p):
        return pltpu.make_async_remote_copy(
            src_ref=near_send.at[h, d, p], dst_ref=near_recv.at[h, d, p],
            send_sem=near_s.at[h, d, p], recv_sem=near_r.at[h, d, p],
            device_id={"rel": towards(d)}, device_id_type=MESH,
        )

    def half(h):
        return slice(h * HALF, h * HALF + HALF)

    def late_rows(h, owner):
        span = pl.ds(pl.multiple_of(owner * OWN, OWN), OWN)
        acc[span, half(h)] += jnp.dot(late_hot[span, :], late_recv[h], **DOTS)

    def rel_first(h):
        each(range(LATE), lambda i: late_copy(h, i).wait_recv())
        across = lax.rem(q + 2, REL)
        late_rows(h, across)
        for d in range(2):
            far_send[h, d] = acc[rows_of(across, d), half(h)].astype(BF16)
            far_copy(h, d).start()
        for d in range(2):
            late_rows(h, towards(d))
            near_send[h, d, 1 - d] = acc[rows_of(towards(d), 1 - d), half(h)].astype(BF16)
            near_copy(h, d, 1 - d).start()
        late_rows(h, q)

    def rel_second(h):
        for d in range(2):
            far_copy(h, d).wait_recv()
            mine = acc[rows_of(towards(d), d), half(h)]
            near_send[h, d, d] = (mine + far_recv[h, d].astype(F32)).astype(BF16)
            near_copy(h, d, d).start()

    def rel_last(h):
        for p in range(2):
            for d in range(2):
                near_copy(h, d, p).wait_recv()
            ga[p * PART:p * PART + PART, half(h)] = (
                acc[rows_of(q, p), half(h)]
                + near_recv[h, 0, p].astype(F32) + near_recv[h, 1, p].astype(F32)
            )

    loop(0, GROUP // 256, hot_rows)
    scatter(3)
    scatter(4)
    for i in range(3):
        scatter(i)
    rel_first(0)
    rel_second(0)
    a_first()
    rel_first(1)
    a_second()
    rel_last(0)
    rel_second(1)
    b_first()
    all_authors(au_s)
    each(RELAYED, lambda t: relay_copy(t).wait_send())
    each(RELAYED + DIRECT, lambda t: msg_copy(t).wait_send())
    for h in range(2):
        each(range(LATE), lambda i: late_copy(h, i).wait_send())
    core_copy.wait_send()
    b_last()
    rel_last(1)

    for h in range(2):
        for d in range(2):
            far_copy(h, d).wait_send()
            for p in range(2):
                near_copy(h, d, p).wait_send()
    for d in range(2):
        afar_copy(d).wait_send()
        for p in range(2):
            anear_copy(d, p).wait_send()
    for d in range(1, SIDE):
        b_copy(d).wait_send()


def hand_over(a, b, c, ao, bo, co):
    ao[...] = a[...]
    bo[...] = b[...]
    co[...] = c[...]


def on_device(grad_out, paper_feat, saved_agg, rel_weight, slot_paper, slot_author, block_count):
    vmem = pl.BlockSpec(memory_space=pltpu.VMEM)
    smem = pl.BlockSpec(memory_space=pltpu.SMEM)
    hbm = pl.BlockSpec(memory_space=pl.ANY)
    dma = pltpu.SemaphoreType.DMA
    limit = 56 * 1024 * 1024
    whole = (WHOLE * SLOTS, AUTH_W)
    late = (2, LATE * SLOTS, HALF)
    ga, gr, gs = pl.pallas_call(
        kernel,
        out_shape=(
            jax.ShapeDtypeStruct((OWN, AUTH_W), F32),
            jax.ShapeDtypeStruct((8, OUT_W), F32),
            jax.ShapeDtypeStruct((24, AUTH_W), F32),
        ),
        in_specs=[smem, smem, vmem, hbm, hbm, hbm, hbm],
        out_specs=(vmem, vmem, vmem),
        scratch_shapes=[
            pltpu.VMEM((AUTH_W, OUT_W), BF16),
            pltpu.VMEM((OUT_W, AUTH_W), BF16),
            pltpu.VMEM((PAPERS, OUT_W), BF16),
            pltpu.VMEM((PAPERS, PAPER_W), BF16),
            pltpu.VMEM((PAPERS, AUTH_W), BF16),
            pltpu.VMEM((2 * PAPERS, HALF), F32),
            pltpu.VMEM((2 * SLOTS, HALF), F32),
            pltpu.VMEM(whole, BF16),
            pltpu.VMEM((len(RELAYED) * SLOTS, AUTH_W), BF16),
            pltpu.VMEM(whole, BF16),
            pltpu.VMEM(late, BF16),
            pltpu.VMEM(late, BF16),
            pltpu.VMEM((GROUP, LATE * SLOTS), BF16),
            pltpu.VMEM((NODES, 1, SLOTS), jnp.int32),
            pltpu.VMEM((GROUP, AUTH_W), F32),
            pltpu.VMEM((AUTH_W, OUT_W), F32),
            pltpu.VMEM((AUTH_W, PAPER_W), F32),
            pltpu.VMEM((CN, SIDE * SIDE, PIECE, 128), F32),
            pltpu.VMEM((SIDE * SIDE, PIECE, 128), BF16),
            pltpu.VMEM((SIDE * SIDE, PIECE, 128), BF16),
            pltpu.VMEM((2, 2, PIECE, 128), BF16),
            pltpu.VMEM((2, 2, PIECE, 128), BF16),
            pltpu.VMEM((2, 2, 2, PIECE, 128), BF16),
            pltpu.VMEM((2, 2, 2, PIECE, 128), BF16),
            pltpu.VMEM((SIDE, PIECE, 128), F32),
            pltpu.VMEM((SIDE, PIECE, 128), BF16),
            pltpu.VMEM((SIDE - 1, PIECE, 128), BF16),
            pltpu.VMEM((2, 2, PART, HALF), BF16),
            pltpu.VMEM((2, 2, PART, HALF), BF16),
            pltpu.VMEM((2, 2, 2, PART, HALF), BF16),
            pltpu.VMEM((2, 2, 2, PART, HALF), BF16),
            dma, dma((STEPS,)), dma((CHUNKS,)), dma((CHUNKS,)),
            dma, dma, dma((WHOLE,)), dma((WHOLE,)),
            dma((len(RELAYED),)), dma((len(RELAYED),)), dma((2 * LATE,)), dma((2 * LATE,)),
            dma, dma, dma((2,)), dma((2,)), dma((4,)), dma((4,)), dma((3,)), dma((3,)),
            dma((2, 2)), dma((2, 2)), dma((2, 2, 2)), dma((2, 2, 2)),
        ],
        compiler_params=pltpu.CompilerParams(
            collective_id=0, has_side_effects=True, vmem_limit_bytes=limit
        ),
    )(
        slot_paper[0, 0], block_count[0, 0],
        slot_author[0, 0][:, None, :], rel_weight[0], grad_out, paper_feat, saved_agg[0],
    )
    ga, gr, gs = pl.pallas_call(
        hand_over,
        out_shape=tuple(jax.ShapeDtypeStruct(v.shape, F32) for v in (ga, gr, gs)),
        in_specs=[vmem] * 3,
        out_specs=(vmem,) * 3,
    )(ga, gr, gs)
    return ga, gr[None], gs


def solution(mesh):
    return jax.shard_map(
        on_device,
        mesh=mesh,
        in_specs=(
            P("nodes", None),
            P("nodes", None),
            P("rel", "nodes", None),
            P("rel", None, None),
            P("nodes", "rel", None, None),
            P("nodes", "rel", None, None),
            P("nodes", "rel", None),
        ),
        out_specs=(P(("nodes", "rel"), None), P("rel", "nodes", None), P("nodes", "rel")),
        check_vma=False,
    )
```

```python
import jax
import jax.numpy as jnp
from jax import lax
from jax.experimental import pallas as pl
from jax.experimental.pallas import tpu as pltpu
from jax.sharding import PartitionSpec as P

MESH = pl.DeviceIdType.MESH
F32 = jnp.float32
BF16 = jnp.bfloat16
DOTS = dict(preferred_element_type=F32)

NODES, REL = 32, 4
SIDE, CN = 4, 2
PAPERS, OUT_W, AUTH_W, PAPER_W = 4608, 1024, 256, 768
SLOTS, GROUP, OWN = 128, 2048, 512
CHUNK = 768
CHUNKS = PAPERS // CHUNK
STEP = 384
STEPS = PAPERS // STEP
AHEAD = 5
PIECE = 112
PER_SCAT = 4
SCAT_ROWS = 1024
WHOLE = 20
LATE = NODES - WHOLE
HALF = AUTH_W // 2
PART = OWN // 2


def chunk(k):
    return pl.ds(pl.multiple_of(k * CHUNK, CHUNK), CHUNK)


def block(t):
    if isinstance(t, int):
        return pl.ds(t * SLOTS, SLOTS)
    return pl.ds(pl.multiple_of(t * SLOTS, SLOTS), SLOTS)


ROW, COLUMN = 0, 1
GROUPS = [(ROW, 2, 0), (COLUMN, 2), (ROW, 2, 1), (ROW, 0, 0), (ROW, 0, 1), (COLUMN, 0), (COLUMN, 1), (COLUMN, 3)]


def in_group(group, j):
    if group[0] == ROW:
        return group[1], j, group[2]
    return 1 + 2 * (j // 2), group[1], j % 2


SLOT_OFFSETS = [in_group(group, j) for group in GROUPS for j in range(4)]
HERE = SLOT_OFFSETS.index((0, 0, 0))
OTHERS = [t for t in range(NODES) if t != HERE]
RELAYED = [t for t in OTHERS if 2 in SLOT_OFFSETS[t][:2]]
DIRECT = [t for t in OTHERS if t < WHOLE and t not in RELAYED]


def first_hop(t):
    da, db, dc = SLOT_OFFSETS[t]
    ha = (1 if db < 2 else 3) if da == 2 else 0
    hb = (1 if da in (1, 2) else 3) if db == 2 else 0
    return ha, hb, 0


def second_hop(t):
    da, db, dc = SLOT_OFFSETS[t]
    ha, hb, _ = first_hop(t)
    return (da - ha) % SIDE, (db - hb) % SIDE, dc


class Place:
    def __init__(self):
        me = lax.axis_index("nodes")
        y = lax.div(me, SIDE * CN)
        z = lax.rem(lax.div(me, CN), SIDE)
        c = lax.rem(me, CN)
        self.me, self.c = me, c
        self.a, self.b = y + c * (z - y), z + c * (y - z)
        self.stride_a = SIDE * CN - (SIDE * CN - CN) * c
        self.stride_b = CN + (SIDE * CN - CN) * c
        self.sign = 1 + 2 * c
        self.a_at = [lax.rem(self.a + self.sign * k, SIDE) for k in range(SIDE)]
        self.b_at = [lax.rem(self.b + self.sign * k, SIDE) for k in range(SIDE)]
        self.a_nodes = [v * self.stride_a for v in self.a_at]
        self.b_nodes = [v * self.stride_b for v in self.b_at]
        self.cs = [c, 1 - c]

    def node(self, da, db, dc):
        return self.a_nodes[da] + self.b_nodes[db] + self.cs[dc]

    def peer(self, t):
        return self.node(*SLOT_OFFSETS[t])

    def peer_in(self, k, j):
        group = GROUPS[k]
        if group[0] == ROW:
            b = lax.rem(self.b + self.sign * j, SIDE)
            return self.a_nodes[group[1]] + b * self.stride_b + self.cs[group[2]]
        a = lax.rem(self.a + self.sign * (1 + 2 * lax.div(j, 2)), SIDE)
        return a * self.stride_a + self.b_nodes[group[1]] + lax.rem(self.c + lax.rem(j, 2), CN)


def each(slots, body):
    for t in slots:
        body(t)


def loop(lo, hi, body):
    def step(t, _):
        body(t)
        return 0

    lax.fori_loop(lo, hi, step, 0)


def kernel(
    papers, counts, authors, w_hbm, go_hbm, pf_hbm, sa_hbm,
    ga, gr, gs,
    w, wt, g, feat, agg, table, rows, send, relay, recv, late_send, late_recv, late_hot, auth, acc,
    racc, sacc, wg, csend, crecv, afar_send, afar_recv, anear_send, anear_recv, own_sum, b_send, b_recv,
    far_send, far_recv, near_send, near_recv,
    wsem, gsem, fsem, asem, au_s, au_r, ms_s, ms_r, rl_s, rl_r, lt_s, lt_r,
    c_s, c_r, af_s, af_r, an_s, an_r, b_s, b_r, far_s, far_r, near_s, near_r,
):
    at = Place()
    q = lax.axis_index("rel")
    me, c, node = at.me, at.c, at.node

    def g_copy(k):
        span = pl.ds(pl.multiple_of(k * STEP, STEP), STEP)
        return pltpu.make_async_copy(go_hbm.at[span], g.at[span], gsem.at[k])

    def f_copy(k):
        return pltpu.make_async_copy(pf_hbm.at[chunk(k)], feat.at[chunk(k)], fsem.at[k])

    def a_copy(k):
        return pltpu.make_async_copy(sa_hbm.at[chunk(k)], agg.at[chunk(k)], asem.at[k])

    def load_rest(k):
        a_copy(k).start()
        f_copy(k).start()

    w_copy = pltpu.make_async_copy(w_hbm, w, wsem)
    w_copy.start()
    loop(0, AHEAD, lambda k: g_copy(k).start())

    barrier = pltpu.get_barrier_semaphore()

    def greet(t):
        pl.semaphore_signal(barrier, inc=1, device_id={"nodes": at.peer(t)}, device_id_type=MESH)

    each(OTHERS, greet)
    for d in (1, REL - 1):
        pl.semaphore_signal(
            barrier, inc=1, device_id={"rel": lax.rem(q + d, REL)}, device_id_type=MESH
        )

    w_copy.wait()
    wt[...] = w[...].astype(F32).T.astype(BF16)

    def shared(src, dst, send_sem, recv_sem, to):
        return pltpu.make_async_remote_copy(
            src_ref=src, dst_ref=dst, send_sem=send_sem, recv_sem=recv_sem,
            device_id={"nodes": to}, device_id_type=MESH,
        )

    def remote(src, dst, sems, i, to):
        return shared(src, dst, sems[0].at[i], sems[1].at[i], to)

    def wait_bytes(ref, sem):
        pltpu.make_async_copy(ref, ref, sem).wait()

    def auth_copy(t):
        return shared(authors.at[at.peer(t)], auth.at[t], au_s, au_r, at.peer(t))

    def all_authors(sem):
        wait_bytes(auth.at[0:NODES - 1], sem)

    def back_step(k):
        g_copy(k).wait()

        @pl.when(k + AHEAD < STEPS)
        def _():
            g_copy(k + AHEAD).start()

        lo = pl.multiple_of(k * STEP, STEP)
        back = jnp.dot(g[pl.ds(lo, STEP), :], wt[...], **DOTS)
        for h in range(2):
            table[pl.ds(2 * lo + h, STEP, stride=2), :] = back[:, h * HALF:h * HALF + HALF]

    loop(0, STEPS, back_step)
    loop(0, CHUNKS, load_rest)
    pl.semaphore_wait(barrier, NODES - 1 + 2)

    def relay_copy(t):
        i = RELAYED.index(t)
        return shared(
            send.at[block(t)], relay.at[block(i)], rl_s, rl_r.at[i], node(*first_hop(t))
        )

    def msg_copy(t):
        if t in RELAYED:
            source, to = relay.at[block(RELAYED.index(t))], node(*second_hop(t))
        else:
            source, to = send.at[block(t)], at.peer(t)
        return shared(source, recv.at[block(t)], ms_s, ms_r.at[t], to)

    def late_copy(h, i):
        return shared(
            late_send.at[h, block(i)], late_recv.at[h, block(i)],
            lt_s.at[h], lt_r.at[h], at.peer(WHOLE + i),
        )

    def gather(b):
        for u in range(SLOTS):
            p = papers[b, u] * 2
            rows[2 * u:2 * u + 2, :] = table[pl.ds(p, 2), :]
        live = counts[b]
        scale = lax.rsqrt(jnp.full((1, HALF), live, jnp.int32).astype(F32))
        slot = lax.broadcasted_iota(jnp.int32, (SLOTS, HALF), 0)
        return [
            jnp.where(slot < live, rows[pl.ds(h, SLOTS, stride=2), :] * scale, 0.0).astype(BF16)
            for h in range(2)
        ]

    for k in range(WHOLE // 4):

        def whole_step(j):
            left, right = gather(at.peer_in(k, j))
            send[block(k * 4 + j), :HALF] = left
            send[block(k * 4 + j), HALF:] = right

        loop(0, 4, whole_step)
        for t in range(k * 4, k * 4 + 4):
            if t in RELAYED:
                relay_copy(t).start()
            elif t != HERE:
                msg_copy(t).start()
    for k in range(LATE // 4):

        def late_step(j):
            left, right = gather(at.peer_in(WHOLE // 4 + k, j))
            late_send[0, block(k * 4 + j), :] = left
            late_send[1, block(k * 4 + j), :] = right

        loop(0, 4, late_step)
    each(OTHERS, lambda t: auth_copy(t).start())
    auth[HERE] = authors[me]
    recv[block(HERE), :] = send[block(HERE), :]

    racc[...] = jnp.zeros_like(racc)
    sacc[...] = jnp.zeros_like(sacc)
    cols = pl.ds(pl.multiple_of(q * AUTH_W, AUTH_W), AUTH_W)
    over0 = (((0,), (0,)), ((), ()))

    def grads_step(k):
        a_copy(k).wait()
        f_copy(k).wait()
        racc[...] += lax.dot_general(agg[chunk(k), :], g[chunk(k), :], over0, **DOTS)
        sacc[...] += lax.dot_general(g[chunk(k), cols], feat[chunk(k), :], over0, **DOTS)

    def forward(t):
        relay_copy(t).wait_recv()
        msg_copy(t).start()

    loop(0, 3, grads_step)
    each(RELAYED, forward)
    for h in range(2):
        each(range(LATE), lambda i: late_copy(h, i).start())
    loop(3, CHUNKS, grads_step)

    sacc_t = sacc[...].T
    for n in range(NODES):
        co, y, z = n % CN, n // CN // SIDE, n // CN % SIDE
        ab = (y * SIDE + z, z * SIDE + y)[co]
        for k in range(8):
            wg[co, ab, 8 * k:8 * k + 8, :] = racc[8 * n:8 * n + 8, 128 * k:128 * k + 128]
        for i in range(3):
            for h in range(2):
                r0 = 64 + (2 * i + h) * 8
                wg[co, ab, r0:r0 + 8, :] = sacc_t[24 * n + 8 * i:24 * n + 8 * i + 8, 128 * h:128 * h + 128]

    core_copy = pltpu.make_async_remote_copy(
        src_ref=csend, dst_ref=crecv, send_sem=c_s, recv_sem=c_r,
        device_id={"nodes": node(0, 0, 1)}, device_id_type=MESH,
    )

    def core_round(i):
        csend[i] = wg[1 - c, i].astype(BF16)

    loop(0, SIDE * SIDE, core_round)
    core_copy.start()

    acc[...] = jnp.zeros_like(acc)
    all_authors(au_r)

    def add_rows(first_slot, msg, cols):
        targets = [auth[first_slot + u] for u in range(PER_SCAT)]

        def some(m):
            span = pl.ds(pl.multiple_of(m * SCAT_ROWS, SCAT_ROWS), SCAT_ROWS)
            ids = lax.broadcasted_iota(jnp.int32, (SCAT_ROWS, SLOTS), 0) + m * SCAT_ROWS
            onehot = jnp.concatenate(
                [jnp.where(ids == a, 1.0, 0.0).astype(BF16) for a in targets], axis=1
            )
            acc[span, cols] += jnp.dot(onehot, msg, **DOTS)

        loop(0, GROUP // SCAT_ROWS, some)

    def group(s):
        width = PER_SCAT * SLOTS
        return pl.ds(pl.multiple_of(s * width, width), width)

    def scatter(s):
        for u in range(PER_SCAT):
            if s * PER_SCAT + u != HERE:
                msg_copy(s * PER_SCAT + u).wait_recv()
        add_rows(s * PER_SCAT, recv[group(s), :], slice(None))

    def hot_rows(m):
        span = pl.ds(pl.multiple_of(m * 256, 256), 256)
        ids = lax.broadcasted_iota(jnp.int32, (256, SLOTS), 0) + m * 256
        for u in range(LATE):
            late_hot[span, u * SLOTS:u * SLOTS + SLOTS] = jnp.where(
                ids == auth[WHOLE + u], 1.0, 0.0
            ).astype(BF16)

    def pair(to, p):
        return to * SIDE + 2 * p

    def afar_copy(d):
        return remote(afar_send.at[d], afar_recv.at[d], (af_s, af_r), d, node(1 + 2 * d, 0, 0))

    def anear_copy(d, p):
        return remote(
            anear_send.at[d, p], anear_recv.at[d, p], (an_s, an_r), 2 * d + p, node(1 + 2 * d, 0, 0)
        )

    def b_copy(d):
        return remote(
            b_send.at[at.b_at[d]], b_recv.at[d - 1], (b_s, b_r), d - 1, node(0, d, 0)
        )

    def core_sum(i):
        wg[c, i] = wg[c, i] + crecv[i].astype(F32)

    def a_first():
        core_copy.wait_recv()
        loop(0, SIDE * SIDE, core_sum)
        for d in range(2):
            for i in range(2):
                afar_send[d, i] = wg[c, pair(at.a_at[2], d) + i].astype(BF16)
            afar_copy(d).start()
        for d in range(2):
            for i in range(2):
                anear_send[d, 1 - d, i] = wg[c, pair(at.a_at[1 + 2 * d], 1 - d) + i].astype(BF16)
            anear_copy(d, 1 - d).start()

    def a_second():
        for d in range(2):
            afar_copy(d).wait_recv()
            for i in range(2):
                total = wg[c, pair(at.a_at[1 + 2 * d], d) + i] + afar_recv[d, i].astype(F32)
                anear_send[d, d, i] = total.astype(BF16)
            anear_copy(d, d).start()

    def b_first():
        for p in range(2):
            for d in range(2):
                anear_copy(d, p).wait_recv()
            for i in range(2):
                total = (
                    wg[c, pair(at.a, p) + i]
                    + anear_recv[0, p, i].astype(F32) + anear_recv[1, p, i].astype(F32)
                )
                own_sum[2 * p + i] = total
                b_send[2 * p + i] = total.astype(BF16)
        for d in range(1, SIDE):
            b_copy(d).start()

    def b_last():
        for d in range(1, SIDE):
            b_copy(d).wait_recv()
        total = own_sum[at.b]
        for d in range(SIDE - 1):
            total = total + b_recv[d].astype(F32)
        for k in range(8):
            gr[:, 128 * k:128 * k + 128] = total[8 * k:8 * k + 8, :]
        for i in range(3):
            for h in range(2):
                r0 = 64 + (2 * i + h) * 8
                gs[8 * i:8 * i + 8, 128 * h:128 * h + 128] = total[r0:r0 + 8, :]

    def towards(d):
        return lax.rem(q + (1, REL - 1)[d] * at.sign, REL)

    def rows_of(owner, p):
        return pl.ds(pl.multiple_of(owner * OWN + p * PART, PART), PART)

    def far_copy(h, d):
        return pltpu.make_async_remote_copy(
            src_ref=far_send.at[h, d], dst_ref=far_recv.at[h, d],
            send_sem=far_s.at[h, d], recv_sem=far_r.at[h, d],
            device_id={"rel": towards(d)}, device_id_type=MESH,
        )

    def near_copy(h, d, p):
        return pltpu.make_async_remote_copy(
            src_ref=near_send.at[h, d, p], dst_ref=near_recv.at[h, d, p],
            send_sem=near_s.at[h, d, p], recv_sem=near_r.at[h, d, p],
            device_id={"rel": towards(d)}, device_id_type=MESH,
        )

    def half(h):
        return slice(h * HALF, h * HALF + HALF)

    def late_rows(h, owner):
        span = pl.ds(pl.multiple_of(owner * OWN, OWN), OWN)
        acc[span, half(h)] += jnp.dot(late_hot[span, :], late_recv[h], **DOTS)

    def rel_first(h):
        wait_bytes(late_recv.at[h], lt_r.at[h])
        across = lax.rem(q + 2, REL)
        late_rows(h, across)
        for d in range(2):
            far_send[h, d] = acc[rows_of(across, d), half(h)].astype(BF16)
            far_copy(h, d).start()
        for d in range(2):
            late_rows(h, towards(d))
            near_send[h, d, 1 - d] = acc[rows_of(towards(d), 1 - d), half(h)].astype(BF16)
            near_copy(h, d, 1 - d).start()
        late_rows(h, q)

    def rel_second(h):
        for d in range(2):
            far_copy(h, d).wait_recv()
            mine = acc[rows_of(towards(d), d), half(h)]
            near_send[h, d, d] = (mine + far_recv[h, d].astype(F32)).astype(BF16)
            near_copy(h, d, d).start()

    def rel_last(h):
        for p in range(2):
            for d in range(2):
                near_copy(h, d, p).wait_recv()
            ga[p * PART:p * PART + PART, half(h)] = (
                acc[rows_of(q, p), half(h)]
                + near_recv[h, 0, p].astype(F32) + near_recv[h, 1, p].astype(F32)
            )

    loop(0, GROUP // 256, hot_rows)
    scatter(3)
    scatter(4)
    for i in range(3):
        scatter(i)
    rel_first(0)
    rel_second(0)
    a_first()
    rel_first(1)
    a_second()
    rel_last(0)
    rel_second(1)
    b_first()
    all_authors(au_s)
    wait_bytes(relay, rl_s)
    wait_bytes(recv.at[0:(WHOLE - 1) * SLOTS], ms_s)
    for h in range(2):
        wait_bytes(late_send.at[h], lt_s.at[h])
    core_copy.wait_send()
    b_last()
    rel_last(1)

    for h in range(2):
        for d in range(2):
            far_copy(h, d).wait_send()
            for p in range(2):
                near_copy(h, d, p).wait_send()
    for d in range(2):
        afar_copy(d).wait_send()
        for p in range(2):
            anear_copy(d, p).wait_send()
    for d in range(1, SIDE):
        b_copy(d).wait_send()


def hand_over(a, b, c, ao, bo, co):
    ao[...] = a[...]
    bo[...] = b[...]
    co[...] = c[...]


def on_device(grad_out, paper_feat, saved_agg, rel_weight, slot_paper, slot_author, block_count):
    vmem = pl.BlockSpec(memory_space=pltpu.VMEM)
    smem = pl.BlockSpec(memory_space=pltpu.SMEM)
    hbm = pl.BlockSpec(memory_space=pl.ANY)
    dma = pltpu.SemaphoreType.DMA
    limit = 56 * 1024 * 1024
    whole = (WHOLE * SLOTS, AUTH_W)
    late = (2, LATE * SLOTS, HALF)
    ga, gr, gs = pl.pallas_call(
        kernel,
        out_shape=(
            jax.ShapeDtypeStruct((OWN, AUTH_W), F32),
            jax.ShapeDtypeStruct((8, OUT_W), F32),
            jax.ShapeDtypeStruct((24, AUTH_W), F32),
        ),
        in_specs=[smem, smem, vmem, hbm, hbm, hbm, hbm],
        out_specs=(vmem, vmem, vmem),
        scratch_shapes=[
            pltpu.VMEM((AUTH_W, OUT_W), BF16),
            pltpu.VMEM((OUT_W, AUTH_W), BF16),
            pltpu.VMEM((PAPERS, OUT_W), BF16),
            pltpu.VMEM((PAPERS, PAPER_W), BF16),
            pltpu.VMEM((PAPERS, AUTH_W), BF16),
            pltpu.VMEM((2 * PAPERS, HALF), F32),
            pltpu.VMEM((2 * SLOTS, HALF), F32),
            pltpu.VMEM(whole, BF16),
            pltpu.VMEM((len(RELAYED) * SLOTS, AUTH_W), BF16),
            pltpu.VMEM(whole, BF16),
            pltpu.VMEM(late, BF16),
            pltpu.VMEM(late, BF16),
            pltpu.VMEM((GROUP, LATE * SLOTS), BF16),
            pltpu.VMEM((NODES, 1, SLOTS), jnp.int32),
            pltpu.VMEM((GROUP, AUTH_W), F32),
            pltpu.VMEM((AUTH_W, OUT_W), F32),
            pltpu.VMEM((AUTH_W, PAPER_W), F32),
            pltpu.VMEM((CN, SIDE * SIDE, PIECE, 128), F32),
            pltpu.VMEM((SIDE * SIDE, PIECE, 128), BF16),
            pltpu.VMEM((SIDE * SIDE, PIECE, 128), BF16),
            pltpu.VMEM((2, 2, PIECE, 128), BF16),
            pltpu.VMEM((2, 2, PIECE, 128), BF16),
            pltpu.VMEM((2, 2, 2, PIECE, 128), BF16),
            pltpu.VMEM((2, 2, 2, PIECE, 128), BF16),
            pltpu.VMEM((SIDE, PIECE, 128), F32),
            pltpu.VMEM((SIDE, PIECE, 128), BF16),
            pltpu.VMEM((SIDE - 1, PIECE, 128), BF16),
            pltpu.VMEM((2, 2, PART, HALF), BF16),
            pltpu.VMEM((2, 2, PART, HALF), BF16),
            pltpu.VMEM((2, 2, 2, PART, HALF), BF16),
            pltpu.VMEM((2, 2, 2, PART, HALF), BF16),
            dma, dma((STEPS,)), dma((CHUNKS,)), dma((CHUNKS,)),
            dma, dma, dma, dma((WHOLE,)),
            dma, dma((len(RELAYED),)), dma((2,)), dma((2,)),
            dma, dma, dma((2,)), dma((2,)), dma((4,)), dma((4,)), dma((3,)), dma((3,)),
            dma((2, 2)), dma((2, 2)), dma((2, 2, 2)), dma((2, 2, 2)),
        ],
        compiler_params=pltpu.CompilerParams(
            collective_id=0, has_side_effects=True, vmem_limit_bytes=limit
        ),
    )(
        slot_paper[0, 0], block_count[0, 0],
        slot_author[0, 0][:, None, :], rel_weight[0], grad_out, paper_feat, saved_agg[0],
    )
    ga, gr, gs = pl.pallas_call(
        hand_over,
        out_shape=tuple(jax.ShapeDtypeStruct(v.shape, F32) for v in (ga, gr, gs)),
        in_specs=[vmem] * 3,
        out_specs=(vmem,) * 3,
    )(ga, gr, gs)
    return ga, gr[None], gs


def solution(mesh):
    return jax.shard_map(
        on_device,
        mesh=mesh,
        in_specs=(
            P("nodes", None),
            P("nodes", None),
            P("rel", "nodes", None),
            P("rel", None, None),
            P("nodes", "rel", None, None),
            P("nodes", "rel", None, None),
            P("nodes", "rel", None),
        ),
        out_specs=(P(("nodes", "rel"), None), P("rel", "nodes", None), P("nodes", "rel")),
        check_vma=False,
    )
```

```python
import jax
import jax.numpy as jnp
from jax import lax
from jax.experimental import pallas as pl
from jax.experimental.pallas import tpu as pltpu
from jax.sharding import PartitionSpec as P

MESH = pl.DeviceIdType.MESH
F32 = jnp.float32
BF16 = jnp.bfloat16
DOTS = dict(preferred_element_type=F32)

NODES, REL = 32, 4
SIDE, CN = 4, 2
PAPERS, OUT_W, AUTH_W, PAPER_W = 4608, 1024, 256, 768
SLOTS, GROUP, OWN = 128, 2048, 512
CHUNK = 768
CHUNKS = PAPERS // CHUNK
STEP = 768
STEPS = PAPERS // STEP
AHEAD = 3
PIECE = 112
PER_SCAT = 4
SCAT_ROWS = 1024
WHOLE = 20
LATE = NODES - WHOLE
HALF = AUTH_W // 2
PART = OWN // 2


def chunk(k):
    return pl.ds(pl.multiple_of(k * CHUNK, CHUNK), CHUNK)


def block(t):
    if isinstance(t, int):
        return pl.ds(t * SLOTS, SLOTS)
    return pl.ds(pl.multiple_of(t * SLOTS, SLOTS), SLOTS)


ROW, COLUMN = 0, 1
GROUPS = [(ROW, 2, 0), (COLUMN, 2), (ROW, 2, 1), (ROW, 0, 0), (ROW, 0, 1), (COLUMN, 0), (COLUMN, 1), (COLUMN, 3)]


def in_group(group, j):
    if group[0] == ROW:
        return group[1], j, group[2]
    return 1 + 2 * (j // 2), group[1], j % 2


SLOT_OFFSETS = [in_group(group, j) for group in GROUPS for j in range(4)]
HERE = SLOT_OFFSETS.index((0, 0, 0))
OTHERS = [t for t in range(NODES) if t != HERE]
RELAYED = [t for t in OTHERS if 2 in SLOT_OFFSETS[t][:2]]
DIRECT = [t for t in OTHERS if t < WHOLE and t not in RELAYED]


def first_hop(t):
    da, db, dc = SLOT_OFFSETS[t]
    ha = (1 if db < 2 else 3) if da == 2 else 0
    hb = (1 if da in (1, 2) else 3) if db == 2 else 0
    return ha, hb, 0


def second_hop(t):
    da, db, dc = SLOT_OFFSETS[t]
    ha, hb, _ = first_hop(t)
    return (da - ha) % SIDE, (db - hb) % SIDE, dc


class Place:
    def __init__(self):
        me = lax.axis_index("nodes")
        y = lax.div(me, SIDE * CN)
        z = lax.rem(lax.div(me, CN), SIDE)
        c = lax.rem(me, CN)
        self.me, self.c = me, c
        self.a, self.b = y + c * (z - y), z + c * (y - z)
        self.stride_a = SIDE * CN - (SIDE * CN - CN) * c
        self.stride_b = CN + (SIDE * CN - CN) * c
        self.sign = 1 + 2 * c
        self.a_at = [lax.rem(self.a + self.sign * k, SIDE) for k in range(SIDE)]
        self.b_at = [lax.rem(self.b + self.sign * k, SIDE) for k in range(SIDE)]
        self.a_nodes = [v * self.stride_a for v in self.a_at]
        self.b_nodes = [v * self.stride_b for v in self.b_at]
        self.cs = [c, 1 - c]

    def node(self, da, db, dc):
        return self.a_nodes[da] + self.b_nodes[db] + self.cs[dc]

    def peer(self, t):
        return self.node(*SLOT_OFFSETS[t])

    def peer_in(self, k, j):
        group = GROUPS[k]
        if group[0] == ROW:
            b = lax.rem(self.b + self.sign * j, SIDE)
            return self.a_nodes[group[1]] + b * self.stride_b + self.cs[group[2]]
        a = lax.rem(self.a + self.sign * (1 + 2 * lax.div(j, 2)), SIDE)
        return a * self.stride_a + self.b_nodes[group[1]] + lax.rem(self.c + lax.rem(j, 2), CN)


def each(slots, body):
    for t in slots:
        body(t)


def loop(lo, hi, body):
    def step(t, _):
        body(t)
        return 0

    lax.fori_loop(lo, hi, step, 0)


def kernel(
    papers, counts, authors, w_hbm, go_hbm, pf_hbm, sa_hbm,
    ga, gr, gs,
    w, wt, g, feat, agg, table, rows, send, relay, recv, late_send, late_recv, late_hot, auth, acc,
    racc, sacc, wg, csend, crecv, afar_send, afar_recv, anear_send, anear_recv, own_sum, b_send, b_recv,
    far_send, far_recv, near_send, near_recv,
    wsem, gsem, fsem, asem, au_s, au_r, ms_s, ms_r, rl_s, rl_r, lt_s, lt_r,
    c_s, c_r, af_s, af_r, an_s, an_r, b_s, b_r, far_s, far_r, near_s, near_r,
):
    at = Place()
    q = lax.axis_index("rel")
    me, c, node = at.me, at.c, at.node

    def g_copy(k):
        span = pl.ds(pl.multiple_of(k * STEP, STEP), STEP)
        return pltpu.make_async_copy(go_hbm.at[span], g.at[span], gsem.at[k])

    def f_copy(k):
        return pltpu.make_async_copy(pf_hbm.at[chunk(k)], feat.at[chunk(k)], fsem.at[k])

    def a_copy(k):
        return pltpu.make_async_copy(sa_hbm.at[chunk(k)], agg.at[chunk(k)], asem.at[k])

    def load_rest(k):
        a_copy(k).start()
        f_copy(k).start()

    w_copy = pltpu.make_async_copy(w_hbm, w, wsem)
    w_copy.start()
    loop(0, AHEAD, lambda k: g_copy(k).start())

    barrier = pltpu.get_barrier_semaphore()

    def greet(t):
        pl.semaphore_signal(barrier, inc=1, device_id={"nodes": at.peer(t)}, device_id_type=MESH)

    each(OTHERS, greet)
    for d in (1, REL - 1):
        pl.semaphore_signal(
            barrier, inc=1, device_id={"rel": lax.rem(q + d, REL)}, device_id_type=MESH
        )

    w_copy.wait()
    wt[...] = w[...].astype(F32).T.astype(BF16)

    def shared(src, dst, send_sem, recv_sem, to):
        return pltpu.make_async_remote_copy(
            src_ref=src, dst_ref=dst, send_sem=send_sem, recv_sem=recv_sem,
            device_id={"nodes": to}, device_id_type=MESH,
        )

    def remote(src, dst, sems, i, to):
        return shared(src, dst, sems[0].at[i], sems[1].at[i], to)

    def wait_bytes(ref, sem):
        pltpu.make_async_copy(ref, ref, sem).wait()

    def auth_copy(t):
        return shared(authors.at[at.peer(t)], auth.at[t], au_s, au_r, at.peer(t))

    def all_authors(sem):
        wait_bytes(auth.at[0:NODES - 1], sem)

    def back_step(k):
        g_copy(k).wait()

        @pl.when(k + AHEAD < STEPS)
        def _():
            g_copy(k + AHEAD).start()

        lo = pl.multiple_of(k * STEP, STEP)
        back = jnp.dot(g[pl.ds(lo, STEP), :], wt[...], **DOTS)
        for h in range(2):
            table[pl.ds(2 * lo + h, STEP, stride=2), :] = back[:, h * HALF:h * HALF + HALF]

    loop(0, STEPS, back_step)
    loop(0, CHUNKS, load_rest)
    pl.semaphore_wait(barrier, NODES - 1 + 2)

    def relay_copy(t):
        i = RELAYED.index(t)
        return shared(
            send.at[block(t)], relay.at[block(i)], rl_s, rl_r.at[i], node(*first_hop(t))
        )

    def msg_copy(t):
        if t in RELAYED:
            source, to = relay.at[block(RELAYED.index(t))], node(*second_hop(t))
        else:
            source, to = send.at[block(t)], at.peer(t)
        return shared(source, recv.at[block(t)], ms_s, ms_r.at[t], to)

    def late_copy(h, i):
        return shared(
            late_send.at[h, block(i)], late_recv.at[h, block(i)],
            lt_s.at[h], lt_r.at[h], at.peer(WHOLE + i),
        )

    def gather(b):
        for u in range(SLOTS):
            p = papers[b, u] * 2
            rows[2 * u:2 * u + 2, :] = table[pl.ds(p, 2), :]
        live = counts[b]
        scale = lax.rsqrt(jnp.full((1, HALF), live, jnp.int32).astype(F32))
        slot = lax.broadcasted_iota(jnp.int32, (SLOTS, HALF), 0)
        return [
            jnp.where(slot < live, rows[pl.ds(h, SLOTS, stride=2), :] * scale, 0.0).astype(BF16)
            for h in range(2)
        ]

    for k in range(WHOLE // 4):

        def whole_step(j):
            left, right = gather(at.peer_in(k, j))
            send[block(k * 4 + j), :HALF] = left
            send[block(k * 4 + j), HALF:] = right

        loop(0, 4, whole_step)
        for t in range(k * 4, k * 4 + 4):
            if t in RELAYED:
                relay_copy(t).start()
            elif t != HERE:
                msg_copy(t).start()
    for k in range(LATE // 4):

        def late_step(j):
            left, right = gather(at.peer_in(WHOLE // 4 + k, j))
            late_send[0, block(k * 4 + j), :] = left
            late_send[1, block(k * 4 + j), :] = right

        loop(0, 4, late_step)
    each(OTHERS, lambda t: auth_copy(t).start())
    auth[HERE] = authors[me]
    recv[block(HERE), :] = send[block(HERE), :]

    racc[...] = jnp.zeros_like(racc)
    sacc[...] = jnp.zeros_like(sacc)
    cols = pl.ds(pl.multiple_of(q * AUTH_W, AUTH_W), AUTH_W)
    over0 = (((0,), (0,)), ((), ()))

    def grads_step(k):
        a_copy(k).wait()
        f_copy(k).wait()
        racc[...] += lax.dot_general(agg[chunk(k), :], g[chunk(k), :], over0, **DOTS)
        sacc[...] += lax.dot_general(g[chunk(k), cols], feat[chunk(k), :], over0, **DOTS)

    def forward(t):
        relay_copy(t).wait_recv()
        msg_copy(t).start()

    loop(0, 3, grads_step)
    each(RELAYED, forward)
    for h in range(2):
        each(range(LATE), lambda i: late_copy(h, i).start())
    loop(3, CHUNKS, grads_step)

    sacc_t = sacc[...].T
    for n in range(NODES):
        co, y, z = n % CN, n // CN // SIDE, n // CN % SIDE
        ab = (y * SIDE + z, z * SIDE + y)[co]
        for k in range(8):
            wg[co, ab, 8 * k:8 * k + 8, :] = racc[8 * n:8 * n + 8, 128 * k:128 * k + 128]
        for i in range(3):
            for h in range(2):
                r0 = 64 + (2 * i + h) * 8
                wg[co, ab, r0:r0 + 8, :] = sacc_t[24 * n + 8 * i:24 * n + 8 * i + 8, 128 * h:128 * h + 128]

    core_copy = pltpu.make_async_remote_copy(
        src_ref=csend, dst_ref=crecv, send_sem=c_s, recv_sem=c_r,
        device_id={"nodes": node(0, 0, 1)}, device_id_type=MESH,
    )

    def core_round(i):
        csend[i] = wg[1 - c, i].astype(BF16)

    loop(0, SIDE * SIDE, core_round)
    core_copy.start()

    acc[...] = jnp.zeros_like(acc)
    all_authors(au_r)

    def add_rows(first_slot, msg, cols):
        targets = [auth[first_slot + u] for u in range(PER_SCAT)]

        def some(m):
            span = pl.ds(pl.multiple_of(m * SCAT_ROWS, SCAT_ROWS), SCAT_ROWS)
            ids = lax.broadcasted_iota(jnp.int32, (SCAT_ROWS, SLOTS), 0) + m * SCAT_ROWS
            onehot = jnp.concatenate(
                [jnp.where(ids == a, 1.0, 0.0).astype(BF16) for a in targets], axis=1
            )
            acc[span, cols] += jnp.dot(onehot, msg, **DOTS)

        loop(0, GROUP // SCAT_ROWS, some)

    def group(s):
        width = PER_SCAT * SLOTS
        return pl.ds(pl.multiple_of(s * width, width), width)

    def scatter(s):
        for u in range(PER_SCAT):
            if s * PER_SCAT + u != HERE:
                msg_copy(s * PER_SCAT + u).wait_recv()
        add_rows(s * PER_SCAT, recv[group(s), :], slice(None))

    def hot_rows(m):
        span = pl.ds(pl.multiple_of(m * 256, 256), 256)
        ids = lax.broadcasted_iota(jnp.int32, (256, SLOTS), 0) + m * 256
        for u in range(LATE):
            late_hot[span, u * SLOTS:u * SLOTS + SLOTS] = jnp.where(
                ids == auth[WHOLE + u], 1.0, 0.0
            ).astype(BF16)

    def pair(to, p):
        return to * SIDE + 2 * p

    def afar_copy(d):
        return remote(afar_send.at[d], afar_recv.at[d], (af_s, af_r), d, node(1 + 2 * d, 0, 0))

    def anear_copy(d, p):
        return remote(
            anear_send.at[d, p], anear_recv.at[d, p], (an_s, an_r), 2 * d + p, node(1 + 2 * d, 0, 0)
        )

    def b_copy(d):
        return remote(
            b_send.at[at.b_at[d]], b_recv.at[d - 1], (b_s, b_r), d - 1, node(0, d, 0)
        )

    def core_sum(i):
        wg[c, i] = wg[c, i] + crecv[i].astype(F32)

    def a_first():
        core_copy.wait_recv()
        loop(0, SIDE * SIDE, core_sum)
        for d in range(2):
            for i in range(2):
                afar_send[d, i] = wg[c, pair(at.a_at[2], d) + i].astype(BF16)
            afar_copy(d).start()
        for d in range(2):
            for i in range(2):
                anear_send[d, 1 - d, i] = wg[c, pair(at.a_at[1 + 2 * d], 1 - d) + i].astype(BF16)
            anear_copy(d, 1 - d).start()

    def a_second():
        for d in range(2):
            afar_copy(d).wait_recv()
            for i in range(2):
                total = wg[c, pair(at.a_at[1 + 2 * d], d) + i] + afar_recv[d, i].astype(F32)
                anear_send[d, d, i] = total.astype(BF16)
            anear_copy(d, d).start()

    def b_first():
        for p in range(2):
            for d in range(2):
                anear_copy(d, p).wait_recv()
            for i in range(2):
                total = (
                    wg[c, pair(at.a, p) + i]
                    + anear_recv[0, p, i].astype(F32) + anear_recv[1, p, i].astype(F32)
                )
                own_sum[2 * p + i] = total
                b_send[2 * p + i] = total.astype(BF16)
        for d in range(1, SIDE):
            b_copy(d).start()

    def b_last():
        for d in range(1, SIDE):
            b_copy(d).wait_recv()
        total = own_sum[at.b]
        for d in range(SIDE - 1):
            total = total + b_recv[d].astype(F32)
        for k in range(8):
            gr[:, 128 * k:128 * k + 128] = total[8 * k:8 * k + 8, :]
        for i in range(3):
            for h in range(2):
                r0 = 64 + (2 * i + h) * 8
                gs[8 * i:8 * i + 8, 128 * h:128 * h + 128] = total[r0:r0 + 8, :]

    def towards(d):
        return lax.rem(q + (1, REL - 1)[d] * at.sign, REL)

    def rows_of(owner, p):
        return pl.ds(pl.multiple_of(owner * OWN + p * PART, PART), PART)

    def far_copy(h, d):
        return pltpu.make_async_remote_copy(
            src_ref=far_send.at[h, d], dst_ref=far_recv.at[h, d],
            send_sem=far_s.at[h, d], recv_sem=far_r.at[h, d],
            device_id={"rel": towards(d)}, device_id_type=MESH,
        )

    def near_copy(h, d, p):
        return pltpu.make_async_remote_copy(
            src_ref=near_send.at[h, d, p], dst_ref=near_recv.at[h, d, p],
            send_sem=near_s.at[h, d, p], recv_sem=near_r.at[h, d, p],
            device_id={"rel": towards(d)}, device_id_type=MESH,
        )

    def half(h):
        return slice(h * HALF, h * HALF + HALF)

    def late_rows(h, owner):
        span = pl.ds(pl.multiple_of(owner * OWN, OWN), OWN)
        acc[span, half(h)] += jnp.dot(late_hot[span, :], late_recv[h], **DOTS)

    def rel_first(h):
        wait_bytes(late_recv.at[h], lt_r.at[h])
        across = lax.rem(q + 2, REL)
        late_rows(h, across)
        for d in range(2):
            far_send[h, d] = acc[rows_of(across, d), half(h)].astype(BF16)
            far_copy(h, d).start()
        for d in range(2):
            late_rows(h, towards(d))
            near_send[h, d, 1 - d] = acc[rows_of(towards(d), 1 - d), half(h)].astype(BF16)
            near_copy(h, d, 1 - d).start()
        late_rows(h, q)

    def rel_second(h):
        for d in range(2):
            far_copy(h, d).wait_recv()
            mine = acc[rows_of(towards(d), d), half(h)]
            near_send[h, d, d] = (mine + far_recv[h, d].astype(F32)).astype(BF16)
            near_copy(h, d, d).start()

    def rel_last(h):
        for p in range(2):
            for d in range(2):
                near_copy(h, d, p).wait_recv()
            ga[p * PART:p * PART + PART, half(h)] = (
                acc[rows_of(q, p), half(h)]
                + near_recv[h, 0, p].astype(F32) + near_recv[h, 1, p].astype(F32)
            )

    loop(0, GROUP // 256, hot_rows)
    scatter(3)
    scatter(4)
    for i in range(3):
        scatter(i)
    rel_first(0)
    rel_second(0)
    a_first()
    rel_first(1)
    a_second()
    rel_last(0)
    rel_second(1)
    b_first()
    all_authors(au_s)
    wait_bytes(relay, rl_s)
    wait_bytes(recv.at[0:(WHOLE - 1) * SLOTS], ms_s)
    for h in range(2):
        wait_bytes(late_send.at[h], lt_s.at[h])
    core_copy.wait_send()
    b_last()
    rel_last(1)

    for h in range(2):
        for d in range(2):
            far_copy(h, d).wait_send()
            for p in range(2):
                near_copy(h, d, p).wait_send()
    for d in range(2):
        afar_copy(d).wait_send()
        for p in range(2):
            anear_copy(d, p).wait_send()
    for d in range(1, SIDE):
        b_copy(d).wait_send()


def hand_over(a, b, c, ao, bo, co):
    ao[...] = a[...]
    bo[...] = b[...]
    co[...] = c[...]


def on_device(grad_out, paper_feat, saved_agg, rel_weight, slot_paper, slot_author, block_count):
    vmem = pl.BlockSpec(memory_space=pltpu.VMEM)
    smem = pl.BlockSpec(memory_space=pltpu.SMEM)
    hbm = pl.BlockSpec(memory_space=pl.ANY)
    dma = pltpu.SemaphoreType.DMA
    limit = 56 * 1024 * 1024
    whole = (WHOLE * SLOTS, AUTH_W)
    late = (2, LATE * SLOTS, HALF)
    ga, gr, gs = pl.pallas_call(
        kernel,
        out_shape=(
            jax.ShapeDtypeStruct((OWN, AUTH_W), F32),
            jax.ShapeDtypeStruct((8, OUT_W), F32),
            jax.ShapeDtypeStruct((24, AUTH_W), F32),
        ),
        in_specs=[smem, smem, vmem, hbm, hbm, hbm, hbm],
        out_specs=(vmem, vmem, vmem),
        scratch_shapes=[
            pltpu.VMEM((AUTH_W, OUT_W), BF16),
            pltpu.VMEM((OUT_W, AUTH_W), BF16),
            pltpu.VMEM((PAPERS, OUT_W), BF16),
            pltpu.VMEM((PAPERS, PAPER_W), BF16),
            pltpu.VMEM((PAPERS, AUTH_W), BF16),
            pltpu.VMEM((2 * PAPERS, HALF), F32),
            pltpu.VMEM((2 * SLOTS, HALF), F32),
            pltpu.VMEM(whole, BF16),
            pltpu.VMEM((len(RELAYED) * SLOTS, AUTH_W), BF16),
            pltpu.VMEM(whole, BF16),
            pltpu.VMEM(late, BF16),
            pltpu.VMEM(late, BF16),
            pltpu.VMEM((GROUP, LATE * SLOTS), BF16),
            pltpu.VMEM((NODES, 1, SLOTS), jnp.int32),
            pltpu.VMEM((GROUP, AUTH_W), F32),
            pltpu.VMEM((AUTH_W, OUT_W), F32),
            pltpu.VMEM((AUTH_W, PAPER_W), F32),
            pltpu.VMEM((CN, SIDE * SIDE, PIECE, 128), F32),
            pltpu.VMEM((SIDE * SIDE, PIECE, 128), BF16),
            pltpu.VMEM((SIDE * SIDE, PIECE, 128), BF16),
            pltpu.VMEM((2, 2, PIECE, 128), BF16),
            pltpu.VMEM((2, 2, PIECE, 128), BF16),
            pltpu.VMEM((2, 2, 2, PIECE, 128), BF16),
            pltpu.VMEM((2, 2, 2, PIECE, 128), BF16),
            pltpu.VMEM((SIDE, PIECE, 128), F32),
            pltpu.VMEM((SIDE, PIECE, 128), BF16),
            pltpu.VMEM((SIDE - 1, PIECE, 128), BF16),
            pltpu.VMEM((2, 2, PART, HALF), BF16),
            pltpu.VMEM((2, 2, PART, HALF), BF16),
            pltpu.VMEM((2, 2, 2, PART, HALF), BF16),
            pltpu.VMEM((2, 2, 2, PART, HALF), BF16),
            dma, dma((STEPS,)), dma((CHUNKS,)), dma((CHUNKS,)),
            dma, dma, dma, dma((WHOLE,)),
            dma, dma((len(RELAYED),)), dma((2,)), dma((2,)),
            dma, dma, dma((2,)), dma((2,)), dma((4,)), dma((4,)), dma((3,)), dma((3,)),
            dma((2, 2)), dma((2, 2)), dma((2, 2, 2)), dma((2, 2, 2)),
        ],
        compiler_params=pltpu.CompilerParams(
            collective_id=0, has_side_effects=True, vmem_limit_bytes=limit
        ),
    )(
        slot_paper[0, 0], block_count[0, 0],
        slot_author[0, 0][:, None, :], rel_weight[0], grad_out, paper_feat, saved_agg[0],
    )
    ga, gr, gs = pl.pallas_call(
        hand_over,
        out_shape=tuple(jax.ShapeDtypeStruct(v.shape, F32) for v in (ga, gr, gs)),
        in_specs=[vmem] * 3,
        out_specs=(vmem,) * 3,
    )(ga, gr, gs)
    return ga, gr[None], gs


def solution(mesh):
    return jax.shard_map(
        on_device,
        mesh=mesh,
        in_specs=(
            P("nodes", None),
            P("nodes", None),
            P("rel", "nodes", None),
            P("rel", None, None),
            P("nodes", "rel", None, None),
            P("nodes", "rel", None, None),
            P("nodes", "rel", None),
        ),
        out_specs=(P(("nodes", "rel"), None), P("rel", "nodes", None), P("nodes", "rel")),
        check_vma=False,
    )
```

```python
import jax
import jax.numpy as jnp
from jax import lax
from jax.experimental import pallas as pl
from jax.experimental.pallas import tpu as pltpu
from jax.sharding import PartitionSpec as P

MESH = pl.DeviceIdType.MESH
F32 = jnp.float32
BF16 = jnp.bfloat16
DOTS = dict(preferred_element_type=F32)

NODES, REL = 32, 4
SIDE, CN = 4, 2
PAPERS, OUT_W, AUTH_W, PAPER_W = 4608, 1024, 256, 768
SLOTS, GROUP, OWN = 128, 2048, 512
CHUNK = 768
CHUNKS = PAPERS // CHUNK
STEP = 768
STEPS = PAPERS // STEP
AHEAD = 3
PIECE = 112
PER_SCAT = 4
SCAT_ROWS = 1024
WHOLE = 20
LATE = NODES - WHOLE
HALF = AUTH_W // 2
PART = OWN // 2


def chunk(k):
    return pl.ds(pl.multiple_of(k * CHUNK, CHUNK), CHUNK)


def block(t):
    if isinstance(t, int):
        return pl.ds(t * SLOTS, SLOTS)
    return pl.ds(pl.multiple_of(t * SLOTS, SLOTS), SLOTS)


ROW, COLUMN = 0, 1
GROUPS = [(ROW, 2, 0), (COLUMN, 2), (ROW, 2, 1), (ROW, 0, 0), (ROW, 0, 1), (COLUMN, 0), (COLUMN, 1), (COLUMN, 3)]


def in_group(group, j):
    if group[0] == ROW:
        return group[1], j, group[2]
    return 1 + 2 * (j // 2), group[1], j % 2


SLOT_OFFSETS = [in_group(group, j) for group in GROUPS for j in range(4)]
HERE = SLOT_OFFSETS.index((0, 0, 0))
OTHERS = [t for t in range(NODES) if t != HERE]
RELAYED = [t for t in OTHERS if 2 in SLOT_OFFSETS[t][:2]]
DIRECT = [t for t in OTHERS if t < WHOLE and t not in RELAYED]


def first_hop(t):
    da, db, dc = SLOT_OFFSETS[t]
    ha = (1 if db < 2 else 3) if da == 2 else 0
    hb = (1 if da in (1, 2) else 3) if db == 2 else 0
    return ha, hb, 0


def second_hop(t):
    da, db, dc = SLOT_OFFSETS[t]
    ha, hb, _ = first_hop(t)
    return (da - ha) % SIDE, (db - hb) % SIDE, dc


class Place:
    def __init__(self):
        me = lax.axis_index("nodes")
        y = lax.div(me, SIDE * CN)
        z = lax.rem(lax.div(me, CN), SIDE)
        c = lax.rem(me, CN)
        self.me, self.c = me, c
        self.a, self.b = y + c * (z - y), z + c * (y - z)
        self.stride_a = SIDE * CN - (SIDE * CN - CN) * c
        self.stride_b = CN + (SIDE * CN - CN) * c
        self.sign = 1 + 2 * c
        self.a_at = [lax.rem(self.a + self.sign * k, SIDE) for k in range(SIDE)]
        self.b_at = [lax.rem(self.b + self.sign * k, SIDE) for k in range(SIDE)]
        self.a_nodes = [v * self.stride_a for v in self.a_at]
        self.b_nodes = [v * self.stride_b for v in self.b_at]
        self.cs = [c, 1 - c]

    def node(self, da, db, dc):
        return self.a_nodes[da] + self.b_nodes[db] + self.cs[dc]

    def peer(self, t):
        return self.node(*SLOT_OFFSETS[t])

    def peer_in(self, k, j):
        group = GROUPS[k]
        if group[0] == ROW:
            b = lax.rem(self.b + self.sign * j, SIDE)
            return self.a_nodes[group[1]] + b * self.stride_b + self.cs[group[2]]
        a = lax.rem(self.a + self.sign * (1 + 2 * lax.div(j, 2)), SIDE)
        return a * self.stride_a + self.b_nodes[group[1]] + lax.rem(self.c + lax.rem(j, 2), CN)


def each(slots, body):
    for t in slots:
        body(t)


def loop(lo, hi, body):
    def step(t, _):
        body(t)
        return 0

    lax.fori_loop(lo, hi, step, 0)


def kernel(
    papers, counts, authors, w_hbm, go_hbm, pf_hbm, sa_hbm,
    ga, gr, gs,
    w, wt, g, feat, agg, table, rows, send, relay, recv, late_send, late_recv, late_hot, auth, acc,
    racc, sacc, wg, csend, crecv, afar_send, afar_recv, anear_send, anear_recv, own_sum, b_send, b_recv,
    far_send, far_recv, near_send, near_recv,
    wsem, gsem, fsem, asem, au_s, au_r, ms_s, ms_r, rl_s, rl_r, lt_s, lt_r,
    c_s, c_r, af_s, af_r, an_s, an_r, b_s, b_r, far_s, far_r, near_s, near_r,
):
    at = Place()
    q = lax.axis_index("rel")
    me, c, node = at.me, at.c, at.node

    def g_copy(k):
        span = pl.ds(pl.multiple_of(k * STEP, STEP), STEP)
        return pltpu.make_async_copy(go_hbm.at[span], g.at[span], gsem.at[k])

    def f_copy(k):
        return pltpu.make_async_copy(pf_hbm.at[chunk(k)], feat.at[chunk(k)], fsem.at[k])

    def a_copy(k):
        return pltpu.make_async_copy(sa_hbm.at[chunk(k)], agg.at[chunk(k)], asem.at[k])

    def load_rest(k):
        a_copy(k).start()
        f_copy(k).start()

    w_copy = pltpu.make_async_copy(w_hbm, w, wsem)
    w_copy.start()
    loop(0, AHEAD, lambda k: g_copy(k).start())

    barrier = pltpu.get_barrier_semaphore()

    def greet(t):
        pl.semaphore_signal(barrier, inc=1, device_id={"nodes": at.peer(t)}, device_id_type=MESH)

    each(OTHERS, greet)
    for d in (1, REL - 1):
        pl.semaphore_signal(
            barrier, inc=1, device_id={"rel": lax.rem(q + d, REL)}, device_id_type=MESH
        )

    w_copy.wait()
    wt[...] = w[...].astype(F32).T.astype(BF16)

    def shared(src, dst, send_sem, recv_sem, to):
        return pltpu.make_async_remote_copy(
            src_ref=src, dst_ref=dst, send_sem=send_sem, recv_sem=recv_sem,
            device_id={"nodes": to}, device_id_type=MESH,
        )

    def remote(src, dst, sems, i, to):
        return shared(src, dst, sems[0].at[i], sems[1].at[i], to)

    def wait_bytes(ref, sem):
        pltpu.make_async_copy(ref, ref, sem).wait()

    def auth_copy(t):
        return shared(authors.at[at.peer(t)], auth.at[t], au_s, au_r, at.peer(t))

    def all_authors(sem):
        wait_bytes(auth.at[0:NODES - 1], sem)

    def back_step(k):
        g_copy(k).wait()

        @pl.when(k + AHEAD < STEPS)
        def _():
            g_copy(k + AHEAD).start()

        lo = pl.multiple_of(k * STEP, STEP)
        back = jnp.dot(g[pl.ds(lo, STEP), :], wt[...], **DOTS)
        for h in range(2):
            table[pl.ds(2 * lo + h, STEP, stride=2), :] = back[:, h * HALF:h * HALF + HALF]

    loop(0, STEPS, back_step)
    loop(0, CHUNKS, load_rest)
    pl.semaphore_wait(barrier, NODES - 1 + 2)

    def relay_copy(t):
        i = RELAYED.index(t)
        return shared(
            send.at[block(t)], relay.at[block(i)], rl_s, rl_r.at[i], node(*first_hop(t))
        )

    def msg_copy(t):
        if t in RELAYED:
            source, to = relay.at[block(RELAYED.index(t))], node(*second_hop(t))
        else:
            source, to = send.at[block(t)], at.peer(t)
        return shared(source, recv.at[block(t)], ms_s, ms_r.at[t], to)

    def late_copy(h, i):
        return shared(
            late_send.at[h, block(i)], late_recv.at[h, block(i)],
            lt_s.at[h], lt_r.at[h], at.peer(WHOLE + i),
        )

    def gather(b):
        for u in range(SLOTS):
            p = papers[b, u] * 2
            rows[2 * u:2 * u + 2, :] = table[pl.ds(p, 2), :]
        live = counts[b]
        scale = lax.rsqrt(jnp.full((1, HALF), live, jnp.int32).astype(F32))
        slot = lax.broadcasted_iota(jnp.int32, (SLOTS, HALF), 0)
        return [
            jnp.where(slot < live, rows[pl.ds(h, SLOTS, stride=2), :] * scale, 0.0).astype(BF16)
            for h in range(2)
        ]

    for k in range(WHOLE // 4):

        def whole_step(j):
            left, right = gather(at.peer_in(k, j))
            send[block(k * 4 + j), :HALF] = left
            send[block(k * 4 + j), HALF:] = right

        loop(0, 4, whole_step)
        for t in range(k * 4, k * 4 + 4):
            if t in RELAYED:
                relay_copy(t).start()
            elif t != HERE:
                msg_copy(t).start()
    for k in range(LATE // 4):

        def late_step(j):
            left, right = gather(at.peer_in(WHOLE // 4 + k, j))
            late_send[0, block(k * 4 + j), :] = left
            late_send[1, block(k * 4 + j), :] = right

        loop(0, 4, late_step)
    each(OTHERS, lambda t: auth_copy(t).start())
    auth[HERE] = authors[me]
    recv[block(HERE), :] = send[block(HERE), :]

    racc[...] = jnp.zeros_like(racc)
    sacc[...] = jnp.zeros_like(sacc)
    cols = pl.ds(pl.multiple_of(q * AUTH_W, AUTH_W), AUTH_W)
    over0 = (((0,), (0,)), ((), ()))

    def grads_step(k):
        a_copy(k).wait()
        f_copy(k).wait()
        racc[...] += lax.dot_general(agg[chunk(k), :], g[chunk(k), :], over0, **DOTS)
        sacc[...] += lax.dot_general(g[chunk(k), cols], feat[chunk(k), :], over0, **DOTS)

    def forward(t):
        relay_copy(t).wait_recv()
        msg_copy(t).start()

    loop(0, 4, grads_step)
    each(RELAYED, forward)
    for h in range(2):
        each(range(LATE), lambda i: late_copy(h, i).start())
    loop(4, CHUNKS, grads_step)

    sacc_t = sacc[...].T
    for n in range(NODES):
        co, y, z = n % CN, n // CN // SIDE, n // CN % SIDE
        ab = (y * SIDE + z, z * SIDE + y)[co]
        for k in range(8):
            wg[co, ab, 8 * k:8 * k + 8, :] = racc[8 * n:8 * n + 8, 128 * k:128 * k + 128]
        for i in range(3):
            for h in range(2):
                r0 = 64 + (2 * i + h) * 8
                wg[co, ab, r0:r0 + 8, :] = sacc_t[24 * n + 8 * i:24 * n + 8 * i + 8, 128 * h:128 * h + 128]

    core_copy = pltpu.make_async_remote_copy(
        src_ref=csend, dst_ref=crecv, send_sem=c_s, recv_sem=c_r,
        device_id={"nodes": node(0, 0, 1)}, device_id_type=MESH,
    )

    def core_round(i):
        csend[i] = wg[1 - c, i].astype(BF16)

    loop(0, SIDE * SIDE, core_round)
    core_copy.start()

    acc[...] = jnp.zeros_like(acc)
    all_authors(au_r)

    def add_rows(first_slot, msg, cols):
        targets = [auth[first_slot + u] for u in range(PER_SCAT)]

        def some(m):
            span = pl.ds(pl.multiple_of(m * SCAT_ROWS, SCAT_ROWS), SCAT_ROWS)
            ids = lax.broadcasted_iota(jnp.int32, (SCAT_ROWS, SLOTS), 0) + m * SCAT_ROWS
            onehot = jnp.concatenate(
                [jnp.where(ids == a, 1.0, 0.0).astype(BF16) for a in targets], axis=1
            )
            acc[span, cols] += jnp.dot(onehot, msg, **DOTS)

        loop(0, GROUP // SCAT_ROWS, some)

    def group(s):
        width = PER_SCAT * SLOTS
        return pl.ds(pl.multiple_of(s * width, width), width)

    def scatter(s):
        for u in range(PER_SCAT):
            if s * PER_SCAT + u != HERE:
                msg_copy(s * PER_SCAT + u).wait_recv()
        add_rows(s * PER_SCAT, recv[group(s), :], slice(None))

    def hot_rows(m):
        span = pl.ds(pl.multiple_of(m * 256, 256), 256)
        ids = lax.broadcasted_iota(jnp.int32, (256, SLOTS), 0) + m * 256
        for u in range(LATE):
            late_hot[span, u * SLOTS:u * SLOTS + SLOTS] = jnp.where(
                ids == auth[WHOLE + u], 1.0, 0.0
            ).astype(BF16)

    def pair(to, p):
        return to * SIDE + 2 * p

    def afar_copy(d):
        return remote(afar_send.at[d], afar_recv.at[d], (af_s, af_r), d, node(1 + 2 * d, 0, 0))

    def anear_copy(d, p):
        return remote(
            anear_send.at[d, p], anear_recv.at[d, p], (an_s, an_r), 2 * d + p, node(1 + 2 * d, 0, 0)
        )

    def b_copy(d):
        return remote(
            b_send.at[at.b_at[d]], b_recv.at[d - 1], (b_s, b_r), d - 1, node(0, d, 0)
        )

    def core_sum(i):
        wg[c, i] = wg[c, i] + crecv[i].astype(F32)

    def a_first():
        core_copy.wait_recv()
        loop(0, SIDE * SIDE, core_sum)
        for d in range(2):
            for i in range(2):
                afar_send[d, i] = wg[c, pair(at.a_at[2], d) + i].astype(BF16)
            afar_copy(d).start()
        for d in range(2):
            for i in range(2):
                anear_send[d, 1 - d, i] = wg[c, pair(at.a_at[1 + 2 * d], 1 - d) + i].astype(BF16)
            anear_copy(d, 1 - d).start()

    def a_second():
        for d in range(2):
            afar_copy(d).wait_recv()
            for i in range(2):
                total = wg[c, pair(at.a_at[1 + 2 * d], d) + i] + afar_recv[d, i].astype(F32)
                anear_send[d, d, i] = total.astype(BF16)
            anear_copy(d, d).start()

    def b_first():
        for p in range(2):
            for d in range(2):
                anear_copy(d, p).wait_recv()
            for i in range(2):
                total = (
                    wg[c, pair(at.a, p) + i]
                    + anear_recv[0, p, i].astype(F32) + anear_recv[1, p, i].astype(F32)
                )
                own_sum[2 * p + i] = total
                b_send[2 * p + i] = total.astype(BF16)
        for d in range(1, SIDE):
            b_copy(d).start()

    def b_last():
        for d in range(1, SIDE):
            b_copy(d).wait_recv()
        total = own_sum[at.b]
        for d in range(SIDE - 1):
            total = total + b_recv[d].astype(F32)
        for k in range(8):
            gr[:, 128 * k:128 * k + 128] = total[8 * k:8 * k + 8, :]
        for i in range(3):
            for h in range(2):
                r0 = 64 + (2 * i + h) * 8
                gs[8 * i:8 * i + 8, 128 * h:128 * h + 128] = total[r0:r0 + 8, :]

    def towards(d):
        return lax.rem(q + (1, REL - 1)[d] * at.sign, REL)

    def rows_of(owner, p):
        return pl.ds(pl.multiple_of(owner * OWN + p * PART, PART), PART)

    def far_copy(h, d):
        return pltpu.make_async_remote_copy(
            src_ref=far_send.at[h, d], dst_ref=far_recv.at[h, d],
            send_sem=far_s.at[h, d], recv_sem=far_r.at[h, d],
            device_id={"rel": towards(d)}, device_id_type=MESH,
        )

    def near_copy(h, d, p):
        return pltpu.make_async_remote_copy(
            src_ref=near_send.at[h, d, p], dst_ref=near_recv.at[h, d, p],
            send_sem=near_s.at[h, d, p], recv_sem=near_r.at[h, d, p],
            device_id={"rel": towards(d)}, device_id_type=MESH,
        )

    def half(h):
        return slice(h * HALF, h * HALF + HALF)

    def late_rows(h, owner):
        span = pl.ds(pl.multiple_of(owner * OWN, OWN), OWN)
        acc[span, half(h)] += jnp.dot(late_hot[span, :], late_recv[h], **DOTS)

    def rel_first(h):
        wait_bytes(late_recv.at[h], lt_r.at[h])
        across = lax.rem(q + 2, REL)
        late_rows(h, across)
        for d in range(2):
            far_send[h, d] = acc[rows_of(across, d), half(h)].astype(BF16)
            far_copy(h, d).start()
        for d in range(2):
            late_rows(h, towards(d))
            near_send[h, d, 1 - d] = acc[rows_of(towards(d), 1 - d), half(h)].astype(BF16)
            near_copy(h, d, 1 - d).start()
        late_rows(h, q)

    def rel_second(h):
        for d in range(2):
            far_copy(h, d).wait_recv()
            mine = acc[rows_of(towards(d), d), half(h)]
            near_send[h, d, d] = (mine + far_recv[h, d].astype(F32)).astype(BF16)
            near_copy(h, d, d).start()

    def rel_last(h):
        for p in range(2):
            for d in range(2):
                near_copy(h, d, p).wait_recv()
            ga[p * PART:p * PART + PART, half(h)] = (
                acc[rows_of(q, p), half(h)]
                + near_recv[h, 0, p].astype(F32) + near_recv[h, 1, p].astype(F32)
            )

    loop(0, GROUP // 256, hot_rows)
    scatter(3)
    scatter(4)
    for i in range(3):
        scatter(i)
    rel_first(0)
    rel_second(0)
    a_first()
    rel_first(1)
    a_second()
    rel_last(0)
    rel_second(1)
    b_first()
    all_authors(au_s)
    wait_bytes(relay, rl_s)
    wait_bytes(recv.at[0:(WHOLE - 1) * SLOTS], ms_s)
    for h in range(2):
        wait_bytes(late_send.at[h], lt_s.at[h])
    core_copy.wait_send()
    b_last()
    rel_last(1)

    for h in range(2):
        for d in range(2):
            far_copy(h, d).wait_send()
            for p in range(2):
                near_copy(h, d, p).wait_send()
    for d in range(2):
        afar_copy(d).wait_send()
        for p in range(2):
            anear_copy(d, p).wait_send()
    for d in range(1, SIDE):
        b_copy(d).wait_send()


def hand_over(a, b, c, ao, bo, co):
    ao[...] = a[...]
    bo[...] = b[...]
    co[...] = c[...]


def on_device(grad_out, paper_feat, saved_agg, rel_weight, slot_paper, slot_author, block_count):
    vmem = pl.BlockSpec(memory_space=pltpu.VMEM)
    smem = pl.BlockSpec(memory_space=pltpu.SMEM)
    hbm = pl.BlockSpec(memory_space=pl.ANY)
    dma = pltpu.SemaphoreType.DMA
    limit = 56 * 1024 * 1024
    whole = (WHOLE * SLOTS, AUTH_W)
    late = (2, LATE * SLOTS, HALF)
    ga, gr, gs = pl.pallas_call(
        kernel,
        out_shape=(
            jax.ShapeDtypeStruct((OWN, AUTH_W), F32),
            jax.ShapeDtypeStruct((8, OUT_W), F32),
            jax.ShapeDtypeStruct((24, AUTH_W), F32),
        ),
        in_specs=[smem, smem, vmem, hbm, hbm, hbm, hbm],
        out_specs=(vmem, vmem, vmem),
        scratch_shapes=[
            pltpu.VMEM((AUTH_W, OUT_W), BF16),
            pltpu.VMEM((OUT_W, AUTH_W), BF16),
            pltpu.VMEM((PAPERS, OUT_W), BF16),
            pltpu.VMEM((PAPERS, PAPER_W), BF16),
            pltpu.VMEM((PAPERS, AUTH_W), BF16),
            pltpu.VMEM((2 * PAPERS, HALF), F32),
            pltpu.VMEM((2 * SLOTS, HALF), F32),
            pltpu.VMEM(whole, BF16),
            pltpu.VMEM((len(RELAYED) * SLOTS, AUTH_W), BF16),
            pltpu.VMEM(whole, BF16),
            pltpu.VMEM(late, BF16),
            pltpu.VMEM(late, BF16),
            pltpu.VMEM((GROUP, LATE * SLOTS), BF16),
            pltpu.VMEM((NODES, 1, SLOTS), jnp.int32),
            pltpu.VMEM((GROUP, AUTH_W), F32),
            pltpu.VMEM((AUTH_W, OUT_W), F32),
            pltpu.VMEM((AUTH_W, PAPER_W), F32),
            pltpu.VMEM((CN, SIDE * SIDE, PIECE, 128), F32),
            pltpu.VMEM((SIDE * SIDE, PIECE, 128), BF16),
            pltpu.VMEM((SIDE * SIDE, PIECE, 128), BF16),
            pltpu.VMEM((2, 2, PIECE, 128), BF16),
            pltpu.VMEM((2, 2, PIECE, 128), BF16),
            pltpu.VMEM((2, 2, 2, PIECE, 128), BF16),
            pltpu.VMEM((2, 2, 2, PIECE, 128), BF16),
            pltpu.VMEM((SIDE, PIECE, 128), F32),
            pltpu.VMEM((SIDE, PIECE, 128), BF16),
            pltpu.VMEM((SIDE - 1, PIECE, 128), BF16),
            pltpu.VMEM((2, 2, PART, HALF), BF16),
            pltpu.VMEM((2, 2, PART, HALF), BF16),
            pltpu.VMEM((2, 2, 2, PART, HALF), BF16),
            pltpu.VMEM((2, 2, 2, PART, HALF), BF16),
            dma, dma((STEPS,)), dma((CHUNKS,)), dma((CHUNKS,)),
            dma, dma, dma, dma((WHOLE,)),
            dma, dma((len(RELAYED),)), dma((2,)), dma((2,)),
            dma, dma, dma((2,)), dma((2,)), dma((4,)), dma((4,)), dma((3,)), dma((3,)),
            dma((2, 2)), dma((2, 2)), dma((2, 2, 2)), dma((2, 2, 2)),
        ],
        compiler_params=pltpu.CompilerParams(
            collective_id=0, has_side_effects=True, vmem_limit_bytes=limit
        ),
    )(
        slot_paper[0, 0], block_count[0, 0],
        slot_author[0, 0][:, None, :], rel_weight[0], grad_out, paper_feat, saved_agg[0],
    )
    ga, gr, gs = pl.pallas_call(
        hand_over,
        out_shape=tuple(jax.ShapeDtypeStruct(v.shape, F32) for v in (ga, gr, gs)),
        in_specs=[vmem] * 3,
        out_specs=(vmem,) * 3,
    )(ga, gr, gs)
    return ga, gr[None], gs


def solution(mesh):
    return jax.shard_map(
        on_device,
        mesh=mesh,
        in_specs=(
            P("nodes", None),
            P("nodes", None),
            P("rel", "nodes", None),
            P("rel", None, None),
            P("nodes", "rel", None, None),
            P("nodes", "rel", None, None),
            P("nodes", "rel", None),
        ),
        out_specs=(P(("nodes", "rel"), None), P("rel", "nodes", None), P("nodes", "rel")),
        check_vma=False,
    )
```
